32 devices in a mesh: dp: 4 (over z), expert: 8 (over y, x, core).
Axes of the slice: x: 2, y: 2, z: 4, core: 2. Of those that a mesh axis runs over, the one named last changes fastest.
Arguments:
- tokens: bfloat16 [16384, 1280], P(('dp', 'expert')), may hold values from -6 to 6
- cotangent: bfloat16 [16384, 1280], P(('dp', 'expert')), may hold values from -6 to 6
- lengths: int32 [32], P(('dp', 'expert')), may hold values from 1 to 512, as said below
- choices: int32 [16384, 7], P(('dp', 'expert')), may hold values from 0 to 15, all different within a row; in each aligned block of 512 rows (0 to 511, 512 to 1023, ...) at most 256 rows name the same one
- attn_weight: float32 [4, 1280, 1280], P(None, ('dp', 'expert')), may hold values from -1 to 1
- attn_moment: float32 [4, 1280, 1280], P(None, ('dp', 'expert')), may hold values from -224 to 224
- attn_average: float32 [4, 1280, 1280], P(None, ('dp', 'expert')), may hold values from -0.15625 to 0.15625
- router_weight: float32 [1280, 16], P(('dp', 'expert')), may hold values from -0.078125 to 0.078125
- router_moment: float32 [1280, 16], P(('dp', 'expert')), may hold values from -4096 to 4096
- router_average: float32 [1280, 16], P(('dp', 'expert')), may hold values from -0.078125 to 0.078125
- shared_weight: float32 [3, 1280, 896], P(None, ('dp', 'expert')), may hold values from -4 to 4
- shared_moment: float32 [3, 1280, 896], P(None, ('dp', 'expert')), may hold values from -384 to 384
- shared_average: float32 [3, 1280, 896], P(None, ('dp', 'expert')), may hold values from -0.15625 to 0.15625
- routed_weight: float32 [16, 3, 1280, 896], P('expert', None, 'dp'), may hold values from -4 to 4
- routed_moment: float32 [16, 3, 1280, 896], P('expert', None, 'dp'), may hold values from -64 to 64
- routed_average: float32 [16, 3, 1280, 896], P('expert', None, 'dp'), may hold values from -0.15625 to 0.15625
- norm_gains: float32 [2, 1280], P(None, ('dp', 'expert')), may hold values from 0.5 to 1.5
- gain_moment: float32 [2, 1280], P(None, ('dp', 'expert')), may hold values from -384 to 384
- gain_average: float32 [2, 1280], P(None, ('dp', 'expert')), may hold values from 0.5 to 1.5
Outputs:
- block_out: bfloat16 [16384, 1280], P(('dp', 'expert'))
- input_grad: float32 [16384, 1280], P(('dp', 'expert'))
- masked_rms: float32 [2], replicated
- attn_grad: float32 [4, 1280, 1280], P(None, ('dp', 'expert'))
- attn_new: float32 [4, 1280, 1280], P(None, ('dp', 'expert'))
- attn_moment_new: float32 [4, 1280, 1280], P(None, ('dp', 'expert'))
- attn_average_new: float32 [4, 1280, 1280], P(None, ('dp', 'expert'))
- attn_copy: bfloat16 [4, 1280, 1280], P(None, ('dp', 'expert'))
- router_grad: float32 [1280, 16], P(('dp', 'expert'))
- router_new: float32 [1280, 16], P(('dp', 'expert'))
- router_moment_new: float32 [1280, 16], P(('dp', 'expert'))
- router_average_new: float32 [1280, 16], P(('dp', 'expert'))
- router_copy: bfloat16 [1280, 16], P(('dp', 'expert'))
- shared_grad: float32 [3, 1280, 896], P(None, ('dp', 'expert'))
- shared_new: float32 [3, 1280, 896], P(None, ('dp', 'expert'))
- shared_moment_new: float32 [3, 1280, 896], P(None, ('dp', 'expert'))
- shared_average_new: float32 [3, 1280, 896], P(None, ('dp', 'expert'))
- shared_copy: bfloat16 [3, 1280, 896], P(None, ('dp', 'expert'))
- routed_grad: float32 [16, 3, 1280, 896], P('expert', None, 'dp')
- routed_new: float32 [16, 3, 1280, 896], P('expert', None, 'dp')
- routed_moment_new: float32 [16, 3, 1280, 896], P('expert', None, 'dp')
- routed_average_new: float32 [16, 3, 1280, 896], P('expert', None, 'dp')
- routed_copy: bfloat16 [16, 3, 1280, 896], P('expert', None, 'dp')
- gain_grad: float32 [2, 1280], P(None, ('dp', 'expert'))
- gain_new: float32 [2, 1280], P(None, ('dp', 'expert'))
- gain_moment_new: float32 [2, 1280], P(None, ('dp', 'expert'))
- gain_average_new: float32 [2, 1280], P(None, ('dp', 'expert'))
The draws below stay inside these ranges and needn't reach their ends.
Inputs may be any that keep to these rules, and one draw needn't show every extreme that they name: `lengths`: one sequence has exactly 512 real tokens. `choices`: a token's 7 experts differ; in the rows of one sequence no expert is named more than 256 times, a bound that some block reaches.
All inputs are finite; a program needn't handle non-finite values.
Results may differ from the reference program's by a relative error of at most 0.018.
Values may be sent and summed in bfloat16 or wider, within the bound.
No kernel may reach another device: no remote copies, remote signals or barrier semaphores. Data moves between devices by JAX's collectives and lax.ppermute only.
A program may use at most 384 MiB of HBM per device.

```python
import math
import jax
import jax.numpy as jnp
import numpy as np
from jax import lax

D = 1280
HEADS = 10
HEAD_DIM = 128
FF = 896
TOPK = 7
SEQ_LEN = 512
STEP = 3
SEQS = 32
TOKENS = 16384
ROUTED = 16
CAP = 256
N_DP = 4
N_EXPERT = 8


def layered_normal(key, array_shape, factors):
    normal_draw = jax.random.truncated_normal(key, -4.0, 4.0, array_shape, jnp.float32)
    return normal_draw * factors


def draw_lengths(key, part):
    key = jax.random.fold_in(key, 11)
    seq_index = jnp.arange(SEQS, dtype=jnp.int32)
    outer_index = seq_index // N_EXPERT
    inner_index = seq_index % N_EXPERT
    outer_span = max(N_DP - 1, 1)
    inner_span = max(N_EXPERT - 1, 1)
    upper_end = SEQ_LEN * (outer_span + 2 * outer_index) * (inner_span + 2 * inner_index) // (9 * outer_span * inner_span)
    upper_end = jnp.maximum(upper_end, 4)
    lower_end = upper_end - upper_end // 4
    drawn_bits = jax.random.randint(key, (SEQS,), 0, 1 << 20, dtype=jnp.int32)
    length_value = lower_end + drawn_bits % (upper_end - lower_end + 1)
    return jnp.where(seq_index == SEQS - 1, SEQ_LEN, length_value).astype(jnp.int32)


def draw_attn_weight(key, part):
    key = jax.random.fold_in(key, 21)
    factors = jnp.array([1.0, 1.0, 1.0, math.sqrt(SEQ_LEN) / 8.0], jnp.float32).reshape(4, 1, 1) / math.sqrt(D)
    return layered_normal(key, (4, D, D), factors)


def draw_shared_weight(key, part):
    key = jax.random.fold_in(key, 31)
    factors = jnp.array([1.0 / math.sqrt(D), 1.0 / math.sqrt(D), 2.0 / math.sqrt(FF)], jnp.float32).reshape(3, 1, 1)
    return layered_normal(key, (3, D, FF), factors)


def draw_routed_weight(key, part):
    key = jax.random.fold_in(key, 41)
    factors = jnp.array([1.0 / math.sqrt(D), 1.0 / math.sqrt(D), 5.0 / math.sqrt(FF)], jnp.float32).reshape(1, 3, 1, 1)
    return layered_normal(key, (ROUTED, 3, D, FF), factors)


def levels(own_key, dims, split, smallest, largest):
    loudness = 1.0
    for axis_at, parts in split:
        draws = jax.random.uniform(jax.random.fold_in(jax.random.fold_in(own_key, 6), axis_at), (parts,), jnp.float32, smallest / len(split), largest / len(split))
        loudness = loudness * jnp.repeat(jnp.exp(draws), dims[axis_at] // parts).reshape((-1,) + (1,) * (len(dims) - 1 - axis_at))
    return loudness


def routed_block(key, own, number, rows, amount, top, bound, lean):
    order = jax.random.permutation(key, amount)
    crowded, usual = shares(amount, rows * top, bound, lean, True), shares(amount, rows * top, bound, lean, False)
    places = jnp.arange(amount)

    def named(sizes, rotation):
        used = int((sizes > 0).sum())
        fixed = max(1, used // 4)
        moved = fixed + (places - fixed + rotation * (used - fixed)) % max(1, amount - fixed)
        return jnp.zeros((amount,), jnp.int32).at[order[jnp.where(places < fixed, places, moved)]].set(jnp.asarray(sizes, jnp.int32))

    sizes = jnp.where(number % 4 == 0, named(crowded, number // 4), named(usual, number - number // 4 - 1))
    mixed = jax.random.permutation(jax.random.fold_in(own, 3), amount)
    giver, taker = mixed[0:amount // 2 * 2:2], mixed[1:amount // 2 * 2:2]
    slack = jnp.minimum(sizes[giver] - 1, bound - sizes[taker]) // 2
    slack = jnp.where((giver == order[0]) | (taker == order[0]) | (sizes[taker] == 0), 0, jnp.maximum(slack, 0))
    moved = jax.random.randint(jax.random.fold_in(own, 4), (amount // 2,), 0, 1 << 20) % (slack + 1)
    sizes = sizes.at[giver].add(-moved).at[taker].add(moved)
    labels = jnp.searchsorted(jnp.cumsum(sizes), jnp.arange(rows * top), side="right").astype(jnp.int32)
    grid = labels.reshape(top, rows).T
    grid = grid[jax.random.permutation(jax.random.fold_in(own, 1), rows)]
    rotation = jax.random.randint(jax.random.fold_in(own, 2), (rows, 1), 0, top)
    return jnp.take_along_axis(grid, (jnp.arange(top)[None, :] + rotation) % top, axis=1)


def shares(count, total, bound, skew, full):
    weights = [(1 << 20) // math.isqrt(standing ** skew) + 1 for standing in range(1, count + 1)]
    largest = bound if full else min(bound, max(-(-total // count), total * weights[0] // sum(weights)))
    least = 1 if total - largest >= count - 1 else 0
    counts, spare = [largest] + [least] * (count - 1), total - largest - least * (count - 1)
    while spare > 0:
        movable = [i for i in range(1, count) if counts[i] < largest] or [i for i in range(1, count) if counts[i] < bound]
        pool, budget = sum([weights[i] for i in movable]), spare
        for i in movable:
            extra = min(bound - counts[i], max(1, budget * weights[i] // pool), spare)
            counts[i] = counts[i] + extra
            spare = spare - extra
    return np.array(counts)


def normal_values(rng, shape, deviation, bound, cuts=(), held_as=jnp.bfloat16):
    values = deviation * jax.random.normal(rng, shape, jnp.float32)
    if cuts:
        values = values * levels(rng, shape, cuts, -0.22, 0.18)
    return jnp.clip(values, -bound, bound).astype(held_as)


def setup_inputs(seed: int = 0) -> dict:
    keys = jax.random.split(jax.random.key(seed), 20)
    tokens = normal_values(keys[0], (TOKENS, D), 1.0, 6.0, ((0, 32),))
    cotangent = normal_values(keys[1], (TOKENS, D), 1.0, 6.0, ((0, 32),))
    lengths = draw_lengths(jax.random.fold_in(keys[19], 71), 0)
    choices_keys = jax.random.split(jax.random.fold_in(keys[3], 1), TOKENS // SEQ_LEN)
    choices_turns = jax.random.permutation(jax.random.fold_in(keys[3], 3), TOKENS // SEQ_LEN)
    choices = jax.vmap(lambda own, number: routed_block(jax.random.fold_in(keys[3], 2), own, number, SEQ_LEN, ROUTED, TOPK, CAP, 1))(choices_keys, choices_turns).reshape((TOKENS, TOPK))
    attn_weight = draw_attn_weight(jax.random.fold_in(keys[19], 71), 0)
    attn_moment = normal_values(keys[5], (4, D, D), (0.3 * TOKENS ** 0.5), 224.0, ((1, 32),), jnp.float32)
    attn_average = normal_values(keys[6], (4, D, D), D ** -0.5, 0.15625, ((1, 32),), jnp.float32)
    router_weight = normal_values(keys[7], (D, ROUTED), (4 * D) ** -0.5, 0.078125, ((0, 32),), jnp.float32)
    router_moment = normal_values(keys[8], (D, ROUTED), (0.15 * (D * TOKENS) ** 0.5), 4096.0, ((0, 32),), jnp.float32)
    router_average = normal_values(keys[9], (D, ROUTED), (4 * D) ** -0.5, 0.078125, ((0, 32),), jnp.float32)
    shared_weight = draw_shared_weight(jax.random.fold_in(keys[19], 71), 0)
    shared_moment = normal_values(keys[11], (3, D, FF), (0.5 * TOKENS ** 0.5), 384.0, ((1, 32),), jnp.float32)
    shared_average = normal_values(keys[12], (3, D, FF), D ** -0.5, 0.15625, ((1, 32),), jnp.float32)
    routed_weight = draw_routed_weight(jax.random.fold_in(keys[19], 71), 0)
    routed_moment = normal_values(keys[14], (ROUTED, 3, D, FF), (0.08 * TOKENS ** 0.5), 64.0, ((0, 8), (2, 4)), jnp.float32)
    routed_average = normal_values(keys[15], (ROUTED, 3, D, FF), D ** -0.5, 0.15625, ((0, 8), (2, 4)), jnp.float32)
    norm_gains = jnp.clip(1.0 + 0.1 * jax.random.normal(keys[16], (2, D), jnp.float32), 0.5, 1.5)
    gain_moment = normal_values(keys[17], (2, D), (0.5 * TOKENS ** 0.5), 384.0, ((1, 32),), jnp.float32)
    gain_average = jnp.clip(1.0 + 0.1 * jax.random.normal(keys[18], (2, D), jnp.float32), 0.5, 1.5)
    return dict(tokens=tokens, cotangent=cotangent, lengths=lengths, choices=choices, attn_weight=attn_weight, attn_moment=attn_moment, attn_average=attn_average, router_weight=router_weight, router_moment=router_moment, router_average=router_average, shared_weight=shared_weight, shared_moment=shared_moment, shared_average=shared_average, routed_weight=routed_weight, routed_moment=routed_moment, routed_average=routed_average, norm_gains=norm_gains, gain_moment=gain_moment, gain_average=gain_average)


highest_precision = lax.Precision.HIGHEST
eps_norm = 1e-06
momentum_rate = 0.9
decay_rate = 0.0001
rate_attention = 0.01
rate_router = 0.03
rate_shared = 0.01
rate_routed = 0.04
rate_gains = 0.2
masked_score = -1e+30

@jax.custom_vjp
def low(v):
    return lax.optimization_barrier(v.astype(jnp.bfloat16)).astype(jnp.float32)

@jax.custom_vjp
def low_back(v):
    return v

def low_keep(v):
    return (low(v), None)

def low_pass(kept, grad):
    return (grad,)

def back_keep(v):
    return (v, None)

def back_low(kept, grad):
    return (low(grad),)
low.defvjp(low_keep, low_pass)
low_back.defvjp(back_keep, back_low)

def rms_norm(values, gain_row):
    inverse = lax.rsqrt(lax.optimization_barrier(jnp.mean(values * values, axis=-1, keepdims=True)) + eps_norm)
    return values * inverse * gain_row

def rotate(values, positions, direction):
    half_dim = values.shape[-1] // 2
    frequency = 10000.0 ** (-jnp.arange(half_dim, dtype=jnp.float32) / half_dim)
    angles = positions.astype(jnp.float32)[:, None] * frequency[None, :]
    cosine = jnp.cos(angles)[:, None, :]
    sine_part = direction * jnp.sin(angles)[:, None, :]
    first_half = values[..., :half_dim]
    second_half = values[..., half_dim:]
    return jnp.concatenate([first_half * cosine - second_half * sine_part, second_half * cosine + first_half * sine_part], axis=-1)

def attention_branch(seq_tokens, seq_length, attn_low, gain_row):
    normed = low(rms_norm(seq_tokens, gain_row))
    positions = jnp.arange(SEQ_LEN, dtype=jnp.int32)

    def project(which):
        return jnp.dot(normed, attn_low[which], precision=highest_precision)
    queries = low(rotate(low_back(project(0)).reshape(SEQ_LEN, HEADS, HEAD_DIM), positions, 1.0))
    key_heads = low(rotate(low_back(project(1)).reshape(SEQ_LEN, HEADS, HEAD_DIM), positions, 1.0))
    value_heads = low(low_back(project(2))).reshape(SEQ_LEN, HEADS, HEAD_DIM)
    raw_scores = jnp.einsum('qhd,khd->hqk', queries, key_heads, precision=highest_precision)
    scores = low_back(raw_scores * (1.0 / math.sqrt(HEAD_DIM)))
    allowed = (positions[None, :] <= positions[:, None]) & (positions[None, :] < seq_length)
    masked = jnp.where(allowed[None], scores, masked_score)
    row_peak = lax.optimization_barrier(jnp.max(masked, axis=-1, keepdims=True))
    exp_part = jnp.exp(masked - row_peak)
    probability = exp_part / lax.optimization_barrier(jnp.sum(exp_part, axis=-1, keepdims=True))
    context = jnp.einsum('hqk,khd->qhd', low(probability), value_heads, precision=highest_precision)
    context = low(low_back(context)).reshape(SEQ_LEN, D)
    return low_back(jnp.dot(context, attn_low[3], precision=highest_precision))

def routing_tables(choice_ids):
    per_sequence = choice_ids.reshape(SEQS, SEQ_LEN * TOPK)
    onehot = (per_sequence[:, :, None] == jnp.arange(ROUTED, dtype=jnp.int32)[None, None, :]).astype(jnp.int32)
    slot_rank = lax.optimization_barrier(jnp.sum((jnp.cumsum(onehot, axis=1) - onehot) * onehot, axis=2))
    seq_index = jnp.arange(SEQS, dtype=jnp.int32)[:, None]
    position = per_sequence * (SEQS * CAP) + seq_index * CAP + slot_rank
    token_index = seq_index * SEQ_LEN + jnp.arange(SEQ_LEN * TOPK, dtype=jnp.int32)[None, :] // TOPK
    slot_table = jnp.full((ROUTED * SEQS * CAP,), -1, dtype=jnp.int32).at[position.reshape(-1)].set(token_index.reshape(-1))
    return (position.reshape(TOKENS, TOPK), slot_table.reshape(ROUTED, SEQS * CAP))

def update(weight, moment, average, gradient, step_rate):
    decayed = gradient + decay_rate * weight
    moment_new = momentum_rate * moment + decayed
    weight_new = weight - step_rate * (decayed + momentum_rate * moment_new)
    average_new = average + (weight_new - average) / (STEP + 1.0)
    return (gradient, weight_new, moment_new, average_new, weight_new.astype(jnp.bfloat16))

def reference(tokens, cotangent, lengths, choices, attn_weight, attn_moment, attn_average, router_weight, router_moment, router_average, shared_weight, shared_moment, shared_average, routed_weight, routed_moment, routed_average, norm_gains, gain_moment, gain_average):
    position, slot_table = routing_tables(choices)
    seq_positions = jnp.arange(TOKENS, dtype=jnp.int32) % SEQ_LEN
    valid_rows = (seq_positions < jnp.repeat(lengths, SEQ_LEN)).astype(jnp.float32)[:, None]
    choice_table = (choices[:, :, None] == jnp.arange(ROUTED, dtype=jnp.int32)[None, None, :]).astype(jnp.float32)

    def forward(residual_in, attn_master, router_master, shared_master, routed_master, gain_master):
        attn_low = low(attn_master)
        router_low = low(router_master)
        shared_low = low(shared_master)
        routed_low = low(routed_master)
        gain_low = low(gain_master)

        def one_sequence(inputs_pair):
            return attention_branch(inputs_pair[0], inputs_pair[1], attn_low, gain_low[0])
        attn_out = lax.map(jax.checkpoint(one_sequence), (residual_in.reshape(SEQS, SEQ_LEN, D), lengths)).reshape(TOKENS, D)
        hidden_state = residual_in + attn_out
        normed = low(rms_norm(hidden_state, gain_low[1]))
        logits = jnp.dot(normed, router_low, precision=highest_precision)
        chosen = lax.optimization_barrier(jnp.sum(logits[:, None, :] * choice_table, axis=2))
        chosen_exp = jnp.exp(chosen - lax.optimization_barrier(jnp.max(chosen, axis=1, keepdims=True)))
        gate_weights = chosen_exp / lax.optimization_barrier(jnp.sum(chosen_exp, axis=1, keepdims=True))
        shared_gate = low_back(jnp.dot(normed, shared_low[0], precision=highest_precision))
        shared_up = low_back(jnp.dot(normed, shared_low[1], precision=highest_precision))
        shared_hidden = low(jax.nn.silu(shared_gate) * shared_up)
        shared_out = low_back(jnp.dot(shared_hidden, shared_low[2].T, precision=highest_precision))

        def one_expert(inputs_pair):
            expert_w, expert_rows = inputs_pair
            present = (expert_rows >= 0)[:, None]
            gathered = low_back(jnp.where(present, normed[jnp.maximum(expert_rows, 0)], 0.0))
            pre_gate = low_back(jnp.dot(gathered, expert_w[0], precision=highest_precision))
            pre_up = low_back(jnp.dot(gathered, expert_w[1], precision=highest_precision))
            hidden = low(jax.nn.silu(pre_gate) * pre_up)
            return low(low_back(jnp.dot(hidden, expert_w[2].T, precision=highest_precision)))
        expert_out = lax.map(jax.checkpoint(one_expert), (routed_low, slot_table))
        picked = expert_out.reshape(ROUTED * SEQS * CAP, D)[position.reshape(-1)].reshape(TOKENS, TOPK, D)
        routed_sum = lax.optimization_barrier(jnp.sum(gate_weights[:, :, None] * picked, axis=1))
        return hidden_state + shared_out + routed_sum
    block_value, pullback = jax.vjp(forward, tokens.astype(jnp.float32), attn_weight, router_weight, shared_weight, routed_weight, norm_gains)
    gradients = pullback(cotangent.astype(jnp.float32) * valid_rows)
    input_grad = gradients[0]
    step_root = 1.0 / math.sqrt(TOKENS)
    attn_parts = update(attn_weight, attn_moment, attn_average, gradients[1], rate_attention * step_root)
    router_parts = update(router_weight, router_moment, router_average, gradients[2], rate_router * step_root)
    shared_parts = update(shared_weight, shared_moment, shared_average, gradients[3], rate_shared * step_root)
    routed_parts = update(routed_weight, routed_moment, routed_average, gradients[4], rate_routed * step_root)
    gain_parts = update(norm_gains, gain_moment, gain_average, gradients[5], rate_gains * step_root)
    denominator = D * jnp.sum(lengths).astype(jnp.float32)
    masked_rms = jnp.stack([jnp.sqrt(jnp.sum(valid_rows * block_value * block_value) / denominator), jnp.sqrt(jnp.sum(valid_rows * input_grad * input_grad) / denominator)])
    return (block_value.astype(jnp.bfloat16), input_grad, masked_rms, attn_parts[0], attn_parts[1], attn_parts[2], attn_parts[3], attn_parts[4], router_parts[0], router_parts[1], router_parts[2], router_parts[3], router_parts[4], shared_parts[0], shared_parts[1], shared_parts[2], shared_parts[3], shared_parts[4], routed_parts[0], routed_parts[1], routed_parts[2], routed_parts[3], routed_parts[4], gain_parts[0], gain_parts[1], gain_parts[2], gain_parts[3])
```

```python
import functools
import math

import jax
import jax.numpy as jnp
from jax import lax
from jax.experimental import pallas as pl
from jax.experimental.pallas import tpu as pltpu
from jax.sharding import PartitionSpec as P

HEADS = 10
STEP = 3
BF = jnp.bfloat16
F32 = jnp.float32
BOTH = ("dp", "expert")


eps_norm = 1e-06
momentum_rate = 0.9
decay_rate = 0.0001
rate_attention = 0.01
rate_router = 0.03
rate_shared = 0.01
rate_routed = 0.04
rate_gains = 0.2
masked_score = -1e30
block_limit = 512


def norm_forward(values, gain_row):
    inverse = lax.rsqrt(jnp.mean(values * values, axis=-1, keepdims=True) + eps_norm)
    normal_part = values * inverse
    return (normal_part * gain_row, normal_part, inverse)


def norm_backward(grad_out, normal_part, inverse, gain_row):
    grad_hat = grad_out * gain_row
    grad_in = inverse * (
        grad_hat - normal_part * jnp.mean(grad_hat * normal_part, axis=-1, keepdims=True)
    )
    return (grad_in, jnp.sum(grad_out * normal_part, axis=0))


def rotate(values, positions, direction):
    half_dim = values.shape[-1] // 2
    frequency = 10000.0 ** (-jnp.arange(half_dim, dtype=F32) / half_dim)
    angles = positions.astype(F32)[:, None] * frequency[None, :]
    cosine = jnp.cos(angles)[:, None, :]
    sine_part = direction * jnp.sin(angles)[:, None, :]
    first_half = values[..., :half_dim]
    second_half = values[..., half_dim:]
    return jnp.concatenate(
        [
            first_half * cosine - second_half * sine_part,
            second_half * cosine + first_half * sine_part,
        ],
        axis=-1,
    )


def silu_slope(pre_value):
    sigmoid_part = jax.nn.sigmoid(pre_value)
    return sigmoid_part * (1.0 + pre_value * (1.0 - sigmoid_part))


def update(weight, moment, average, gradient, step_rate):
    decayed = gradient + decay_rate * weight
    moment_new = momentum_rate * moment + decayed
    weight_new = weight - step_rate * (decayed + momentum_rate * moment_new)
    average_new = average + (weight_new - average) / (STEP + 1.0)
    return (gradient, weight_new, moment_new, average_new, weight_new.astype(BF))


def dot_nn(a,b): return lax.dot_general(a,b,(((1,),(0,)),((),())),preferred_element_type=F32)
def dot_nt(a,b): return lax.dot_general(a,b,(((1,),(1,)),((),())),preferred_element_type=F32)
def dot_tn(a,b): return lax.dot_general(a,b,(((0,),(0,)),((),())),preferred_element_type=F32)

def chunks(n,c): return [(s,min(c,n-s)) for s in range(0,n,c)]

def expert_kernel(first, n_seq, sps, *refs):
    it=iter(refs)
    eid_ref=next(it); choice_ref=next(it); slot_ref=next(it); router_ref=next(it); w_hbm=next(it)
    sec_hbm=[next(it) for _ in range(n_seq)]
    dout_hbm=[next(it) for _ in range(n_seq)]
    prev=None
    if not first: prev=[next(it) for _ in range(4)]
    outs=[next(it) for _ in range(4)]
    dg_ref=next(it); wg_hbm=next(it)
    w_v,tok,rows_v,dy_v,h_v,da_v,db_v,ob,wsem,tsem,osem,gsem=it
    n_dp=w_hbm.shape[0]; slab=w_hbm.shape[2]
    seq=slot_ref.shape[1]
    width=sec_hbm[0].shape[1]
    ff=w_v.shape[2]
    cap=rows_v.shape[0]//n_seq
    steps=n_seq//sps
    def wcopy(d,j): return pltpu.make_async_copy(w_hbm.at[d,j], w_v.at[j,pl.ds(d*slab,slab)], wsem.at[d,j])
    def tcopy(k,q,j,slot):
        src=(sec_hbm if j==0 else dout_hbm)[k*sps+q]
        return pltpu.make_async_copy(src.at[pl.ds(0,seq)], tok.at[slot,q,j], tsem.at[slot,q,j])
    def ocopy(p,q,j):
        return pltpu.make_async_copy(ob.at[q,j], outs[2*j+q].at[p], osem.at[q,j])
    def pcopy(p,q,j):
        return pltpu.make_async_copy(prev[2*j+q].at[p], ob.at[q,j], gsem.at[q,j])
    for q in range(sps):
        for j in range(2): tcopy(0,q,j,0).start()
    for j in range(3):
        for d in range(n_dp): wcopy(d,j).start()
    lane=lax.broadcasted_iota(jnp.int32,(seq,128),1)
    sub=lax.broadcasted_iota(jnp.int32,(cap,seq),0)
    eid=eid_ref[0]; loc=eid_ref[1]
    def step(p,carry):
        slot=lax.rem(p,2)
        for k in range(1,steps):
            @pl.when(p+1==k)
            def _():
                for q in range(sps):
                    for j in range(2): tcopy(k,q,j,lax.rem(k,2)).start()
        for q in range(sps):
            for j in range(2): tcopy(0,q,j,slot).wait()
        @pl.when(p>0)
        def _():
            for q in range(sps):
                for j in range(2): ocopy(p-1,q,j).wait()
        if not first:
            for q in range(sps):
                for j in range(2): pcopy(p,q,j).start()
        base=pl.multiple_of(p*sps*cap,sps*cap)
        gcols=[];onehots=[]
        for q in range(sps):
            sec=tok[slot,q,0]
            r=p*sps+q
            logits=dot_nt(sec,router_ref[...])
            ch=choice_ref[r]
            table=ch[:,0:1]==lane
            for k in range(1,ch.shape[1]): table=table|(ch[:,k:k+1]==lane)
            masked=jnp.where(table,logits,-1e30)
            ex=jnp.exp(masked-jnp.max(masked,axis=1,keepdims=True))
            ex=jnp.where(table,ex,0.0)
            gates=ex/jnp.sum(ex,axis=1,keepdims=True)
            gcol=jnp.sum(jnp.where(lane==eid,gates,0.0),axis=1,keepdims=True)
            onehot=(slot_ref[pl.ds(r,1),:]==sub).astype(F32).astype(BF)
            rows_v[pl.ds(base+q*cap,cap),:]=dot_nn(onehot,sec).astype(BF)
            gd=(gcol*tok[slot,q,1].astype(F32)).astype(BF)
            dy_v[pl.ds(base+q*cap,cap),:]=dot_nn(onehot,gd).astype(BF)
            gcols.append(gcol); onehots.append(onehot)
        @pl.when(p==0)
        def _():
            for j in range(3):
                for d in range(n_dp): wcopy(d,j).wait()
        win=pl.ds(base,sps*cap)
        for c0,cn in chunks(ff,256):
            cs=slice(c0,c0+cn)
            rows2=rows_v[win,:]
            a=dot_nn(rows2,w_v[0,:,cs]); b=dot_nn(rows2,w_v[1,:,cs]); dh=dot_nn(dy_v[win,:],w_v[2,:,cs])
            sig=1.0/(1.0+jnp.exp(-a))
            silu=a*sig
            h_v[win,cs]=(silu*b).astype(BF)
            da_v[win,cs]=(dh*b*(sig*(1.0+a*(1.0-sig)))).astype(BF)
            db_v[win,cs]=(dh*silu).astype(BF)
        if not first:
            for q in range(sps):
                for j in range(2): pcopy(p,q,j).wait()
        dgs=[jnp.zeros((seq,1),F32) for _ in range(sps)]
        for n0,nn in chunks(width,256):
            ns=slice(n0,n0+nn)
            y=dot_nt(h_v[win,:],w_v[2,ns,:]).astype(BF)
            dr=(dot_nt(da_v[win,:],w_v[0,ns,:])+dot_nt(db_v[win,:],w_v[1,ns,:])).astype(BF)
            for q in range(sps):
                yt=dot_tn(onehots[q],y[q*cap:(q+1)*cap])
                dt=dot_tn(onehots[q],dr[q*cap:(q+1)*cap])
                dgs[q]=dgs[q]+jnp.sum(tok[slot,q,1,:,ns].astype(F32)*yt,axis=1,keepdims=True)
                yt=yt*gcols[q]
                if not first:
                    yt=yt+ob[q,0,:,ns].astype(F32); dt=dt+ob[q,1,:,ns].astype(F32)
                ob[q,0,:,ns]=yt.astype(BF); ob[q,1,:,ns]=dt.astype(BF)
        for q in range(sps):
            r=p*sps+q
            dgt=jnp.transpose(jnp.where(lane==0,dgs[q],0.0))
            dg_ref[r]=dgt[0:8,:]
            for j in range(2): ocopy(p,q,j).start()
        return carry
    lax.fori_loop(0,steps,step,0)
    for q in range(sps):
        for j in range(2): ocopy(0,q,j).wait()
    def wg(i,carry):
        m=pl.ds(pl.multiple_of(i*256,256),256)
        rt=rows_v[:,m]
        w_v[0,m,:]=dot_tn(rt,da_v[...]).astype(BF)
        w_v[1,m,:]=dot_tn(rt,db_v[...]).astype(BF)
        w_v[2,m,:]=dot_tn(dy_v[:,m],h_v[...]).astype(BF)
        return carry
    lax.fori_loop(0,width//256,wg,0)
    def gcopy(d,j): return pltpu.make_async_copy(w_v.at[j,pl.ds(d*slab,slab)], wg_hbm.at[d,j], wsem.at[d,j])
    for j in range(3):
        for d in range(n_dp): gcopy(d,j).start()
    for j in range(3):
        for d in range(n_dp): gcopy(d,j).wait()

def expert_call(eid, choice_rel, slots, router_pad, w, secs, douts, prev, cap):
    n_seq=len(secs); sps=2
    seq=slots.shape[1]
    width=secs[0].shape[1]
    n_dp,_,slab,ff=w.shape
    first=prev is None
    ANY=pl.BlockSpec(memory_space=pl.ANY); VM=pl.BlockSpec(memory_space=pltpu.VMEM); SM=pl.BlockSpec(memory_space=pltpu.SMEM)
    args=[eid,choice_rel,slots,router_pad,w,*secs,*douts]+([] if first else list(prev))
    in_specs=[SM,VM,VM,VM]+[ANY]*(len(args)-4)
    half=jax.ShapeDtypeStruct((n_seq//2,seq,width),BF)
    out_shape=[half]*4+[jax.ShapeDtypeStruct((n_seq,8,seq),F32),jax.ShapeDtypeStruct(w.shape,BF)]
    out_specs=[ANY]*4+[VM,ANY]
    R=n_seq*cap
    scratch=[pltpu.VMEM((3,width,ff),BF),pltpu.VMEM((2,sps,2,seq,width),BF),pltpu.VMEM((R,width),BF),pltpu.VMEM((R,width),BF),
      pltpu.VMEM((R,ff),BF),pltpu.VMEM((R,ff),BF),pltpu.VMEM((R,ff),BF),pltpu.VMEM((sps,2,seq,width),BF),
      pltpu.SemaphoreType.DMA((n_dp,3)),pltpu.SemaphoreType.DMA((2,sps,2)),pltpu.SemaphoreType.DMA((sps,2)),pltpu.SemaphoreType.DMA((sps,2))]
    fl=2*R*width*ff*9+2*4*n_seq*cap*seq*width
    return pl.pallas_call(functools.partial(expert_kernel,first,n_seq,sps),out_shape=out_shape,in_specs=in_specs,out_specs=out_specs,
      scratch_shapes=scratch,compiler_params=pltpu.CompilerParams(vmem_limit_bytes=62*1024*1024),
      cost_estimate=pl.CostEstimate(flops=fl,bytes_accessed=60_000_000,transcendentals=R*ff),name="routed_expert")(*args)


def permute(values, pairs):
    return lax.ppermute(values, "expert", pairs)


def pairs_of(mask, count):
    return [(i, i ^ mask) for i in range(count)]


def mixed_pairs(even_mask, odd_mask, count):
    return [(i, i ^ (odd_mask if i % 2 else even_mask)) for i in range(count)]


def after(values, *others):
    return lax.optimization_barrier((values, others))[0]


def ring_pairs():
    count = lax.axis_size("dp")
    return [(i, (i + 1) % count) for i in range(count)]


def gather_ring(own):
    count = lax.axis_size("dp")
    here = lax.axis_index("dp")
    whole = jnp.zeros((count,) + own.shape, own.dtype)
    origin = (0,) * own.ndim
    for step in range(count):
        whole = lax.dynamic_update_slice(whole, own[None], (lax.rem(here - step + count, count),) + origin)
        if step < count - 1:
            own = lax.ppermute(own, "dp", ring_pairs())
    return whole


def scatter_ring(terms):
    count = lax.axis_size("dp")
    here = lax.axis_index("dp")
    take = lambda step: lax.dynamic_index_in_dim(terms, lax.rem(here - step + count, count), axis=0, keepdims=False)
    held = take(1)
    for step in range(1, count):
        arrived = lax.ppermute(held, "dp", ring_pairs())
        total = arrived.astype(F32) + take(step + 1 if step < count - 1 else 0).astype(F32)
        held = total.astype(terms.dtype)
    return total


def total_of(values):
    for axis in ("expert", "dp"):
        step = 1
        while step < lax.axis_size(axis):
            values = values + lax.ppermute(values, axis, [(i, i ^ step) for i in range(lax.axis_size(axis))])
            step *= 2
    return values


def gather_chips(own, is_core0):
    count = lax.axis_size("expert")
    from_x = permute(own, pairs_of(2, count))
    from_y = permute(own, pairs_of(4, count))
    onward = jnp.where(is_core0, from_x, from_y)
    from_far = permute(onward, mixed_pairs(4, 2, count))
    return [own, from_x, from_y, from_far]


def gather_plane(own, is_core0):
    count = lax.axis_size("expert")
    found = []
    for piece in gather_chips(own, is_core0):
        found += [piece, permute(piece, pairs_of(1, count))]
    return found


def reduce_plane(even, odd, is_core0):
    count = lax.axis_size("expert")
    kind = even.dtype
    other = permute(odd, pairs_of(1, count))
    both = even.astype(F32) + other.astype(F32)
    far = permute(both[3].astype(kind), mixed_pairs(4, 2, count)).astype(F32)
    to_x = (both[1] + jnp.where(is_core0, far, 0.0)).astype(kind)
    to_y = (both[2] + jnp.where(is_core0, 0.0, far)).astype(kind)
    return both[0] + permute(to_x, pairs_of(2, count)).astype(F32) + permute(to_y, pairs_of(4, count)).astype(F32)


def place_rows(pieces, me):
    parts, rows, width = pieces[0].shape
    whole = jnp.zeros((parts, len(pieces), rows, width), pieces[0].dtype)
    for r, piece in enumerate(pieces):
        whole = lax.dynamic_update_slice(whole, piece[:, None], (0, me ^ r, 0, 0))
    return whole.reshape(parts * len(pieces) * rows, width)


def scatter_rows(whole, me, is_core0, kind):
    parts, count = lax.axis_size("dp"), lax.axis_size("expert")
    rows = whole.shape[0] // (parts * count)
    cut = whole.reshape(parts, count, rows, whole.shape[1])
    take = lambda r: lax.dynamic_index_in_dim(cut, me ^ r, axis=1, keepdims=False).astype(kind)
    even = jnp.stack([take(r) for r in range(0, count, 2)])
    odd = jnp.stack([take(r) for r in range(1, count, 2)])
    return scatter_ring(reduce_plane(even, odd, is_core0).astype(kind))


def scatter_dp(values):
    return lax.psum_scatter(values, "dp", scatter_dimension=0, tiled=False).astype(F32)


def local(
    tokens,
    cotangent,
    lengths,
    choices,
    attn_weight,
    attn_moment,
    attn_average,
    router_weight,
    router_moment,
    router_average,
    shared_weight,
    shared_moment,
    shared_average,
    routed_weight,
    routed_moment,
    routed_average,
    norm_gains,
    gain_moment,
    gain_average,
):
    seq_len, model_width = tokens.shape
    topk_count = choices.shape[1]
    head_dim = model_width // HEADS
    groups = lax.axis_size("expert")
    routed_count = routed_weight.shape[0] * groups
    capacity = (seq_len * topk_count * 8 // (7 * routed_count) + 7) // 8 * 8
    total_tokens = seq_len * groups * lax.axis_size("dp")
    step_root = 1.0 / math.sqrt(total_tokens)
    score_scale = 1.0 / math.sqrt(head_dim)
    block_rows = min(seq_len, block_limit)
    block_count = seq_len // block_rows
    me = lax.axis_index("expert")
    is_core0 = lax.rem(me, 2) == 0
    relative = me ^ jnp.arange(groups, dtype=jnp.int32)
    per_device = routed_weight.shape[0]
    positions = jnp.arange(seq_len, dtype=jnp.int32)
    length_here = lengths[0]
    valid_rows = (positions < length_here).astype(F32)[:, None]
    grad_out = cotangent.astype(F32) * valid_rows
    grad_out16 = grad_out.astype(BF)

    routed16 = [lax.all_gather(routed_weight[e].astype(BF), "dp", axis=0, tiled=False) for e in range(per_device)]
    small = jnp.pad(jnp.concatenate([router_weight, norm_gains.T], axis=1).astype(BF), ((0, 0), (0, 110)))
    small_cut = gather_ring(small)
    small_all = place_rows(gather_plane(small_cut, is_core0), me)
    small_all = small_all.T
    router16t = small_all[:routed_count]
    gains16 = small_all[routed_count : routed_count + 2]
    attn16 = []
    pieces = gather_plane(gather_ring(attn_weight[:2].astype(BF)), is_core0)
    attn16 += [place_rows([p[:, j] for p in pieces], me) for j in range(2)]
    pieces = gather_plane(gather_ring(attn_weight[2:].astype(BF)), is_core0)
    attn16 += [place_rows([p[:, j] for p in pieces], me) for j in range(2)]

    choice_rows = jnp.pad(choices.T.astype(BF), ((0, 16 - topk_count), (0, model_width - seq_len)))
    marked = jnp.concatenate([grad_out16, choice_rows], axis=0)
    grads_all = gather_plane(after(marked, pieces[6]), is_core0)
    pieces = gather_plane(gather_ring(shared_weight.astype(BF)), is_core0)
    shared16 = [place_rows([p[:, j] for p in pieces], me) for j in range(3)]

    choice_all = jnp.stack([g[seq_len : seq_len + topk_count, :seq_len] for g in grads_all]).astype(jnp.int32)
    own_experts = me * per_device + jnp.arange(per_device, dtype=jnp.int32)
    hits = jnp.any(choice_all[:, None] == own_experts[None, :, None, None], axis=2)
    before = (positions[:, None] < positions[None, :]).astype(BF)
    ranks = jnp.einsum("set,tu->seu", hits.astype(BF), before, preferred_element_type=F32).astype(jnp.int32)
    slot_all = jnp.where(hits, ranks, -1)
    choice_all = jnp.transpose(choice_all, (0, 2, 1))
    gain_first = gains16[0].astype(F32)
    gain_second = gains16[1].astype(F32)
    key_positions = positions[None, :]
    residual_in = tokens.astype(F32)
    normed_first, hat_first, inverse_first = norm_forward(residual_in, gain_first)
    first16 = normed_first.astype(BF)
    query_linear = jnp.dot(first16, attn16[0], preferred_element_type=F32)
    key_linear = jnp.dot(first16, attn16[1], preferred_element_type=F32)
    value_linear = jnp.dot(first16, attn16[2], preferred_element_type=F32)
    query16 = rotate(query_linear.reshape(seq_len, HEADS, head_dim), positions, 1.0).astype(
        BF
    )
    key16 = rotate(key_linear.reshape(seq_len, HEADS, head_dim), positions, 1.0).astype(
        BF
    )
    value16 = value_linear.reshape(seq_len, HEADS, head_dim).astype(BF)

    def block_scores(start_row):
        scores = (
            jnp.einsum("qhd,khd->hqk", query16, key16, preferred_element_type=F32)
            * score_scale
        )
        query_positions = start_row + jnp.arange(block_rows, dtype=jnp.int32)[:, None]
        allowed = (key_positions <= query_positions) & (key_positions < length_here)
        return (query16, jnp.where(allowed[None], scores, masked_score))

    def forward_block(block_index):
        query_block, masked = block_scores(block_index * block_rows)
        row_peak = jnp.max(masked, axis=-1, keepdims=True)
        exp_part = jnp.exp(masked - row_peak)
        row_total = jnp.sum(exp_part, axis=-1, keepdims=True)
        probs16 = (exp_part / row_total).astype(BF)
        context = jnp.einsum("hqk,khd->qhd", probs16, value16, preferred_element_type=F32)
        return (context.astype(BF), (row_peak + jnp.log(row_total))[..., 0])

    contexts, log_totals = lax.map(forward_block, jnp.arange(block_count))
    context16 = contexts.reshape(seq_len, model_width)
    attn_out = jnp.dot(context16, attn16[3], preferred_element_type=F32)
    hidden_state = residual_in + attn_out
    normed_second, hat_second, inverse_second = norm_forward(hidden_state, gain_second)
    second16 = normed_second.astype(BF)
    seconds_all = gather_plane(second16, is_core0)
    router_pad = jnp.pad(router16t, ((0, 128 - routed_count), (0, 0)))
    partial = None
    gate_grads, routed_grads = [], []
    for e in range(per_device):
        ids = jnp.stack([own_experts[e], own_experts[e]])
        *partial, gate_part, weight_part = expert_call(
            ids, choice_all, slot_all[:, e], router_pad, routed16[e], seconds_all, grads_all, partial, capacity
        )
        gate_grads.append(gate_part[:, 0])
        routed_grads.append(scatter_dp(weight_part))
    routed_sum = reduce_plane(partial[0], partial[1], is_core0)
    routed_back = reduce_plane(partial[2], partial[3], is_core0)
    gate_sent = jnp.take(jnp.stack(gate_grads, axis=1), relative, axis=0)
    gate_back = lax.all_to_all(gate_sent, "expert", split_axis=0, concat_axis=0, tiled=True)
    grad_gate = gate_back.reshape(routed_count, seq_len).T

    logits = lax.dot_general(second16, router16t, (((1,), (1,)), ((), ())), preferred_element_type=F32)
    table = jnp.any(choices[:, :, None] == jnp.arange(routed_count, dtype=jnp.int32)[None, None, :], axis=1)
    chosen = jnp.where(table, logits, masked_score)
    chosen_exp = jnp.where(table, jnp.exp(chosen - jnp.max(chosen, axis=1, keepdims=True)), 0.0)
    gate_weights = chosen_exp / jnp.sum(chosen_exp, axis=1, keepdims=True)
    shared_gate = jnp.dot(second16, shared16[0], preferred_element_type=F32)
    shared_up = jnp.dot(second16, shared16[1], preferred_element_type=F32)
    shared_hidden = (jax.nn.silu(shared_gate) * shared_up).astype(BF)
    shared_out = jnp.einsum(
        "lf,df->ld", shared_hidden, shared16[2], preferred_element_type=F32
    )
    block_value = hidden_state + shared_out + routed_sum
    grad_shared_hidden = jnp.dot(grad_out16, shared16[2], preferred_element_type=F32)
    grad_shared_gate16 = (grad_shared_hidden * shared_up * silu_slope(shared_gate)).astype(
        BF
    )
    grad_shared_up16 = (grad_shared_hidden * jax.nn.silu(shared_gate)).astype(BF)
    shared_grads = (
        [
            jnp.einsum(
                "ld,lf->df", second16, grad_shared_gate16, preferred_element_type=F32
            ),
            jnp.einsum("ld,lf->df", second16, grad_shared_up16, preferred_element_type=F32),
            jnp.einsum("ld,lf->df", grad_out16, shared_hidden, preferred_element_type=F32),
        ]
    )
    grad_second = jnp.einsum(
        "lf,df->ld", grad_shared_gate16, shared16[0], preferred_element_type=F32
    )
    grad_second = grad_second + jnp.einsum(
        "lf,df->ld", grad_shared_up16, shared16[1], preferred_element_type=F32
    )
    routed_back, early = lax.optimization_barrier((routed_back, routed_grads[0]))
    routed_grad_shard = jnp.stack([early] + routed_grads[1:])
    grad_second = grad_second + routed_back
    gate_mean = jnp.sum(gate_weights * grad_gate, axis=1, keepdims=True)
    grad_logits = gate_weights * (grad_gate - gate_mean)
    router_float = router16t.astype(F32)
    grad_second = grad_second + jnp.dot(grad_logits, router_float, precision=lax.Precision.HIGHEST)
    router_grad_full = lax.dot_general(
        grad_logits, second16.astype(F32), (((0,), (0,)), ((), ())), precision=lax.Precision.HIGHEST
    )
    grad_norm_second, grad_gain_second = norm_backward(
        grad_second, hat_second, inverse_second, gain_second
    )
    grad_hidden_state = grad_out + grad_norm_second
    grad_attn16 = grad_hidden_state.astype(BF)
    grad_out_proj = jnp.einsum(
        "ld,le->de", context16, grad_attn16, preferred_element_type=F32
    )
    grad_context16 = (
        jnp.einsum("le,de->ld", grad_attn16, attn16[3], preferred_element_type=F32)
        .astype(BF)
        .reshape(seq_len, HEADS, head_dim)
    )

    def backward_block(carried, inputs):
        grad_keys, grad_values = carried
        block_index, log_block = inputs
        start_row = block_index * block_rows
        query_block, masked = block_scores(start_row)
        probability = jnp.exp(masked - log_block[..., None])
        grad_probs = jnp.einsum(
            "qhd,khd->hqk", grad_context16, value16, preferred_element_type=F32
        )
        row_delta = jnp.sum(probability * grad_probs, axis=-1, keepdims=True)
        grad_scores16 = (probability * (grad_probs - row_delta)).astype(BF)
        grad_query = (
            jnp.einsum("hqk,khd->qhd", grad_scores16, key16, preferred_element_type=F32)
            * score_scale
        )
        grad_keys = (
            grad_keys
            + jnp.einsum(
                "hqk,qhd->khd", grad_scores16, query_block, preferred_element_type=F32
            )
            * score_scale
        )
        grad_values = grad_values + jnp.einsum(
            "hqk,qhd->khd",
            probability.astype(BF),
            grad_context16,
            preferred_element_type=F32,
        )
        return ((grad_keys, grad_values), grad_query)

    zero_heads = jnp.zeros((seq_len, HEADS, head_dim), F32)
    (grad_keys, grad_values), grad_queries = lax.scan(
        backward_block, (zero_heads, zero_heads), (jnp.arange(block_count), log_totals)
    )
    grad_query16 = (
        rotate(grad_queries.reshape(seq_len, HEADS, head_dim), positions, -1.0)
        .reshape(seq_len, model_width)
        .astype(BF)
    )
    grad_key16 = (
        rotate(grad_keys, positions, -1.0).reshape(seq_len, model_width).astype(BF)
    )
    grad_value16 = grad_values.reshape(seq_len, model_width).astype(BF)
    attn_grads = (
        [
            jnp.einsum("ld,le->de", first16, grad_query16, preferred_element_type=F32),
            jnp.einsum("ld,le->de", first16, grad_key16, preferred_element_type=F32),
            jnp.einsum("ld,le->de", first16, grad_value16, preferred_element_type=F32),
            grad_out_proj,
        ]
    )
    grad_first = jnp.einsum(
        "le,de->ld", grad_query16, attn16[0], preferred_element_type=F32
    )
    grad_first = grad_first + jnp.einsum(
        "le,de->ld", grad_key16, attn16[1], preferred_element_type=F32
    )
    grad_first = grad_first + jnp.einsum(
        "le,de->ld", grad_value16, attn16[2], preferred_element_type=F32
    )
    grad_norm_first, grad_gain_first = norm_backward(
        grad_first, hat_first, inverse_first, gain_first
    )
    input_grad = grad_hidden_state + grad_norm_first
    scalars = jnp.stack(
        [
            jnp.sum(valid_rows * block_value * block_value),
            jnp.sum(valid_rows * input_grad * input_grad),
            length_here.astype(F32),
        ]
    )
    row_sums = total_of(scalars)
    small_grads = jnp.concatenate([router_grad_full, grad_gain_first[None], grad_gain_second[None]])
    small_grads = jnp.pad(small_grads, ((0, 128 - small_grads.shape[0]), (0, 0))).T
    small_grad = scatter_rows(small_grads, me, is_core0, F32)
    router_grad = small_grad[:, :routed_count]
    gain_grad = small_grad[:, routed_count : routed_count + 2].T
    shared_grad = jnp.stack([scatter_rows(g, me, is_core0, BF) for g in shared_grads])
    attn_grad = jnp.stack([scatter_rows(g, me, is_core0, BF) for g in attn_grads])
    denominator = model_width * row_sums[2]
    masked_rms = jnp.stack(
        [jnp.sqrt(row_sums[0] / denominator), jnp.sqrt(row_sums[1] / denominator)]
    )
    attn_parts = update(
        attn_weight, attn_moment, attn_average, attn_grad, rate_attention * step_root
    )
    router_parts = update(
        router_weight, router_moment, router_average, router_grad, rate_router * step_root
    )
    shared_parts = update(
        shared_weight, shared_moment, shared_average, shared_grad, rate_shared * step_root
    )
    routed_parts = update(
        routed_weight, routed_moment, routed_average, routed_grad_shard, rate_routed * step_root
    )
    gain_parts = update(norm_gains, gain_moment, gain_average, gain_grad, rate_gains * step_root)
    return (
        block_value.astype(BF),
        input_grad,
        masked_rms,
        attn_parts[0],
        attn_parts[1],
        attn_parts[2],
        attn_parts[3],
        attn_parts[4],
        router_parts[0],
        router_parts[1],
        router_parts[2],
        router_parts[3],
        router_parts[4],
        shared_parts[0],
        shared_parts[1],
        shared_parts[2],
        shared_parts[3],
        shared_parts[4],
        routed_parts[0],
        routed_parts[1],
        routed_parts[2],
        routed_parts[3],
        routed_parts[4],
        gain_parts[0],
        gain_parts[1],
        gain_parts[2],
        gain_parts[3],
    )


def solution(mesh):
    placed = (
        P(("dp", "expert"), None),
        P(("dp", "expert"), None),
        P(("dp", "expert")),
        P(("dp", "expert"), None),
        P(None, ("dp", "expert"), None),
        P(None, ("dp", "expert"), None),
        P(None, ("dp", "expert"), None),
        P(("dp", "expert"), None),
        P(("dp", "expert"), None),
        P(("dp", "expert"), None),
        P(None, ("dp", "expert"), None),
        P(None, ("dp", "expert"), None),
        P(None, ("dp", "expert"), None),
        P("expert", None, "dp", None),
        P("expert", None, "dp", None),
        P("expert", None, "dp", None),
        P(None, ("dp", "expert")),
        P(None, ("dp", "expert")),
        P(None, ("dp", "expert")),
    )
    return jax.shard_map(
        local,
        mesh=mesh,
        in_specs=placed,
        out_specs=(
            P(("dp", "expert"), None),
            P(("dp", "expert"), None),
            P(),
            P(None, ("dp", "expert"), None),
            P(None, ("dp", "expert"), None),
            P(None, ("dp", "expert"), None),
            P(None, ("dp", "expert"), None),
            P(None, ("dp", "expert"), None),
            P(("dp", "expert"), None),
            P(("dp", "expert"), None),
            P(("dp", "expert"), None),
            P(("dp", "expert"), None),
            P(("dp", "expert"), None),
            P(None, ("dp", "expert"), None),
            P(None, ("dp", "expert"), None),
            P(None, ("dp", "expert"), None),
            P(None, ("dp", "expert"), None),
            P(None, ("dp", "expert"), None),
            P("expert", None, "dp", None),
            P("expert", None, "dp", None),
            P("expert", None, "dp", None),
            P("expert", None, "dp", None),
            P("expert", None, "dp", None),
            P(None, ("dp", "expert")),
            P(None, ("dp", "expert")),
            P(None, ("dp", "expert")),
            P(None, ("dp", "expert")),
        ),
        check_vma=False,
    )
```

```python
import functools
import math

import jax
import jax.numpy as jnp
from jax import lax
from jax.experimental import pallas as pl
from jax.experimental.layout import Layout, with_layout_constraint
from jax.experimental.pallas import tpu as pltpu
from jax.sharding import PartitionSpec as P

HEADS = 10
STEP = 3
BF = jnp.bfloat16
F32 = jnp.float32
BOTH = ("dp", "expert")


eps_norm = 1e-06
momentum_rate = 0.9
decay_rate = 0.0001
rate_attention = 0.01
rate_router = 0.03
rate_shared = 0.01
rate_routed = 0.04
rate_gains = 0.2
masked_score = -1e30
VMEM_LIMIT = 58 * 1024 * 1024


def silu_slope(pre_value):
    sigmoid_part = jax.nn.sigmoid(pre_value)
    return sigmoid_part * (1.0 + pre_value * (1.0 - sigmoid_part))


def update(weight, moment, average, gradient, step_rate):
    decayed = gradient + decay_rate * weight
    moment_new = momentum_rate * moment + decayed
    weight_new = weight - step_rate * (decayed + momentum_rate * moment_new)
    average_new = average + (weight_new - average) / (STEP + 1.0)
    return (gradient, weight_new, moment_new, average_new, weight_new.astype(BF))


def estimate(flops):
    return pl.CostEstimate(flops=flops, bytes_accessed=1, transcendentals=0)


def dot_nn(a,b): return lax.dot_general(a,b,(((1,),(0,)),((),())),preferred_element_type=F32)
def dot_nt(a,b): return lax.dot_general(a,b,(((1,),(1,)),((),())),preferred_element_type=F32)
def dot_tn(a,b): return lax.dot_general(a,b,(((0,),(0,)),((),())),preferred_element_type=F32)

def chunks(n,c): return [(s,min(c,n-s)) for s in range(0,n,c)]

def pair_columns(ff):
    return [(c0, cn, 2 * c0, 2 * c0 + cn) for c0, cn in chunks(ff, 256)]


def expert_pair_kernel(first, *refs):
    it = iter(refs)
    take = lambda count: [next(it) for _ in range(count)]
    eid_ref, choice_ref, slot_ref, router_ref, w_hbm = take(5)
    gate_ref = None if first else next(it)
    sources = [take(2), take(2)]
    prev = [] if first else [take(2), take(2)]
    outs = [take(2), take(2)]
    dg_ref, rows_out, dy_out, h_out, dab_out = take(5)
    gate_out = next(it) if first else None
    gu_v, down_v, tok, rows_v, dy_v, h_v, dab_v, ob, wsem, dsem, tsem, psem, osem, ssem = it
    n_dp = w_hbm.shape[0]
    width, ff = down_v.shape
    slab = width // n_dp
    seq = slot_ref.shape[1]
    cap = rows_v.shape[0] // 2
    tcopies = [[pltpu.make_async_copy(sources[j][q], tok.at[q, j], tsem.at[q, j]) for j in range(2)] for q in range(2)]
    wcopies = []
    for d in range(n_dp):
        own = pl.ds(d * slab, slab)
        for c, (c0, cn, g0, u0) in enumerate(pair_columns(ff)):
            for j, to in ((0, g0), (1, u0)):
                src = w_hbm.at[d, j, pl.ds(0, slab), pl.ds(c0, cn)]
                wcopies.append(pltpu.make_async_copy(src, gu_v.at[own, pl.ds(to, cn)], wsem.at[d, c, j]))
    dcopies = [
        pltpu.make_async_copy(w_hbm.at[d, 2, pl.ds(0, slab)], down_v.at[pl.ds(d * slab, slab)], dsem.at[d]) for d in range(n_dp)
    ]
    for copies in tcopies:
        for copy in copies:
            copy.start()
    lane = lax.broadcasted_iota(jnp.int32, (seq, 128), 1)
    sub = lax.broadcasted_iota(jnp.int32, (cap, seq), 0)
    eid = eid_ref[0]
    gcols, onehots = [], []
    for q in range(2):
        tcopies[q][0].wait()
        if q == 0:
            for copy in wcopies + dcopies:
                copy.start()
        sec = tok[q, 0]
        if first:
            logits = dot_nt(sec, router_ref[...])
            table = choice_ref[q, :, 0:1] == lane
            for k in range(1, choice_ref.shape[2]):
                table = table | (choice_ref[q, :, k : k + 1] == lane)
            masked = jnp.where(table, logits, masked_score)
            weight = jnp.where(table, jnp.exp(masked - jnp.max(masked, axis=1, keepdims=True)), 0.0)
            gates = weight / jnp.sum(weight, axis=1, keepdims=True)
            gate_out[q] = gates
        else:
            gates = gate_ref[q]
        gcol = jnp.sum(jnp.where(lane == eid, gates, 0.0), axis=1, keepdims=True)
        onehot = (slot_ref[q : q + 1, :] == sub).astype(F32).astype(BF)
        rows_v[q * cap : (q + 1) * cap, :] = dot_nn(onehot, sec).astype(BF)
        tcopies[q][1].wait()
        gated = (gcol * tok[q, 1].astype(F32)).astype(BF)
        dy_v[q * cap : (q + 1) * cap, :] = dot_nn(onehot, gated).astype(BF)
        gcols.append(gcol)
        onehots.append(onehot)
    pcopies = [pltpu.make_async_copy(prev[j][q], ob.at[q, j], psem.at[q, j]) for q in range(2) for j in range(2) if not first]
    for copy in pcopies:
        copy.start()
    saves = [pltpu.make_async_copy(rows_v, rows_out, ssem.at[0]), pltpu.make_async_copy(dy_v, dy_out, ssem.at[1])]
    for copy in saves:
        copy.start()
    for copy in wcopies + dcopies:
        copy.wait()
    gain_sum = jnp.zeros((2 * cap, 128), F32)
    for c0, cn, g0, u0 in pair_columns(ff):
        both = dot_nn(rows_v[...], gu_v[:, g0 : g0 + 2 * cn])
        a, b = both[:, :cn], both[:, cn:]
        dh = dot_nn(dy_v[...], down_v[:, c0 : c0 + cn])
        sigmoid = 0.5 * jnp.tanh(0.5 * a) + 0.5
        silu = a * sigmoid
        dsilu = dh * silu
        gain = dsilu * b
        for p0, pn in chunks(cn, 128):
            gain_sum = gain_sum + gain[:, p0 : p0 + pn]
        h_v[:, c0 : c0 + cn] = (silu * b).astype(BF)
        dab_v[:, g0 : g0 + cn] = (dh * b * (sigmoid + silu * (1.0 - sigmoid))).astype(BF)
        dab_v[:, u0 : u0 + cn] = dsilu.astype(BF)
    late = [pltpu.make_async_copy(h_v, h_out, ssem.at[2]), pltpu.make_async_copy(dab_v, dab_out, ssem.at[3])]
    for copy in late:
        copy.start()
    for copy in pcopies:
        copy.wait()
    sends = []
    gain_slot = jnp.sum(gain_sum, axis=1, keepdims=True)
    for q in range(2):
        spread = onehots[q].astype(F32) * gain_slot[q * cap : (q + 1) * cap]
        dg_ref[q] = jnp.broadcast_to(jnp.sum(spread, axis=0, keepdims=True), (8, seq))
    for n, (n0, nn) in enumerate(chunks(width, 512)):
        ns = slice(n0, n0 + nn)
        y = dot_nt(h_v[...], down_v[ns, :]).astype(BF)
        dr = dot_nt(dab_v[...], gu_v[ns, :]).astype(BF)
        for q in range(2):
            yt = dot_tn(onehots[q], y[q * cap : (q + 1) * cap])
            dt = dot_tn(onehots[q], dr[q * cap : (q + 1) * cap])
            yt = yt * gcols[q]
            if not first:
                yt = yt + ob[q, 0, :, ns].astype(F32)
                dt = dt + ob[q, 1, :, ns].astype(F32)
            ob[q, 0, :, ns] = yt.astype(BF)
            ob[q, 1, :, ns] = dt.astype(BF)
            for j in range(2):
                part = pl.ds(n0, nn)
                copy = pltpu.make_async_copy(ob.at[q, j, :, part], outs[j][q].at[:, part], osem.at[q, j, n])
                copy.start()
                sends.append(copy)
    for copy in saves + late + sends:
        copy.wait()


def expert_pair_call(eid, choice, slots, router_pad, w, secs, douts, prev, gates, cap):
    seq = slots.shape[1]
    width = secs[0].shape[1]
    n_dp, _, _, ff = w.shape
    parts = len(chunks(width, 512))
    flat = [] if prev is None else [v for pair in prev for v in pair]
    full = jax.ShapeDtypeStruct((seq, width), BF)
    shapes = [(2 * cap, width), (2 * cap, width), (2 * cap, ff), (2 * cap, 2 * ff)]
    dma = pltpu.SemaphoreType.DMA
    out = pl.pallas_call(
        functools.partial(expert_pair_kernel, prev is None),
        out_shape=[full] * 4
        + [jax.ShapeDtypeStruct((2, 8, seq), F32)]
        + [jax.ShapeDtypeStruct(shape, BF) for shape in shapes]
        + [jax.ShapeDtypeStruct((2, seq, 128), F32)] * (prev is None),
        in_specs=kernel_specs("svvva" + "v" * (prev is not None) + "a" * (4 + len(flat))),
        out_specs=kernel_specs("aaaavaaaa" + "v" * (prev is None)),
        scratch_shapes=[pltpu.VMEM((width, 2 * ff), BF), pltpu.VMEM((width, ff), BF), pltpu.VMEM((2, 2, seq, width), BF)]
        + [pltpu.VMEM(shape, BF) for shape in shapes]
        + [pltpu.VMEM((2, 2, seq, width), BF)]
        + [dma((n_dp, len(chunks(ff, 256)), 2)), dma((n_dp,)), dma((2, 2)), dma((2, 2)), dma((2, 2, parts)), dma((4,))],
        compiler_params=pltpu.CompilerParams(vmem_limit_bytes=VMEM_LIMIT),
        cost_estimate=estimate(18 * cap * width * ff),
        name="expert_pair",
    )(eid, choice, slots, router_pad, w, *([] if prev is None else [gates]), *secs, *douts, *flat)
    return (out[0:2], out[2:4]), out[4], out[5:9], out[9] if prev is None else gates


def weight_grad_kernel(count, *refs):
    saved = [refs[4 * i : 4 * i + 4] for i in range(count)]
    out_ref, rows_v, dy_v, h_v, dab_v, g_v, isem, osem = refs[4 * count :]
    width, ff = g_v.shape[1:]
    n_dp = out_ref.shape[0]
    slab = width // n_dp
    piece = rows_v.shape[0] // count
    loads = {}
    for j, to in ((1, dy_v), (2, h_v), (0, rows_v), (3, dab_v)):
        loads[j] = [
            pltpu.make_async_copy(saved[i][j], to.at[pl.ds(i * piece, piece)], isem.at[j, i]) for i in range(count)
        ]
        for copy in loads[j]:
            copy.start()
    stores = [
        [pltpu.make_async_copy(g_v.at[j, pl.ds(d * slab, slab)], out_ref.at[d, j], osem.at[j, d]) for d in range(n_dp)]
        for j in range(3)
    ]
    for copy in loads[1] + loads[2]:
        copy.wait()

    def down(i, carry):
        m = pl.ds(pl.multiple_of(i * 256, 256), 256)
        g_v[2, m, :] = dot_tn(dy_v[:, m], h_v[...]).astype(BF)
        return carry

    lax.fori_loop(0, width // 256, down, 0)
    for copy in stores[2]:
        copy.start()
    for copy in loads[0] + loads[3]:
        copy.wait()

    def front(i, carry):
        m = pl.ds(pl.multiple_of(i * 256, 256), 256)
        both = dot_tn(rows_v[:, m], dab_v[...])
        for c0, cn, g0, u0 in pair_columns(ff):
            g_v[0, m, c0 : c0 + cn] = both[:, g0 : g0 + cn].astype(BF)
            g_v[1, m, c0 : c0 + cn] = both[:, u0 : u0 + cn].astype(BF)
        return carry

    lax.fori_loop(0, width // 256, front, 0)
    for copy in stores[0] + stores[1]:
        copy.start()
    for copy in stores[0] + stores[1] + stores[2]:
        copy.wait()


def weight_grad_call(saved, n_dp):
    count = len(saved)
    width, ff = saved[0][0].shape[1], saved[0][2].shape[1]
    rows = count * saved[0][0].shape[0]
    dma = pltpu.SemaphoreType.DMA
    return pl.pallas_call(
        functools.partial(weight_grad_kernel, count),
        out_shape=jax.ShapeDtypeStruct((n_dp, 3, width // n_dp, ff), BF),
        in_specs=kernel_specs("a" * (4 * count)),
        out_specs=pl.BlockSpec(memory_space=pl.ANY),
        scratch_shapes=[pltpu.VMEM((rows, n), BF) for n in (width, width, ff, 2 * ff)]
        + [pltpu.VMEM((3, width, ff), BF), dma((4, count)), dma((3, n_dp))],
        compiler_params=pltpu.CompilerParams(vmem_limit_bytes=VMEM_LIMIT),
        cost_estimate=estimate(6 * rows * width * ff),
        name="expert_weights",
    )(*[v for part in saved for v in part])


def rotated(values, cosine, sine):
    return values * cosine + pltpu.roll(values, values.shape[1] // 2, 1) * sine


def head_block(h):
    return pl.ds(pl.multiple_of(h * 128, 128), 128)


def masked_scores(query, key, start, length, scale):
    scores = dot_nt(query, key) * scale
    at = lax.broadcasted_iota(jnp.int32, scores.shape, 0) + start
    to = lax.broadcasted_iota(jnp.int32, scores.shape, 1)
    return jnp.where((to <= at) & (to < length), scores, masked_score)


def attention_kernel(
    scale, tok_ref, gain_ref, cos_ref, sin_ref, len_ref, wq, wk, wv, wo,
    first_ref, q_ref, k_ref, v_ref, ctx_ref, lse_ref, hidden_ref, second_ref, w_v, sem,
):
    copies = [pltpu.make_async_copy(w, w_v.at[j], sem.at[j]) for j, w in enumerate((wq, wk, wv, wo))]
    for copy in copies:
        copy.start()
    seq, width = tok_ref.shape
    length = len_ref[0]
    x = tok_ref[...].astype(F32)
    inverse = lax.rsqrt(jnp.mean(x * x, axis=1, keepdims=True) + eps_norm)
    first_ref[...] = (x * inverse * gain_ref[0:1, :]).astype(BF)
    for j, out_ref in enumerate((q_ref, k_ref, v_ref)):
        copies[j].wait()
        for c0, cn in chunks(width, 256):
            lin = dot_nn(first_ref[...], w_v[j, :, c0 : c0 + cn])
            for h0, hn in chunks(cn, 128):
                part = lin[:, h0 : h0 + hn]
                if j < 2:
                    part = rotated(part, cos_ref[...], sin_ref[...])
                out_ref[:, c0 + h0 : c0 + h0 + hn] = part.astype(BF)
    lane = lax.broadcasted_iota(jnp.int32, (seq, 128), 1)
    block = 256

    def heads(g, carry):
        for u in range(2):
            h = g * 2 + u
            hs = head_block(h)
            logs = []
            for start in range(0, seq, block):
                end = start + block
                masked = masked_scores(q_ref[start:end, hs], k_ref[:end, hs], start, length, scale)
                peak = jnp.max(masked, axis=1, keepdims=True)
                weight = jnp.exp(masked - peak)
                total = jnp.sum(weight, axis=1, keepdims=True)
                probs = (weight / total).astype(BF)
                ctx_ref[start:end, hs] = dot_nn(probs, v_ref[:end, hs]).astype(BF)
                logs.append(peak + jnp.log(total))
            log = jnp.concatenate(logs, axis=0)
            lse_ref[...] = jnp.where(lane == h, log, lse_ref[...])
        return carry

    lse_ref[...] = jnp.zeros_like(lse_ref)
    lax.fori_loop(0, width // 256, heads, 0)
    copies[3].wait()
    squares = jnp.zeros((seq, 1), F32)
    for c0, cn in chunks(width, 256):
        cs = slice(c0, c0 + cn)
        hidden = tok_ref[:, cs].astype(F32) + dot_nn(ctx_ref[...], w_v[3, :, cs])
        hidden_ref[:, cs] = hidden
        squares = squares + jnp.sum(hidden * hidden, axis=1, keepdims=True)
    inverse = lax.rsqrt(squares / width + eps_norm)
    second_ref[...] = (hidden_ref[...] * inverse * gain_ref[1:2, :]).astype(BF)


def kernel_specs(places):
    kinds = {"v": pltpu.VMEM, "s": pltpu.SMEM, "a": pl.ANY}
    return [pl.BlockSpec(memory_space=kinds[p]) for p in places]


def attention_call(tokens, gains, cosine, sine, lengths, weights, scale):
    seq, width = tokens.shape
    half = jax.ShapeDtypeStruct((seq, width), BF)
    return pl.pallas_call(
        functools.partial(attention_kernel, scale),
        out_shape=[half] * 5
        + [jax.ShapeDtypeStruct((seq, 128), F32), jax.ShapeDtypeStruct((seq, width), F32), half],
        in_specs=kernel_specs("vvvvsaaaa"),
        out_specs=kernel_specs("vvvvvvvv"),
        scratch_shapes=[pltpu.VMEM((4, width, width), BF), pltpu.SemaphoreType.DMA((4,))],
        compiler_params=pltpu.CompilerParams(vmem_limit_bytes=VMEM_LIMIT),
        cost_estimate=estimate(0),
        name="attention_forward",
    )(tokens, gains, cosine, sine, lengths, *weights)


def store_pieces(even_ref, odd_ref, slot, rows_ref, grad_ref):
    count, _, piece, _ = even_ref.shape
    for part, out_ref in enumerate((even_ref, odd_ref)):
        for j in range(count):
            at = (part * count + j) * piece
            out_ref[j, slot] = dot_nn(rows_ref[at : at + piece, :], grad_ref[...]).astype(BF)


def piece_shape(number, width, out_width):
    count = lax.axis_size("expert") // 2
    return jax.ShapeDtypeStruct((count, number, width // (2 * count), out_width), BF)


def hidden_back_kernel(
    dn_ref, base_ref, side_x_ref, side_y_ref, hidden_ref, dout_ref, gain_ref, ctx_ref, wo, dhid_ref, dctx_ref, even_ref, odd_ref, gain_out, w_v, dattn_v, sem
):
    copy = pltpu.make_async_copy(wo, w_v, sem)
    copy.start()
    seq, width = hidden_ref.shape
    hidden = hidden_ref[...]
    inverse = lax.rsqrt(jnp.mean(hidden * hidden, axis=1, keepdims=True) + eps_norm)
    hat = hidden * inverse
    dn = dn_ref[...] + base_ref[...] + side_x_ref[...].astype(F32) + side_y_ref[...].astype(F32)
    gain_out[...] = jnp.sum(dn * hat, axis=0, keepdims=True)
    scaled = dn * gain_ref[1:2, :]
    mean = jnp.mean(scaled * hat, axis=1, keepdims=True)
    dhid = dout_ref[...].astype(F32) + inverse * (scaled - hat * mean)
    dhid_ref[...] = dhid
    dattn_v[...] = dhid.astype(BF)
    store_pieces(even_ref, odd_ref, 0, ctx_ref, dattn_v)
    copy.wait()
    for c0, cn in chunks(width, 256):
        dctx_ref[:, c0 : c0 + cn] = dot_nt(dattn_v[...], w_v[c0 : c0 + cn, :]).astype(BF)


def hidden_back_call(dn, base, sides, hidden, dout, gains, ctx_rel, wo):
    seq, width = hidden.shape
    half = jax.ShapeDtypeStruct((seq, width), BF)
    part = piece_shape(1, width, width)
    return pl.pallas_call(
        hidden_back_kernel,
        out_shape=[jax.ShapeDtypeStruct((seq, width), F32), half, part, part, jax.ShapeDtypeStruct((1, width), F32)],
        in_specs=kernel_specs("vvvvvvvva"),
        out_specs=kernel_specs("vvvvv"),
        scratch_shapes=[pltpu.VMEM((width, width), BF), pltpu.VMEM((seq, width), BF), pltpu.SemaphoreType.DMA],
        compiler_params=pltpu.CompilerParams(vmem_limit_bytes=VMEM_LIMIT),
        cost_estimate=estimate(0),
        name="hidden_backward",
    )(dn, base, *sides, hidden, dout, gains, ctx_rel, wo)


def heads_back_kernel(
    scale, q_ref, k_ref, v_ref, dctx_ref, lse_ref, cos_ref, sin_ref, first_ref, len_ref,
    dq_ref, dk_ref, dv_ref, even_ref, odd_ref,
):
    seq, width = q_ref.shape
    length = len_ref[0]
    lane = lax.broadcasted_iota(jnp.int32, (seq, 128), 1)
    block = 256

    def heads(g, carry):
        for u in range(2):
            h = g * 2 + u
            hs = head_block(h)
            log = jnp.sum(jnp.where(lane == h, lse_ref[...], 0.0), axis=1, keepdims=True)
            key_parts, value_parts = [], []
            for start in range(0, seq, block):
                end = start + block
                rows = slice(start, end)
                masked = masked_scores(q_ref[rows, hs], k_ref[:end, hs], start, length, scale)
                probs = jnp.exp(masked - log[rows])
                dprobs = dot_nt(dctx_ref[rows, hs], v_ref[:end, hs])
                delta = jnp.sum(probs * dprobs, axis=1, keepdims=True)
                dscores = (probs * (dprobs - delta)).astype(BF)
                dq = dot_nn(dscores, k_ref[:end, hs]) * scale
                dq_ref[rows, hs] = rotated(dq, cos_ref[rows, :], -sin_ref[rows, :]).astype(BF)
                key_parts.append(dot_tn(dscores, q_ref[rows, hs]))
                value_parts.append(dot_tn(probs.astype(BF), dctx_ref[rows, hs]))
            for start in range(0, seq, block):
                rows = slice(start, start + block)
                dk = sum(p[rows] for p in key_parts if p.shape[0] > start) * scale
                dv = sum(p[rows] for p in value_parts if p.shape[0] > start)
                dk_ref[rows, hs] = rotated(dk, cos_ref[rows, :], -sin_ref[rows, :]).astype(BF)
                dv_ref[rows, hs] = dv.astype(BF)
        return carry

    lax.fori_loop(0, width // 256, heads, 0)
    for j, grad_ref in ((2, dv_ref), (1, dk_ref), (0, dq_ref)):
        store_pieces(even_ref, odd_ref, j, first_ref, grad_ref)


def heads_back_call(q, k, v, dctx, lse, cosine, sine, first_rel, lengths, scale):
    seq, width = q.shape
    half = jax.ShapeDtypeStruct((seq, width), BF)
    part = piece_shape(3, width, width)
    return pl.pallas_call(
        functools.partial(heads_back_kernel, scale),
        out_shape=[half] * 3 + [part] * 2,
        in_specs=kernel_specs("vvvvvvvvs"),
        out_specs=kernel_specs("v" * 5),
        compiler_params=pltpu.CompilerParams(vmem_limit_bytes=VMEM_LIMIT),
        cost_estimate=estimate(0),
        name="heads_backward",
    )(q, k, v, dctx, lse, cosine, sine, first_rel, lengths)


def input_back_kernel(
    dq_ref, dk_ref, dv_ref, tok_ref, gain_ref, dhid_ref, len_ref, wq, wk, wv, out_ref, gain_out, sum_ref, w_v, dn_v, sem
):
    copies = [pltpu.make_async_copy(w, w_v.at[j], sem.at[j]) for j, w in enumerate((wq, wk, wv))]
    for copy in copies:
        copy.start()
    seq, width = tok_ref.shape
    x = tok_ref[...].astype(F32)
    inverse = lax.rsqrt(jnp.mean(x * x, axis=1, keepdims=True) + eps_norm)
    for copy in copies:
        copy.wait()
    for c0, cn in chunks(width, 256):
        cs = slice(c0, c0 + cn)
        dn_v[:, cs] = (
            dot_nt(dq_ref[...], w_v[0, cs, :]) + dot_nt(dk_ref[...], w_v[1, cs, :]) + dot_nt(dv_ref[...], w_v[2, cs, :])
        )
    hat = tok_ref[...].astype(F32) * inverse
    dn = dn_v[...]
    gain_out[...] = jnp.sum(dn * hat, axis=0, keepdims=True)
    scaled = dn * gain_ref[0:1, :]
    mean = jnp.mean(scaled * hat, axis=1, keepdims=True)
    result = dhid_ref[...] + inverse * (scaled - hat * mean)
    out_ref[...] = result
    valid = lax.broadcasted_iota(jnp.int32, result.shape, 0) < len_ref[0]
    sum_ref[0] = jnp.sum(jnp.where(valid, result * result, 0.0))


def input_back_call(dq, dk, dv, tokens, gains, dhidden, lengths, weights):
    seq, width = tokens.shape
    return pl.pallas_call(
        input_back_kernel,
        out_shape=[
            jax.ShapeDtypeStruct((seq, width), F32),
            jax.ShapeDtypeStruct((1, width), F32),
            jax.ShapeDtypeStruct((1,), F32),
        ],
        in_specs=kernel_specs("vvvvvvsaaa"),
        out_specs=kernel_specs("vvs"),
        scratch_shapes=[pltpu.VMEM((3, width, width), BF), pltpu.VMEM((seq, width), F32), pltpu.SemaphoreType.DMA((3,))],
        compiler_params=pltpu.CompilerParams(vmem_limit_bytes=VMEM_LIMIT),
        cost_estimate=estimate(0),
        name="input_backward",
    )(dq, dk, dv, tokens, gains, dhidden, lengths, *weights)


def shared_kernel(
    second_ref, second_rel_ref, dout_ref, dout_rel_ref, wg, wu, wd, out_ref, dn_ref, even_ref, odd_ref, w_v, h_v, da_v, db_v, sem
):
    copies = [pltpu.make_async_copy(w, w_v.at[j], sem.at[j]) for j, w in enumerate((wg, wu, wd))]
    for copy in copies:
        copy.start()
    for copy in copies:
        copy.wait()
    width, ff = w_v.shape[1:]
    for c0, cn in chunks(ff, 256):
        cs = slice(c0, c0 + cn)
        gate = dot_nn(second_ref[...], w_v[0, :, cs])
        up = dot_nn(second_ref[...], w_v[1, :, cs])
        back = dot_nn(dout_ref[...], w_v[2, :, cs])
        sigmoid = 1.0 / (1.0 + jnp.exp(-gate))
        silu = gate * sigmoid
        h_v[:, cs] = (silu * up).astype(BF)
        da_v[:, cs] = (back * up * (sigmoid * (1.0 + gate * (1.0 - sigmoid)))).astype(BF)
        db_v[:, cs] = (back * silu).astype(BF)
    for c0, cn in chunks(width, 256):
        cs = slice(c0, c0 + cn)
        out_ref[:, cs] = dot_nt(h_v[...], w_v[2, cs, :])
        dn_ref[:, cs] = dot_nt(da_v[...], w_v[0, cs, :]) + dot_nt(db_v[...], w_v[1, cs, :])
    store_pieces(even_ref, odd_ref, 0, second_rel_ref, da_v)
    store_pieces(even_ref, odd_ref, 1, second_rel_ref, db_v)
    store_pieces(even_ref, odd_ref, 2, dout_rel_ref, h_v)


def shared_call(second, second_rel, dout, dout_rel, weights):
    seq, width = second.shape
    ff = weights[0].shape[1]
    full = jax.ShapeDtypeStruct((seq, width), F32)
    part = piece_shape(3, width, ff)
    return pl.pallas_call(
        shared_kernel,
        out_shape=[full, full, part, part],
        in_specs=kernel_specs("vvvvaaa"),
        out_specs=kernel_specs("vvvv"),
        scratch_shapes=[pltpu.VMEM((3, width, ff), BF)]
        + [pltpu.VMEM((seq, ff), BF)] * 3
        + [pltpu.SemaphoreType.DMA((3,))],
        compiler_params=pltpu.CompilerParams(vmem_limit_bytes=VMEM_LIMIT),
        cost_estimate=estimate(0),
        name="shared_expert",
    )(second, second_rel, dout, dout_rel, *weights)


def update_kernel(rate, grad_ref, w_ref, m_ref, a_ref, *refs):
    grad_out, new_out, moment_out, average_out, copy_out = refs[-5:]
    parts = update(w_ref[0, 0], m_ref[0, 0], a_ref[0, 0], grad_ref[0].astype(F32), rate)
    for target, part in zip((grad_out, new_out, moment_out, average_out, copy_out), parts):
        target[0, 0] = part


def update_call(e, grad, weight, moment, average, done, rate):
    experts, kinds, rows, ff = weight.shape
    cuts = 2 if rows % 32 == 0 else 1
    full = pl.BlockSpec((1, 1, rows // cuts, ff), lambda j, i: (e, j, i, 0))
    return pl.pallas_call(
        functools.partial(update_kernel, rate),
        grid=(kinds, cuts),
        out_shape=[jax.ShapeDtypeStruct(weight.shape, F32)] * 4 + [jax.ShapeDtypeStruct(weight.shape, BF)],
        in_specs=[pl.BlockSpec((1, rows // cuts, ff), lambda j, i: (j, i, 0))]
        + [full] * 3
        + [pl.BlockSpec(memory_space=pl.ANY)] * len(done),
        out_specs=[full] * 5,
        input_output_aliases={4 + i: i for i in range(len(done))},
        compiler_params=pltpu.CompilerParams(vmem_limit_bytes=VMEM_LIMIT),
        cost_estimate=estimate(0),
        name="routed_update",
    )(grad, weight, moment, average, *done)


def permute(values, pairs):
    return lax.ppermute(values, "expert", pairs)


def pairs_of(mask, count):
    return [(i, i ^ mask) for i in range(count)]


def mixed_pairs(even_mask, odd_mask, count):
    return [(i, i ^ (odd_mask if i % 2 else even_mask)) for i in range(count)]


def after(values, *others):
    return lax.optimization_barrier((values, others))[0] if others else values


class Order:
    def __init__(self):
        self.last = ()

    def now(self, values):
        return after(values, *self.last)

    def close(self, *values):
        self.last = values


def send_dp(values, k):
    return lax.ppermute(values, "dp", [(i, i ^ k) for i in range(lax.axis_size("dp"))])


def stack_dp(pieces):
    whole = jnp.zeros((len(pieces),) + pieces[0].shape, pieces[0].dtype)
    for k, piece in enumerate(pieces):
        whole = lax.dynamic_update_slice(whole, piece[None], (lax.axis_index("dp") ^ k,) + (0,) * piece.ndim)
    return whole


def sum_dp(terms, axis, order):
    here = lax.axis_index("dp")
    found = []
    for k in range(lax.axis_size("dp")):
        term = lax.dynamic_index_in_dim(terms, here ^ k, axis=axis, keepdims=False)
        found.append((send_dp(order.now(term), k) if k else term).astype(F32))
    return tree_sum(found)


def tree_sum(terms):
    while len(terms) > 1:
        terms = [a + b for a, b in zip(terms[::2], terms[1::2])]
    return terms[0]


def permute_near(values):
    count = lax.axis_size("expert")
    return permute(values, pairs_of(2, count)), permute(values, pairs_of(4, count))


def permute_far(values):
    return permute(values, mixed_pairs(4, 2, lax.axis_size("expert")))


def permute_core(values):
    return permute(values, pairs_of(1, lax.axis_size("expert")))


def row_major(values):
    return with_layout_constraint(values, Layout(tuple(range(values.ndim))))


class PlaneSum:
    def __init__(self, even, odd, is_core0):
        self.even, self.odd, self.is_core0, self.kind = even, odd, is_core0, getattr(even, "dtype", BF)
        self.other = [None] * len(even)

    def take(self, j):
        return self.even[j].astype(F32) + self.other[j].astype(F32)

    def core(self, order):
        self.other = row_major(permute_core(row_major(order.now(self.odd))))
        return self.other

    def core_of(self, j, order):
        self.other[j] = permute_core(order.now(self.odd[j]))
        return self.other[j]

    def far(self, order):
        self.third = permute_far(order.now(self.take(3).astype(self.kind)))
        return self.third

    def near(self, order):
        count = lax.axis_size("expert")
        if not isinstance(self.other, list):
            self.other = order.now(self.other)
        third = self.third.astype(F32)
        to_x = (self.take(1) + jnp.where(self.is_core0, third, 0.0)).astype(self.kind)
        to_y = (self.take(2) + jnp.where(self.is_core0, 0.0, third)).astype(self.kind)
        to_x, to_y = order.now((to_x, to_y))
        self.sides = (permute(to_x, pairs_of(2, count)), permute(to_y, pairs_of(4, count)))
        return self.sides

    def total(self):
        return self.take(0) + self.sides[0].astype(F32) + self.sides[1].astype(F32)


def place_rows(pieces, me):
    parts, rows, width = pieces[0].shape
    whole = jnp.zeros((parts, len(pieces), rows, width), pieces[0].dtype)
    for r, piece in enumerate(pieces):
        whole = lax.dynamic_update_slice(whole, piece[:, None], (0, me ^ r, 0, 0))
    return whole.reshape(parts * len(pieces) * rows, width)


def piece_sum(even, odd, is_core0):
    parts = lax.axis_size("dp")
    cut = even.shape[:2] + (parts, even.shape[2] // parts, even.shape[3])
    return PlaneSum(even.reshape(cut), odd.reshape(cut), is_core0)


def relative_rows(me, width):
    parts, count = lax.axis_size("dp"), lax.axis_size("expert")
    rows = width // (parts * count)
    far = jnp.concatenate([jnp.arange(0, count, 2, dtype=jnp.int32), jnp.arange(1, count, 2, dtype=jnp.int32)])
    owner = jnp.arange(parts, dtype=jnp.int32)[None, :] * count + (me ^ far)[:, None]
    return (owner[:, :, None] * rows + jnp.arange(rows, dtype=jnp.int32)).reshape(width)


def local(
    tokens,
    cotangent,
    lengths,
    choices,
    attn_weight,
    attn_moment,
    attn_average,
    router_weight,
    router_moment,
    router_average,
    shared_weight,
    shared_moment,
    shared_average,
    routed_weight,
    routed_moment,
    routed_average,
    norm_gains,
    gain_moment,
    gain_average,
):
    seq_len, model_width = tokens.shape
    topk_count = choices.shape[1]
    head_dim = model_width // HEADS
    groups = lax.axis_size("expert")
    routed_count = routed_weight.shape[0] * groups
    capacity = (seq_len * topk_count * 8 // (7 * routed_count) + 7) // 8 * 8
    total_tokens = seq_len * groups * lax.axis_size("dp")
    step_root = 1.0 / math.sqrt(total_tokens)
    score_scale = 1.0 / math.sqrt(head_dim)
    me = lax.axis_index("expert")
    is_core0 = lax.rem(me, 2) == 0
    relative = me ^ jnp.arange(groups, dtype=jnp.int32)
    per_device = routed_weight.shape[0]
    positions = jnp.arange(seq_len, dtype=jnp.int32)
    length_here = lengths[0]
    valid_rows = (positions < length_here).astype(F32)[:, None]
    grad_out = cotangent.astype(F32) * valid_rows
    grad_out16 = grad_out.astype(BF)

    order = Order()
    select = lambda pair: jnp.where(is_core0, *pair)
    small = jnp.concatenate([router_weight, norm_gains.T], axis=1)
    small = jnp.pad(small[None], ((0, 1), (0, 0), (0, 128 - small.shape[1])))
    parts = lax.axis_size("dp")
    front_own = jnp.concatenate([attn_weight[:2], small], axis=2).astype(BF)
    back_own = attn_weight[2:].astype(BF)
    front_parts = [front_own] + [send_dp(front_own, k) for k in range(1, parts)]
    grad_near = permute_near(grad_out16)
    back_parts = [back_own] + [send_dp(back_own, k) for k in range(1, parts)]
    order.close(front_parts, grad_near)
    slab = routed_weight.shape[2]
    routed_low = [routed_weight[e].astype(BF) for e in range(per_device)]
    routed_low[0] = jnp.concatenate([routed_low[0], shared_weight.astype(BF)], axis=1)
    routed16 = [lax.all_gather(low, "dp", axis=0, tiled=False) for low in order.now(routed_low)]
    front = stack_dp(front_parts)

    choice_own = jnp.pad(choices.T.astype(BF), ((0, 16 - topk_count), (0, 0)))
    front_near = permute_near(order.now(front))
    choice_near = permute_near(order.now(choice_own))
    order.close(front_near, choice_near)
    back = stack_dp(order.now(back_parts))

    back_near = permute_near(order.now(back))
    front_far = permute_far(order.now(select(front_near)))
    choice_far = permute_far(order.now(select(choice_near)))
    front_core = [permute_core(order.now(p)) for p in (front, *front_near)]
    choice_core = [permute_core(order.now(p)) for p in (choice_own, *choice_near)]
    order.close(back_near, front_far, choice_far, front_core, choice_core)

    back_far = permute_far(order.now(select(back_near)))
    back_core = [permute_core(order.now(p)) for p in (back, *back_near)]
    front_core.append(permute_core(order.now(front_far)))
    choice_core.append(permute_core(order.now(choice_far)))
    order.close(back_far, back_core, front_core, choice_core)
    back_core.append(permute_core(order.now(back_far)))
    grad_far = permute_far(order.now(select(grad_near)))
    grad_core = [permute_core(order.now(p)) for p in (grad_out16, *grad_near)]
    front = [p for pair in zip((front, *front_near, front_far), front_core) for p in pair]
    back = [p for pair in zip((back, *back_near, back_far), back_core) for p in pair]
    choice_all = [p for pair in zip((choice_own, *choice_near, choice_far), choice_core) for p in pair]
    attn16 = [place_rows([p[:, j, :, :model_width] for p in front], me) for j in range(2)]
    attn16 += [place_rows([p[:, j] for p in back], me) for j in range(2)]
    small_all = place_rows([p[:, 0, :, model_width:] for p in front], me).T
    router16t = small_all[:routed_count]
    gains16 = small_all[routed_count : routed_count + 2]
    choice_all = jnp.stack([p[:topk_count] for p in choice_all]).astype(jnp.int32)
    own_experts = me * per_device + jnp.arange(per_device, dtype=jnp.int32)
    hits = jnp.any(choice_all[:, None] == own_experts[None, :, None, None], axis=2)
    before = (positions[:, None] < positions[None, :]).astype(BF)
    ranks = jnp.einsum("set,tu->seu", hits.astype(BF), before, preferred_element_type=F32).astype(jnp.int32)
    slot_all = jnp.where(hits, ranks, -1)
    choice_all = jnp.transpose(choice_all, (0, 2, 1))
    gain_first = gains16[0].astype(F32)
    gain_second = gains16[1].astype(F32)
    half_dim = head_dim // 2
    frequency = 10000.0 ** (-jnp.arange(half_dim, dtype=F32) / half_dim)
    angles = positions.astype(F32)[:, None] * frequency[None, :]
    cosine = jnp.concatenate([jnp.cos(angles), jnp.cos(angles)], axis=1)
    sine = jnp.concatenate([-jnp.sin(angles), jnp.sin(angles)], axis=1)
    gains = jnp.stack([gain_first, gain_second])
    first16, query16, key16, value16, context16, log_totals, hidden_state, second16 = attention_call(
        tokens, gains, cosine, sine, lengths, attn16, score_scale
    )
    order.close(second16, grad_far, grad_core)

    router_pad = jnp.pad(router16t, ((0, 128 - routed_count), (0, 0)))
    second_near = permute_near(second16)
    second_core = [permute_core(second16)]
    grad_core.append(permute_core(order.now(grad_far)))
    grads_even = (grad_out16, *grad_near, grad_far)
    seconds_even = [second16, *second_near]

    def pair(e, j, prev, gates):
        return expert_pair_call(
            own_experts[e][None],
            choice_all[2 * j : 2 * j + 2],
            slot_all[2 * j : 2 * j + 2, e],
            router_pad,
            routed16[e],
            order.now((seconds_even[j], second_core[j])),
            (grads_even[j], grad_core[j]),
            prev,
            gates,
            capacity,
        )

    order.close(second_core, grad_core)
    results = [[None] * 4 for _ in range(per_device)]
    results[0][0] = pair(0, 0, None, None)
    sort_rows = (jnp.arange(model_width, dtype=jnp.int32)[None, :] == relative_rows(me, model_width)[:, None]).astype(BF)
    sort = lambda values: lax.dot_general(
        sort_rows, values, (((1,), (1,)), ((), ())), preferred_element_type=F32
    ).astype(BF)
    sorted_rows = [sort(after(v, results[0][0][1])) for v in (first16, second16, context16, grad_out16)]
    order.close(second_near, results[0][0][1], sorted_rows)
    first_rel, second_rel, context_rel, out_rel = order.now(sorted_rows)

    second_far = permute_far(order.now(select(second_near)))
    second_core += [permute_core(order.now(p)) for p in second_near]
    order.close(second_core)
    shared_cut = order.now(routed16[0][:, :, slab:])
    shared_near = permute_near(shared_cut)
    results[0][1] = pair(0, 1, None, None)
    order.close(second_far, results[0][1][1], shared_near)
    seconds_even.append(second_far)
    second_core.append(permute_core(order.now(second_far)))
    shared_far = permute_far(order.now(select(shared_near)))
    shared_core = [permute_core(order.now(p)) for p in (shared_cut, *shared_near)]
    results[0][2] = pair(0, 2, None, None)
    order.close(second_core[3], results[0][2][1], shared_far, shared_core)
    shared_core.append(permute_core(order.now(shared_far)))
    results[0][3] = pair(0, 3, None, None)
    order.close(results[0][3][1], shared_core)
    shared_all = [p for both in zip((shared_cut, *shared_near, shared_far), order.now(shared_core)) for p in both]
    shared16 = [place_rows([p[:, j] for p in shared_all], me) for j in range(3)]
    shared_out, shared_back, shared_even, shared_odd = shared_call(
        order.now(second16), second_rel, grad_out16, out_rel, shared16
    )
    order.close(shared_back)
    routed_grads = []

    def finish_expert(e):
        grads = weight_grad_call(order.now([result[2] for result in results[e]]), parts)
        routed_grads.append(lax.psum_scatter(grads, "dp", scatter_dimension=0, tiled=False))
        return grads

    order.close(finish_expert(0))

    shared_sum = piece_sum(shared_even, shared_odd, is_core0)
    shared_core = shared_sum.core(order)
    for e in range(1, per_device):
        back_sum = PlaneSum([None] * 4, [None] * 4, is_core0) if e == per_device - 1 else None
        out_sum = PlaneSum([None] * 4, [None] * 4, is_core0) if e == per_device - 1 else None

        def step(j):
            results[e][j] = pair(e, j, results[e - 1][j][0], results[e - 1][j][3])
            if back_sum is not None:
                for total, found in zip((out_sum, back_sum), results[e][j][0]):
                    total.even[j], total.odd[j] = found

        step(3)
        order.close(results[e][3][1], shared_core)
        waits = []
        if back_sum is not None:
            waits += [back_sum.core_of(3, order), out_sum.core_of(3, order), shared_sum.far(order)]
        step(1)
        order.close(results[e][1][1], waits)
        if back_sum is not None:
            waits = [back_sum.far(order), back_sum.core_of(1, order), out_sum.core_of(1, order)]
        step(2)
        order.close(results[e][2][1], waits)
        if back_sum is not None:
            order.close(back_sum.core_of(2, order))
            sides = back_sum.near(order)
            waits = [out_sum.core_of(2, order)]
        step(0)
        if back_sum is not None:
            waits += [sides]
        order.close(results[e][0][1], waits)
        if back_sum is not None:
            waits = [back_sum.core_of(0, order), out_sum.far(order), out_sum.core_of(0, order)]
        order.close(finish_expert(e), waits)
    gate_grads = [jnp.concatenate([result[1][:, 0] for result in results[e]]) for e in range(per_device)]
    gate_sent = jnp.take(jnp.stack(gate_grads, axis=1), relative, axis=0)
    gate_back = lax.all_to_all(gate_sent, "expert", split_axis=0, concat_axis=0, tiled=True)
    grad_gate = gate_back.reshape(routed_count, seq_len).T
    logits = lax.dot_general(second16, router16t, (((1,), (1,)), ((), ())), preferred_element_type=F32)
    table = jnp.any(choices[:, :, None] == jnp.arange(routed_count, dtype=jnp.int32)[None, None, :], axis=1)
    chosen = jnp.where(table, logits, masked_score)
    chosen_exp = jnp.where(table, jnp.exp(chosen - jnp.max(chosen, axis=1, keepdims=True)), 0.0)
    gate_weights = chosen_exp / jnp.sum(chosen_exp, axis=1, keepdims=True)
    grad_second = shared_back
    grad_logits = grad_gate - gate_weights * jnp.sum(grad_gate, axis=1, keepdims=True)
    router_float = router16t.astype(F32)
    grad_second = grad_second + jnp.dot(grad_logits, router_float, precision=lax.Precision.HIGHEST)
    router_grad_full = lax.dot_general(
        grad_logits, second16.astype(F32), (((0,), (0,)), ((), ())), precision=lax.Precision.HIGHEST
    )
    order.close(order.now(grad_second))

    out_near = out_sum.near(order)
    grad_hidden_state, grad_context16, out_even, out_odd, grad_gain_second = hidden_back_call(
        order.now(grad_second), back_sum.take(0), sides, hidden_state, grad_out16, gains, context_rel, attn16[3]
    )
    order.close(grad_context16)

    shared_near = shared_sum.near(order)
    proj_sum = piece_sum(out_even, out_odd, is_core0)
    proj_core = proj_sum.core(order)
    grad_query16, grad_key16, grad_value16, head_even, head_odd = heads_back_call(
        query16, key16, value16, order.now(grad_context16), log_totals, cosine, sine, first_rel, lengths, score_scale
    )
    order.close(proj_core, grad_query16, out_near)

    head_sum = piece_sum(head_even, head_odd, is_core0)
    order.close(head_sum.core(order), proj_sum.far(order), shared_near)

    head_far = head_sum.far(order)
    proj_near = proj_sum.near(order)
    input_grad, grad_gain_first, input_square = input_back_call(
        order.now(grad_query16), grad_key16, grad_value16, tokens, gains, grad_hidden_state, lengths, attn16[:3]
    )
    block_value = hidden_state + shared_out + out_sum.total()
    order.close(head_far, input_grad, block_value)

    scalars = jnp.stack(
        [
            jnp.sum(valid_rows * block_value * block_value),
            input_square[0],
            length_here.astype(F32),
        ]
    )
    small_grads = jnp.concatenate([router_grad_full, grad_gain_first, grad_gain_second])
    scalars = jnp.broadcast_to(scalars[:, None], (3, model_width))
    small_grads = jnp.concatenate([small_grads, scalars])
    small_grads = jnp.pad(small_grads, ((0, 128 - small_grads.shape[0]), (0, 0)))
    small_grads = jnp.take(small_grads.T.reshape(parts, groups, -1, 128), relative, axis=1)
    head_near = head_sum.near(order)
    early_parts = update_call(
        0, order.now(routed_grads[0]), routed_weight, routed_moment, routed_average, [], rate_routed * step_root
    )
    order.close(head_near, proj_near, early_parts[-1])

    small_total = tree_sum(
        [small_grads[:, 0]] + [permute(order.now(small_grads[:, r]), pairs_of(r, groups)) for r in range(1, groups)]
    )
    attn_total = jnp.concatenate([head_sum.total(), proj_sum.total()]).astype(BF)
    attn_grad = sum_dp(attn_total, 1, order)
    shared_grad = sum_dp(shared_sum.total().astype(BF), 1, order)
    order.close(small_total)
    small_grad = sum_dp(small_total, 0, order)
    router_grad = small_grad[:, :routed_count]
    gain_grad = small_grad[:, routed_count : routed_count + 2].T
    row_sums = small_grad[0, routed_count + 2 : routed_count + 5]
    denominator = model_width * row_sums[2]
    masked_rms = jnp.stack(
        [jnp.sqrt(row_sums[0] / denominator), jnp.sqrt(row_sums[1] / denominator)]
    )
    attn_parts = update(
        attn_weight, attn_moment, attn_average, attn_grad, rate_attention * step_root
    )
    router_parts = update(
        router_weight, router_moment, router_average, router_grad, rate_router * step_root
    )
    shared_parts = update(
        shared_weight, shared_moment, shared_average, shared_grad, rate_shared * step_root
    )
    routed_parts = early_parts
    for e in range(1, per_device):
        routed_parts = update_call(
            e, routed_grads[e], routed_weight, routed_moment, routed_average, routed_parts, rate_routed * step_root
        )
    gain_parts = update(norm_gains, gain_moment, gain_average, gain_grad, rate_gains * step_root)
    return (
        block_value.astype(BF),
        input_grad,
        masked_rms,
        attn_parts[0],
        attn_parts[1],
        attn_parts[2],
        attn_parts[3],
        attn_parts[4],
        router_parts[0],
        router_parts[1],
        router_parts[2],
        router_parts[3],
        router_parts[4],
        shared_parts[0],
        shared_parts[1],
        shared_parts[2],
        shared_parts[3],
        shared_parts[4],
        routed_parts[0],
        routed_parts[1],
        routed_parts[2],
        routed_parts[3],
        routed_parts[4],
        gain_parts[0],
        gain_parts[1],
        gain_parts[2],
        gain_parts[3],
    )


def solution(mesh):
    placed = (
        P(("dp", "expert"), None),
        P(("dp", "expert"), None),
        P(("dp", "expert")),
        P(("dp", "expert"), None),
        P(None, ("dp", "expert"), None),
        P(None, ("dp", "expert"), None),
        P(None, ("dp", "expert"), None),
        P(("dp", "expert"), None),
        P(("dp", "expert"), None),
        P(("dp", "expert"), None),
        P(None, ("dp", "expert"), None),
        P(None, ("dp", "expert"), None),
        P(None, ("dp", "expert"), None),
        P("expert", None, "dp", None),
        P("expert", None, "dp", None),
        P("expert", None, "dp", None),
        P(None, ("dp", "expert")),
        P(None, ("dp", "expert")),
        P(None, ("dp", "expert")),
    )
    return jax.shard_map(
        local,
        mesh=mesh,
        in_specs=placed,
        out_specs=(
            P(("dp", "expert"), None),
            P(("dp", "expert"), None),
            P(),
            P(None, ("dp", "expert"), None),
            P(None, ("dp", "expert"), None),
            P(None, ("dp", "expert"), None),
            P(None, ("dp", "expert"), None),
            P(None, ("dp", "expert"), None),
            P(("dp", "expert"), None),
            P(("dp", "expert"), None),
            P(("dp", "expert"), None),
            P(("dp", "expert"), None),
            P(("dp", "expert"), None),
            P(None, ("dp", "expert"), None),
            P(None, ("dp", "expert"), None),
            P(None, ("dp", "expert"), None),
            P(None, ("dp", "expert"), None),
            P(None, ("dp", "expert"), None),
            P("expert", None, "dp", None),
            P("expert", None, "dp", None),
            P("expert", None, "dp", None),
            P("expert", None, "dp", None),
            P("expert", None, "dp", None),
            P(None, ("dp", "expert")),
            P(None, ("dp", "expert")),
            P(None, ("dp", "expert")),
            P(None, ("dp", "expert")),
        ),
        check_vma=False,
    )
```

```python
import functools
import math

import jax
import jax.numpy as jnp
from jax import lax
from jax.experimental import pallas as pl
from jax.experimental.layout import Layout, with_layout_constraint
from jax.experimental.pallas import tpu as pltpu
from jax.sharding import PartitionSpec as P

HEADS = 10
STEP = 3
BF = jnp.bfloat16
F32 = jnp.float32
BOTH = ("dp", "expert")


eps_norm = 1e-06
momentum_rate = 0.9
decay_rate = 0.0001
rate_attention = 0.01
rate_router = 0.03
rate_shared = 0.01
rate_routed = 0.04
rate_gains = 0.2
masked_score = -1e30
VMEM_LIMIT = 58 * 1024 * 1024


def silu_slope(pre_value):
    sigmoid_part = jax.nn.sigmoid(pre_value)
    return sigmoid_part * (1.0 + pre_value * (1.0 - sigmoid_part))


def update(weight, moment, average, gradient, step_rate):
    decayed = gradient + decay_rate * weight
    moment_new = momentum_rate * moment + decayed
    weight_new = weight - step_rate * (decayed + momentum_rate * moment_new)
    average_new = average + (weight_new - average) / (STEP + 1.0)
    return (gradient, weight_new, moment_new, average_new, weight_new.astype(BF))


def estimate(flops):
    return pl.CostEstimate(flops=flops, bytes_accessed=1, transcendentals=0)


def dot_nn(a,b): return lax.dot_general(a,b,(((1,),(0,)),((),())),preferred_element_type=F32)
def dot_nt(a,b): return lax.dot_general(a,b,(((1,),(1,)),((),())),preferred_element_type=F32)
def dot_tn(a,b): return lax.dot_general(a,b,(((0,),(0,)),((),())),preferred_element_type=F32)

def chunks(n,c): return [(s,min(c,n-s)) for s in range(0,n,c)]

def pair_columns(ff):
    return [(c0, cn, 2 * c0, 2 * c0 + cn) for c0, cn in chunks(ff, 256)]


def expert_pair_kernel(first, *refs):
    it = iter(refs)
    take = lambda count: [next(it) for _ in range(count)]
    eid_ref, choice_ref, slot_ref, router_ref, w_hbm = take(5)
    gate_ref = None if first else next(it)
    sources = [take(2), take(2)]
    prev = [] if first else [take(2), take(2)]
    outs = [take(2), take(2)]
    dg_ref, rows_out, dy_out, h_out, dab_out = take(5)
    gate_out = next(it) if first else None
    gu_v, down_v, tok, rows_v, dy_v, h_v, dab_v, ob, wsem, dsem, tsem, psem, osem, ssem = it
    n_dp = w_hbm.shape[0]
    width, ff = down_v.shape
    slab = width // n_dp
    seq = slot_ref.shape[1]
    cap = rows_v.shape[0] // 2
    tcopies = [[pltpu.make_async_copy(sources[j][q], tok.at[q, j], tsem.at[q, j]) for j in range(2)] for q in range(2)]
    wcopies = []
    for d in range(n_dp):
        own = pl.ds(d * slab, slab)
        for c, (c0, cn, g0, u0) in enumerate(pair_columns(ff)):
            for j, to in ((0, g0), (1, u0)):
                src = w_hbm.at[d, j, pl.ds(0, slab), pl.ds(c0, cn)]
                wcopies.append(pltpu.make_async_copy(src, gu_v.at[own, pl.ds(to, cn)], wsem.at[d, c, j]))
    dcopies = [
        pltpu.make_async_copy(w_hbm.at[d, 2, pl.ds(0, slab)], down_v.at[pl.ds(d * slab, slab)], dsem.at[d]) for d in range(n_dp)
    ]
    for copies in tcopies:
        for copy in copies:
            copy.start()
    lane = lax.broadcasted_iota(jnp.int32, (seq, 128), 1)
    sub = lax.broadcasted_iota(jnp.int32, (cap, seq), 0)
    eid = eid_ref[0]
    gcols, onehots = [], []
    for q in range(2):
        tcopies[q][0].wait()
        if q == 0:
            for copy in wcopies + dcopies:
                copy.start()
        sec = tok[q, 0]
        if first:
            logits = dot_nt(sec, router_ref[...])
            table = choice_ref[q, :, 0:1] == lane
            for k in range(1, choice_ref.shape[2]):
                table = table | (choice_ref[q, :, k : k + 1] == lane)
            masked = jnp.where(table, logits, masked_score)
            weight = jnp.where(table, jnp.exp(masked - jnp.max(masked, axis=1, keepdims=True)), 0.0)
            gates = weight / jnp.sum(weight, axis=1, keepdims=True)
            gate_out[q] = gates
        else:
            gates = gate_ref[q]
        gcol = jnp.sum(jnp.where(lane == eid, gates, 0.0), axis=1, keepdims=True)
        onehot = (slot_ref[q : q + 1, :] == sub).astype(F32).astype(BF)
        rows_v[q * cap : (q + 1) * cap, :] = dot_nn(onehot, sec).astype(BF)
        tcopies[q][1].wait()
        gated = (gcol * tok[q, 1].astype(F32)).astype(BF)
        dy_v[q * cap : (q + 1) * cap, :] = dot_nn(onehot, gated).astype(BF)
        gcols.append(gcol)
        onehots.append(onehot)
    pcopies = [pltpu.make_async_copy(prev[j][q], ob.at[q, j], psem.at[q, j]) for q in range(2) for j in range(2) if not first]
    for copy in pcopies:
        copy.start()
    saves = [pltpu.make_async_copy(rows_v, rows_out, ssem.at[0]), pltpu.make_async_copy(dy_v, dy_out, ssem.at[1])]
    for copy in saves:
        copy.start()
    for copy in wcopies + dcopies:
        copy.wait()
    gain_sum = jnp.zeros((2 * cap, 128), F32)
    for c0, cn, g0, u0 in pair_columns(ff):
        both = dot_nn(rows_v[...], gu_v[:, g0 : g0 + 2 * cn])
        a, b = both[:, :cn], both[:, cn:]
        dh = dot_nn(dy_v[...], down_v[:, c0 : c0 + cn])
        sigmoid = 0.5 * jnp.tanh(0.5 * a) + 0.5
        silu = a * sigmoid
        dsilu = dh * silu
        gain = dsilu * b
        for p0, pn in chunks(cn, 128):
            gain_sum = gain_sum + gain[:, p0 : p0 + pn]
        h_v[:, c0 : c0 + cn] = (silu * b).astype(BF)
        dab_v[:, g0 : g0 + cn] = (dh * b * (sigmoid + silu * (1.0 - sigmoid))).astype(BF)
        dab_v[:, u0 : u0 + cn] = dsilu.astype(BF)
    late = [pltpu.make_async_copy(h_v, h_out, ssem.at[2]), pltpu.make_async_copy(dab_v, dab_out, ssem.at[3])]
    for copy in late:
        copy.start()
    for copy in pcopies:
        copy.wait()
    sends = []
    gain_slot = jnp.sum(gain_sum, axis=1, keepdims=True)
    for q in range(2):
        spread = onehots[q].astype(F32) * gain_slot[q * cap : (q + 1) * cap]
        dg_ref[q] = jnp.broadcast_to(jnp.sum(spread, axis=0, keepdims=True), (8, seq))
    for n, (n0, nn) in enumerate(chunks(width, 512)):
        ns = slice(n0, n0 + nn)
        y = dot_nt(h_v[...], down_v[ns, :]).astype(BF)
        dr = dot_nt(dab_v[...], gu_v[ns, :]).astype(BF)
        for q in range(2):
            yt = dot_tn(onehots[q], y[q * cap : (q + 1) * cap])
            dt = dot_tn(onehots[q], dr[q * cap : (q + 1) * cap])
            yt = yt * gcols[q]
            if not first:
                yt = yt + ob[q, 0, :, ns].astype(F32)
                dt = dt + ob[q, 1, :, ns].astype(F32)
            ob[q, 0, :, ns] = yt.astype(BF)
            ob[q, 1, :, ns] = dt.astype(BF)
            for j in range(2):
                part = pl.ds(n0, nn)
                copy = pltpu.make_async_copy(ob.at[q, j, :, part], outs[j][q].at[:, part], osem.at[q, j, n])
                copy.start()
                sends.append(copy)
    for copy in saves + late + sends:
        copy.wait()


def expert_pair_call(eid, choice, slots, router_pad, w, secs, douts, prev, gates, cap):
    seq = slots.shape[1]
    width = secs[0].shape[1]
    n_dp, _, _, ff = w.shape
    parts = len(chunks(width, 512))
    flat = [] if prev is None else [v for pair in prev for v in pair]
    full = jax.ShapeDtypeStruct((seq, width), BF)
    shapes = [(2 * cap, width), (2 * cap, width), (2 * cap, ff), (2 * cap, 2 * ff)]
    dma = pltpu.SemaphoreType.DMA
    out = pl.pallas_call(
        functools.partial(expert_pair_kernel, prev is None),
        out_shape=[full] * 4
        + [jax.ShapeDtypeStruct((2, 8, seq), F32)]
        + [jax.ShapeDtypeStruct(shape, BF) for shape in shapes]
        + [jax.ShapeDtypeStruct((2, seq, 128), F32)] * (prev is None),
        in_specs=kernel_specs("svvva" + "v" * (prev is not None) + "a" * (4 + len(flat))),
        out_specs=kernel_specs("aaaavaaaa" + "v" * (prev is None)),
        scratch_shapes=[pltpu.VMEM((width, 2 * ff), BF), pltpu.VMEM((width, ff), BF), pltpu.VMEM((2, 2, seq, width), BF)]
        + [pltpu.VMEM(shape, BF) for shape in shapes]
        + [pltpu.VMEM((2, 2, seq, width), BF)]
        + [dma((n_dp, len(chunks(ff, 256)), 2)), dma((n_dp,)), dma((2, 2)), dma((2, 2)), dma((2, 2, parts)), dma((4,))],
        compiler_params=pltpu.CompilerParams(vmem_limit_bytes=VMEM_LIMIT),
        cost_estimate=estimate(18 * cap * width * ff),
        name="expert_pair",
    )(eid, choice, slots, router_pad, w, *([] if prev is None else [gates]), *secs, *douts, *flat)
    return (out[0:2], out[2:4]), out[4], out[5:9], out[9] if prev is None else gates


def weight_grad_kernel(count, *refs):
    saved = [refs[4 * i : 4 * i + 4] for i in range(count)]
    out_ref, rows_v, dy_v, h_v, dab_v, g_v, isem, osem = refs[4 * count :]
    width, ff = g_v.shape[1:]
    n_dp = out_ref.shape[0]
    slab = width // n_dp
    piece = rows_v.shape[0] // count
    loads = {}
    for j, to in ((1, dy_v), (2, h_v), (0, rows_v), (3, dab_v)):
        loads[j] = [
            pltpu.make_async_copy(saved[i][j], to.at[pl.ds(i * piece, piece)], isem.at[j, i]) for i in range(count)
        ]
        for copy in loads[j]:
            copy.start()
    stores = [
        [pltpu.make_async_copy(g_v.at[j, pl.ds(d * slab, slab)], out_ref.at[d, j], osem.at[j, d]) for d in range(n_dp)]
        for j in range(3)
    ]
    for copy in loads[1] + loads[2]:
        copy.wait()

    def down(i, carry):
        m = pl.ds(pl.multiple_of(i * 256, 256), 256)
        g_v[2, m, :] = dot_tn(dy_v[:, m], h_v[...]).astype(BF)
        return carry

    lax.fori_loop(0, width // 256, down, 0)
    for copy in stores[2]:
        copy.start()
    for copy in loads[0] + loads[3]:
        copy.wait()

    def front(i, carry):
        m = pl.ds(pl.multiple_of(i * 256, 256), 256)
        both = dot_tn(rows_v[:, m], dab_v[...])
        for c0, cn, g0, u0 in pair_columns(ff):
            g_v[0, m, c0 : c0 + cn] = both[:, g0 : g0 + cn].astype(BF)
            g_v[1, m, c0 : c0 + cn] = both[:, u0 : u0 + cn].astype(BF)
        return carry

    lax.fori_loop(0, width // 256, front, 0)
    for copy in stores[0] + stores[1]:
        copy.start()
    for copy in stores[0] + stores[1] + stores[2]:
        copy.wait()


def weight_grad_call(saved, n_dp):
    count = len(saved)
    width, ff = saved[0][0].shape[1], saved[0][2].shape[1]
    rows = count * saved[0][0].shape[0]
    dma = pltpu.SemaphoreType.DMA
    return pl.pallas_call(
        functools.partial(weight_grad_kernel, count),
        out_shape=jax.ShapeDtypeStruct((n_dp, 3, width // n_dp, ff), BF),
        in_specs=kernel_specs("a" * (4 * count)),
        out_specs=pl.BlockSpec(memory_space=pl.ANY),
        scratch_shapes=[pltpu.VMEM((rows, n), BF) for n in (width, width, ff, 2 * ff)]
        + [pltpu.VMEM((3, width, ff), BF), dma((4, count)), dma((3, n_dp))],
        compiler_params=pltpu.CompilerParams(vmem_limit_bytes=VMEM_LIMIT),
        cost_estimate=estimate(6 * rows * width * ff),
        name="expert_weights",
    )(*[v for part in saved for v in part])


def rotated(values, cosine, sine):
    return values * cosine + pltpu.roll(values, values.shape[1] // 2, 1) * sine


def head_block(h):
    return pl.ds(pl.multiple_of(h * 128, 128), 128)


def masked_scores(query, key, start, length, scale):
    scores = dot_nt(query, key) * scale
    at = lax.broadcasted_iota(jnp.int32, scores.shape, 0) + start
    to = lax.broadcasted_iota(jnp.int32, scores.shape, 1)
    return jnp.where((to <= at) & (to < length), scores, masked_score)


def attention_kernel(
    scale, tok_ref, gain_ref, cos_ref, sin_ref, len_ref, wq, wk, wv, wo,
    first_ref, q_ref, k_ref, v_ref, ctx_ref, lse_ref, hidden_ref, second_ref, w_v, sem,
):
    copies = [pltpu.make_async_copy(w, w_v.at[j], sem.at[j]) for j, w in enumerate((wq, wk, wv, wo))]
    for copy in copies:
        copy.start()
    seq, width = tok_ref.shape
    length = len_ref[0]
    x = tok_ref[...].astype(F32)
    inverse = lax.rsqrt(jnp.mean(x * x, axis=1, keepdims=True) + eps_norm)
    first_ref[...] = (x * inverse * gain_ref[0:1, :]).astype(BF)
    for j, out_ref in enumerate((q_ref, k_ref, v_ref)):
        copies[j].wait()
        for c0, cn in chunks(width, 256):
            lin = dot_nn(first_ref[...], w_v[j, :, c0 : c0 + cn])
            for h0, hn in chunks(cn, 128):
                part = lin[:, h0 : h0 + hn]
                if j < 2:
                    part = rotated(part, cos_ref[...], sin_ref[...])
                out_ref[:, c0 + h0 : c0 + h0 + hn] = part.astype(BF)
    lane = lax.broadcasted_iota(jnp.int32, (seq, 128), 1)
    block = 256

    def heads(g, carry):
        for u in range(2):
            h = g * 2 + u
            hs = head_block(h)
            logs = []
            for start in range(0, seq, block):
                end = start + block
                masked = masked_scores(q_ref[start:end, hs], k_ref[:end, hs], start, length, scale)
                peak = jnp.max(masked, axis=1, keepdims=True)
                weight = jnp.exp(masked - peak)
                total = jnp.sum(weight, axis=1, keepdims=True)
                probs = (weight / total).astype(BF)
                ctx_ref[start:end, hs] = dot_nn(probs, v_ref[:end, hs]).astype(BF)
                logs.append(peak + jnp.log(total))
            log = jnp.concatenate(logs, axis=0)
            lse_ref[...] = jnp.where(lane == h, log, lse_ref[...])
        return carry

    lse_ref[...] = jnp.zeros_like(lse_ref)
    lax.fori_loop(0, width // 256, heads, 0)
    copies[3].wait()
    squares = jnp.zeros((seq, 1), F32)
    for c0, cn in chunks(width, 256):
        cs = slice(c0, c0 + cn)
        hidden = tok_ref[:, cs].astype(F32) + dot_nn(ctx_ref[...], w_v[3, :, cs])
        hidden_ref[:, cs] = hidden
        squares = squares + jnp.sum(hidden * hidden, axis=1, keepdims=True)
    inverse = lax.rsqrt(squares / width + eps_norm)
    second_ref[...] = (hidden_ref[...] * inverse * gain_ref[1:2, :]).astype(BF)


def kernel_specs(places):
    kinds = {"v": pltpu.VMEM, "s": pltpu.SMEM, "a": pl.ANY}
    return [pl.BlockSpec(memory_space=kinds[p]) for p in places]


def attention_call(tokens, gains, cosine, sine, lengths, weights, scale):
    seq, width = tokens.shape
    half = jax.ShapeDtypeStruct((seq, width), BF)
    return pl.pallas_call(
        functools.partial(attention_kernel, scale),
        out_shape=[half] * 5
        + [jax.ShapeDtypeStruct((seq, 128), F32), jax.ShapeDtypeStruct((seq, width), F32), half],
        in_specs=kernel_specs("vvvvsaaaa"),
        out_specs=kernel_specs("vvvvvvvv"),
        scratch_shapes=[pltpu.VMEM((4, width, width), BF), pltpu.SemaphoreType.DMA((4,))],
        compiler_params=pltpu.CompilerParams(vmem_limit_bytes=VMEM_LIMIT),
        cost_estimate=estimate(0),
        name="attention_forward",
    )(tokens, gains, cosine, sine, lengths, *weights)


def store_pieces(even_ref, odd_ref, slot, rows_ref, grad_ref):
    count, _, piece, _ = even_ref.shape
    for part, out_ref in enumerate((even_ref, odd_ref)):
        for j in range(count):
            at = (part * count + j) * piece
            out_ref[j, slot] = dot_nn(rows_ref[at : at + piece, :], grad_ref[...]).astype(BF)


def piece_shape(number, width, out_width):
    count = lax.axis_size("expert") // 2
    return jax.ShapeDtypeStruct((count, number, width // (2 * count), out_width), BF)


def hidden_back_kernel(
    dn_ref, logit_ref, router_ref, base_ref, side_x_ref, side_y_ref, hidden_ref, dout_ref, gain_ref, ctx_ref, wo, dhid_ref, dctx_ref, even_ref, odd_ref, gain_out, w_v, dattn_v, sem
):
    copy = pltpu.make_async_copy(wo, w_v, sem)
    copy.start()
    seq, width = hidden_ref.shape
    hidden = hidden_ref[...]
    inverse = lax.rsqrt(jnp.mean(hidden * hidden, axis=1, keepdims=True) + eps_norm)
    hat = hidden * inverse
    logits = logit_ref[...]
    high = logits.astype(BF)
    rest = logits - high.astype(F32)
    low = rest.astype(BF)
    least = (rest - low.astype(F32)).astype(BF)
    routers = sum(dot_nn(part, router_ref[...]) for part in (least, low, high))
    dn = dn_ref[...] + routers + base_ref[...] + side_x_ref[...].astype(F32) + side_y_ref[...].astype(F32)
    gain_out[...] = jnp.sum(dn * hat, axis=0, keepdims=True)
    scaled = dn * gain_ref[1:2, :]
    mean = jnp.mean(scaled * hat, axis=1, keepdims=True)
    dhid = dout_ref[...].astype(F32) + inverse * (scaled - hat * mean)
    dhid_ref[...] = dhid
    dattn_v[...] = dhid.astype(BF)
    store_pieces(even_ref, odd_ref, 0, ctx_ref, dattn_v)
    copy.wait()
    for c0, cn in chunks(width, 256):
        dctx_ref[:, c0 : c0 + cn] = dot_nt(dattn_v[...], w_v[c0 : c0 + cn, :]).astype(BF)


def hidden_back_call(dn, logits, router, base, sides, hidden, dout, gains, ctx_rel, wo):
    seq, width = hidden.shape
    half = jax.ShapeDtypeStruct((seq, width), BF)
    part = piece_shape(1, width, width)
    return pl.pallas_call(
        hidden_back_kernel,
        out_shape=[jax.ShapeDtypeStruct((seq, width), F32), half, part, part, jax.ShapeDtypeStruct((1, width), F32)],
        in_specs=kernel_specs("vvvvvvvvvva"),
        out_specs=kernel_specs("vvvvv"),
        scratch_shapes=[pltpu.VMEM((width, width), BF), pltpu.VMEM((seq, width), BF), pltpu.SemaphoreType.DMA],
        compiler_params=pltpu.CompilerParams(vmem_limit_bytes=VMEM_LIMIT),
        cost_estimate=estimate(15 * seq * width * width),
        name="hidden_backward",
    )(dn, logits, router, base, *sides, hidden, dout, gains, ctx_rel, wo)


def heads_back_kernel(
    scale, q_ref, k_ref, v_ref, dctx_ref, lse_ref, cos_ref, sin_ref, first_ref, len_ref,
    dq_ref, dk_ref, dv_ref, even_ref, odd_ref,
):
    seq, width = q_ref.shape
    length = len_ref[0]
    lane = lax.broadcasted_iota(jnp.int32, (seq, 128), 1)
    block = 256

    def heads(g, carry):
        for u in range(2):
            h = g * 2 + u
            hs = head_block(h)
            log = jnp.sum(jnp.where(lane == h, lse_ref[...], 0.0), axis=1, keepdims=True)
            key_parts, value_parts = [], []
            for start in range(0, seq, block):
                end = start + block
                rows = slice(start, end)
                masked = masked_scores(q_ref[rows, hs], k_ref[:end, hs], start, length, scale)
                probs = jnp.exp(masked - log[rows])
                dprobs = dot_nt(dctx_ref[rows, hs], v_ref[:end, hs])
                delta = jnp.sum(probs * dprobs, axis=1, keepdims=True)
                dscores = (probs * (dprobs - delta)).astype(BF)
                dq = dot_nn(dscores, k_ref[:end, hs]) * scale
                dq_ref[rows, hs] = rotated(dq, cos_ref[rows, :], -sin_ref[rows, :]).astype(BF)
                key_parts.append(dot_tn(dscores, q_ref[rows, hs]))
                value_parts.append(dot_tn(probs.astype(BF), dctx_ref[rows, hs]))
            for start in range(0, seq, block):
                rows = slice(start, start + block)
                dk = sum(p[rows] for p in key_parts if p.shape[0] > start) * scale
                dv = sum(p[rows] for p in value_parts if p.shape[0] > start)
                dk_ref[rows, hs] = rotated(dk, cos_ref[rows, :], -sin_ref[rows, :]).astype(BF)
                dv_ref[rows, hs] = dv.astype(BF)
        return carry

    lax.fori_loop(0, width // 256, heads, 0)
    store_pieces(even_ref, odd_ref, 2, first_ref, dv_ref)
    store_pieces(even_ref, odd_ref, 0, first_ref, dq_ref)
    store_pieces(even_ref, odd_ref, 1, first_ref, dk_ref)


def heads_back_call(q, k, v, dctx, lse, cosine, sine, first_rel, lengths, scale):
    seq, width = q.shape
    half = jax.ShapeDtypeStruct((seq, width), BF)
    wide = piece_shape(3, width, width)
    return pl.pallas_call(
        functools.partial(heads_back_kernel, scale),
        out_shape=[half] * 3 + [wide] * 2,
        in_specs=kernel_specs("vvvvvvvvs"),
        out_specs=kernel_specs("v" * 5),
        compiler_params=pltpu.CompilerParams(vmem_limit_bytes=VMEM_LIMIT),
        cost_estimate=estimate(26 * seq * width * width),
        name="heads_backward",
    )(q, k, v, dctx, lse, cosine, sine, first_rel, lengths)


def input_back_kernel(
    dq_ref, dk_ref, dv_ref, tok_ref, gain_ref, dhid_ref, len_ref, wq, wk, wv, out_ref, gain_out, sum_ref, w_v, dn_v, sem
):
    copies = [pltpu.make_async_copy(w, w_v.at[j], sem.at[j]) for j, w in enumerate((wq, wk, wv))]
    for copy in copies:
        copy.start()
    seq, width = tok_ref.shape
    x = tok_ref[...].astype(F32)
    inverse = lax.rsqrt(jnp.mean(x * x, axis=1, keepdims=True) + eps_norm)
    for copy in copies:
        copy.wait()
    for c0, cn in chunks(width, 256):
        cs = slice(c0, c0 + cn)
        dn_v[:, cs] = (
            dot_nt(dq_ref[...], w_v[0, cs, :]) + dot_nt(dk_ref[...], w_v[1, cs, :]) + dot_nt(dv_ref[...], w_v[2, cs, :])
        )
    hat = tok_ref[...].astype(F32) * inverse
    dn = dn_v[...]
    gain_out[...] = jnp.sum(dn * hat, axis=0, keepdims=True)
    scaled = dn * gain_ref[0:1, :]
    mean = jnp.mean(scaled * hat, axis=1, keepdims=True)
    result = dhid_ref[...] + inverse * (scaled - hat * mean)
    out_ref[...] = result
    valid = lax.broadcasted_iota(jnp.int32, result.shape, 0) < len_ref[0]
    sum_ref[0] = jnp.sum(jnp.where(valid, result * result, 0.0))


def input_back_call(dq, dk, dv, tokens, gains, dhidden, lengths, weights):
    seq, width = tokens.shape
    return pl.pallas_call(
        input_back_kernel,
        out_shape=[
            jax.ShapeDtypeStruct((seq, width), F32),
            jax.ShapeDtypeStruct((1, width), F32),
            jax.ShapeDtypeStruct((1,), F32),
        ],
        in_specs=kernel_specs("vvvvvvsaaa"),
        out_specs=kernel_specs("vvs"),
        scratch_shapes=[pltpu.VMEM((3, width, width), BF), pltpu.VMEM((seq, width), F32), pltpu.SemaphoreType.DMA((3,))],
        compiler_params=pltpu.CompilerParams(vmem_limit_bytes=VMEM_LIMIT),
        cost_estimate=estimate(18 * seq * width * width),
        name="input_backward",
    )(dq, dk, dv, tokens, gains, dhidden, lengths, *weights)


def shared_kernel(
    second_ref, second_rel_ref, dout_ref, dout_rel_ref, wg, wu, wd, out_ref, dn_ref, even_ref, odd_ref, w_v, h_v, da_v, db_v, sem
):
    copies = [pltpu.make_async_copy(w, w_v.at[j], sem.at[j]) for j, w in enumerate((wg, wu, wd))]
    for copy in copies:
        copy.start()
    for copy in copies:
        copy.wait()
    width, ff = w_v.shape[1:]
    for c0, cn in chunks(ff, 256):
        cs = slice(c0, c0 + cn)
        gate = dot_nn(second_ref[...], w_v[0, :, cs])
        up = dot_nn(second_ref[...], w_v[1, :, cs])
        back = dot_nn(dout_ref[...], w_v[2, :, cs])
        sigmoid = 1.0 / (1.0 + jnp.exp(-gate))
        silu = gate * sigmoid
        h_v[:, cs] = (silu * up).astype(BF)
        da_v[:, cs] = (back * up * (sigmoid * (1.0 + gate * (1.0 - sigmoid)))).astype(BF)
        db_v[:, cs] = (back * silu).astype(BF)
    for c0, cn in chunks(width, 256):
        cs = slice(c0, c0 + cn)
        out_ref[:, cs] = dot_nt(h_v[...], w_v[2, cs, :])
        dn_ref[:, cs] = dot_nt(da_v[...], w_v[0, cs, :]) + dot_nt(db_v[...], w_v[1, cs, :])
    store_pieces(even_ref, odd_ref, 0, second_rel_ref, da_v)
    store_pieces(even_ref, odd_ref, 1, second_rel_ref, db_v)
    store_pieces(even_ref, odd_ref, 2, dout_rel_ref, h_v)


def shared_call(second, second_rel, dout, dout_rel, weights):
    seq, width = second.shape
    ff = weights[0].shape[1]
    full = jax.ShapeDtypeStruct((seq, width), F32)
    part = piece_shape(3, width, ff)
    return pl.pallas_call(
        shared_kernel,
        out_shape=[full, full, part, part],
        in_specs=kernel_specs("vvvvaaa"),
        out_specs=kernel_specs("vvvv"),
        scratch_shapes=[pltpu.VMEM((3, width, ff), BF)]
        + [pltpu.VMEM((seq, ff), BF)] * 3
        + [pltpu.SemaphoreType.DMA((3,))],
        compiler_params=pltpu.CompilerParams(vmem_limit_bytes=VMEM_LIMIT),
        cost_estimate=estimate(0),
        name="shared_expert",
    )(second, second_rel, dout, dout_rel, *weights)


def update_kernel(rate, grad_ref, w_ref, m_ref, a_ref, *refs):
    grad_out, new_out, moment_out, average_out, copy_out = refs[-5:]
    parts = update(w_ref[0, 0], m_ref[0, 0], a_ref[0, 0], grad_ref[0].astype(F32), rate)
    for target, part in zip((grad_out, new_out, moment_out, average_out, copy_out), parts):
        target[0, 0] = part


def update_call(e, grad, weight, moment, average, done, rate):
    experts, kinds, rows, ff = weight.shape
    cuts = 2 if rows % 32 == 0 else 1
    full = pl.BlockSpec((1, 1, rows // cuts, ff), lambda j, i: (e, j, i, 0))
    return pl.pallas_call(
        functools.partial(update_kernel, rate),
        grid=(kinds, cuts),
        out_shape=[jax.ShapeDtypeStruct(weight.shape, F32)] * 4 + [jax.ShapeDtypeStruct(weight.shape, BF)],
        in_specs=[pl.BlockSpec((1, rows // cuts, ff), lambda j, i: (j, i, 0))]
        + [full] * 3
        + [pl.BlockSpec(memory_space=pl.ANY)] * len(done),
        out_specs=[full] * 5,
        input_output_aliases={4 + i: i for i in range(len(done))},
        compiler_params=pltpu.CompilerParams(vmem_limit_bytes=VMEM_LIMIT),
        cost_estimate=estimate(10_000_000_000),
        name="routed_update",
    )(grad, weight, moment, average, *done)


def permute(values, pairs):
    return lax.ppermute(values, "expert", pairs)


def pairs_of(mask, count):
    return [(i, i ^ mask) for i in range(count)]


def mixed_pairs(even_mask, odd_mask, count):
    return [(i, i ^ (odd_mask if i % 2 else even_mask)) for i in range(count)]


def after(values, *others):
    return lax.optimization_barrier((values, others))[0] if others else values


class Order:
    def __init__(self):
        self.last = ()

    def now(self, values):
        return after(values, *self.last)

    def close(self, *values):
        self.last = values


def send_dp(values, k):
    return lax.ppermute(values, "dp", [(i, i ^ k) for i in range(lax.axis_size("dp"))])


def stack_kernel(at_ref, *refs):
    count = (len(refs) - 2)
    copies = [
        pltpu.make_async_copy(refs[k], refs[count].at[at_ref[0] ^ k], refs[-1].at[k]) for k in range(count)
    ]
    for copy in copies:
        copy.start()
    for copy in copies:
        copy.wait()


def stack_dp(pieces):
    count = len(pieces)
    return pl.pallas_call(
        stack_kernel,
        out_shape=jax.ShapeDtypeStruct((count,) + pieces[0].shape, BF),
        in_specs=kernel_specs("s" + "a" * count),
        out_specs=pl.BlockSpec(memory_space=pltpu.VMEM),
        scratch_shapes=[pltpu.SemaphoreType.DMA((count,))],
        compiler_params=pltpu.CompilerParams(vmem_limit_bytes=VMEM_LIMIT),
        cost_estimate=estimate(0),
        name="stack_dp",
    )(lax.axis_index("dp")[None], *pieces)


def send_terms(terms, axis, order):
    here = lax.axis_index("dp")
    found = []
    for k in range(lax.axis_size("dp")):
        term = lax.dynamic_index_in_dim(terms, here ^ k, axis=axis, keepdims=False)
        found.append(send_dp(order.now(term), k) if k else order.now(term))
    return found


def sum_terms(found):
    return tree_sum([term.astype(F32) for term in found])


def tree_sum(terms):
    while len(terms) > 1:
        terms = [a + b for a, b in zip(terms[::2], terms[1::2])]
    return terms[0]


def permute_near(values):
    count = lax.axis_size("expert")
    return permute(values, pairs_of(2, count)), permute(values, pairs_of(4, count))


def permute_far(values):
    return permute(values, mixed_pairs(4, 2, lax.axis_size("expert")))


def permute_core(values):
    return permute(values, pairs_of(1, lax.axis_size("expert")))


def row_major(values):
    return with_layout_constraint(values, Layout(tuple(range(values.ndim))))


class PlaneSum:
    def __init__(self, even, odd, is_core0):
        self.even, self.odd, self.is_core0, self.kind = even, odd, is_core0, getattr(even, "dtype", BF)
        self.other = [None] * len(even)

    def take(self, j):
        return self.even[j].astype(F32) + self.other[j].astype(F32)

    def core(self, order):
        self.other = row_major(permute_core(row_major(order.now(self.odd))))
        return self.other

    def core_of(self, j, order):
        self.other[j] = permute_core(order.now(self.odd[j]))
        return self.other[j]

    def far(self, order):
        self.third = permute_far(order.now(self.take(3).astype(self.kind)))
        return self.third

    def near(self, order):
        count = lax.axis_size("expert")
        if not isinstance(self.other, list):
            self.other = order.now(self.other)
        third = self.third.astype(F32)
        to_x = (self.take(1) + jnp.where(self.is_core0, third, 0.0)).astype(self.kind)
        to_y = (self.take(2) + jnp.where(self.is_core0, 0.0, third)).astype(self.kind)
        to_x, to_y = self.sent = order.now((to_x, to_y))
        self.sides = (permute(to_x, pairs_of(2, count)), permute(to_y, pairs_of(4, count)))
        return self.sides

    def total(self):
        return self.take(0) + self.sides[0].astype(F32) + self.sides[1].astype(F32)


def place_kernel(cuts, at_ref, *refs):
    sem = refs[-1]
    outs = refs[-1 - len(cuts) : -1]
    count = sem.shape[0]
    copies = []
    for i, (group, kind, column) in enumerate(cuts):
        for r in range(count):
            source = refs[group * count + r].at[:, kind, :, pl.ds(column, outs[i].shape[3])]
            copies.append(pltpu.make_async_copy(source, outs[i].at[:, at_ref[0] ^ r], sem.at[r, i]))
    for copy in copies:
        copy.start()
    for copy in copies:
        copy.wait()


def place_rows(groups, me, cuts):
    count = len(groups[0])
    parts, _, rows, _ = groups[0][0].shape
    shapes = [(parts, count, rows, cut[3]) for cut in cuts]
    out = pl.pallas_call(
        functools.partial(place_kernel, [cut[:3] for cut in cuts]),
        out_shape=[jax.ShapeDtypeStruct(shape, BF) for shape in shapes],
        in_specs=kernel_specs("s" + "a" * (count * len(groups))),
        out_specs=kernel_specs("v" * len(cuts)),
        scratch_shapes=[pltpu.SemaphoreType.DMA((count, len(cuts)))],
        compiler_params=pltpu.CompilerParams(vmem_limit_bytes=VMEM_LIMIT),
        cost_estimate=estimate(0),
        name="place_rows",
    )(me[None], *[piece for group in groups for piece in group])
    return [v.reshape(parts * count * rows, v.shape[3]) for v in out]


def piece_sum(even, odd, is_core0):
    parts = lax.axis_size("dp")
    cut = even.shape[:2] + (parts, even.shape[2] // parts, even.shape[3])
    return PlaneSum(even.reshape(cut), odd.reshape(cut), is_core0)


def relative_rows(me, width):
    parts, count = lax.axis_size("dp"), lax.axis_size("expert")
    rows = width // (parts * count)
    far = jnp.concatenate([jnp.arange(0, count, 2, dtype=jnp.int32), jnp.arange(1, count, 2, dtype=jnp.int32)])
    owner = jnp.arange(parts, dtype=jnp.int32)[None, :] * count + (me ^ far)[:, None]
    return (owner[:, :, None] * rows + jnp.arange(rows, dtype=jnp.int32)).reshape(width)


def local(
    tokens,
    cotangent,
    lengths,
    choices,
    attn_weight,
    attn_moment,
    attn_average,
    router_weight,
    router_moment,
    router_average,
    shared_weight,
    shared_moment,
    shared_average,
    routed_weight,
    routed_moment,
    routed_average,
    norm_gains,
    gain_moment,
    gain_average,
):
    seq_len, model_width = tokens.shape
    topk_count = choices.shape[1]
    head_dim = model_width // HEADS
    groups = lax.axis_size("expert")
    routed_count = routed_weight.shape[0] * groups
    capacity = (seq_len * topk_count * 8 // (7 * routed_count) + 7) // 8 * 8
    total_tokens = seq_len * groups * lax.axis_size("dp")
    step_root = 1.0 / math.sqrt(total_tokens)
    score_scale = 1.0 / math.sqrt(head_dim)
    me = lax.axis_index("expert")
    is_core0 = lax.rem(me, 2) == 0
    relative = me ^ jnp.arange(groups, dtype=jnp.int32)
    per_device = routed_weight.shape[0]
    positions = jnp.arange(seq_len, dtype=jnp.int32)
    length_here = lengths[0]
    valid_rows = (positions < length_here).astype(F32)[:, None]
    grad_out = cotangent.astype(F32) * valid_rows
    grad_out16 = grad_out.astype(BF)

    order = Order()
    select = lambda pair: jnp.where(is_core0, *pair)
    small = jnp.concatenate([router_weight, norm_gains.T], axis=1)
    small = jnp.pad(small[None], ((0, 1), (0, 0), (0, 128 - small.shape[1])))
    parts = lax.axis_size("dp")
    front_own = jnp.concatenate([attn_weight[:2], small], axis=2).astype(BF)
    back_own = attn_weight[2:].astype(BF)
    shared_own = shared_weight.astype(BF)
    front_parts = [front_own] + [send_dp(front_own, k) for k in range(1, parts)]
    grad_near = permute_near(grad_out16)
    order.close(front_parts, grad_near)
    back_parts = [back_own] + [send_dp(order.now(back_own), k) for k in range(1, parts)]
    front = stack_dp(front_parts)

    choice_own = jnp.pad(choices.T.astype(BF), ((0, 16 - topk_count), (0, 0)))
    choice_all = lax.all_to_all(
        jnp.broadcast_to(choice_own, (groups,) + choice_own.shape), "expert", split_axis=0, concat_axis=0, tiled=True
    )
    front_near = permute_near(order.now(front))
    order.close(front_near, back_parts)
    back = stack_dp(back_parts)
    shared_cut = lax.all_to_all(
        order.now(jnp.broadcast_to(shared_own, (parts,) + shared_own.shape)), "dp", split_axis=0, concat_axis=0, tiled=True
    )

    front_held = list(order.now((front, *front_near)))
    back_near = permute_near(order.now(back))
    front_far = permute_far(order.now(select(front_near)))
    front_core = [permute_core(order.now(p)) for p in (front, *front_near)]
    order.close(back_near, front_far, front_core, shared_cut)
    routed_low = [routed_weight[e].astype(BF) for e in range(per_device)]
    routed16 = [lax.all_gather(low, "dp", axis=0, tiled=False) for low in order.now(routed_low)]

    back_held = list(order.now((back, *back_near)))
    back_far = permute_far(order.now(select(back_near)))
    back_core = [permute_core(order.now(p)) for p in (back, *back_near)]
    front_core.append(permute_core(order.now(front_far)))
    order.close(back_far, back_core, front_core)
    back_core.append(permute_core(order.now(back_far)))
    shared_near = permute_near(order.now(shared_cut))
    grad_core = [permute_core(order.now(p)) for p in (grad_out16, *grad_near)]
    front = [p for pair in zip((*front_held, front_far), front_core) for p in pair]
    back = [p for pair in zip((*back_held, back_far), back_core) for p in pair]
    cuts = [(group, kind, 0, model_width) for group in range(2) for kind in range(2)]
    *attn16, small_all = place_rows([front, back], me, cuts + [(0, 0, model_width, 128)])
    small_all = small_all.T
    router16t = small_all[:routed_count]
    gains16 = small_all[routed_count : routed_count + 2]
    choice_all = jnp.take(choice_all[:, :topk_count], relative, axis=0).astype(jnp.int32)
    own_experts = me * per_device + jnp.arange(per_device, dtype=jnp.int32)
    hits = jnp.any(choice_all[:, None] == own_experts[None, :, None, None], axis=2)
    before = (positions[:, None] < positions[None, :]).astype(BF)
    ranks = jnp.einsum("set,tu->seu", hits.astype(BF), before, preferred_element_type=F32).astype(jnp.int32)
    slot_all = jnp.where(hits, ranks, -1)
    choice_all = jnp.transpose(choice_all, (0, 2, 1))
    gain_first = gains16[0].astype(F32)
    gain_second = gains16[1].astype(F32)
    half_dim = head_dim // 2
    frequency = 10000.0 ** (-jnp.arange(half_dim, dtype=F32) / half_dim)
    angles = positions.astype(F32)[:, None] * frequency[None, :]
    cosine = jnp.concatenate([jnp.cos(angles), jnp.cos(angles)], axis=1)
    sine = jnp.concatenate([-jnp.sin(angles), jnp.sin(angles)], axis=1)
    gains = jnp.stack([gain_first, gain_second])
    first16, query16, key16, value16, context16, log_totals, hidden_state, second16 = attention_call(
        tokens, gains, cosine, sine, lengths, attn16, score_scale
    )
    order.close(second16, shared_near, grad_core)

    router_pad = jnp.pad(router16t, ((0, 128 - routed_count), (0, 0)))
    shared_sent = order.now(select(shared_near))
    shared_far = permute_far(shared_sent)
    second_near = permute_near(after(second16, shared_sent))
    second_core = [permute_core(second16)]
    grads_even = [grad_out16, *grad_near]
    seconds_even = [second16, *second_near]

    def pair(e, j, prev, gates):
        return expert_pair_call(
            own_experts[e][None],
            choice_all[2 * j : 2 * j + 2],
            slot_all[2 * j : 2 * j + 2, e],
            router_pad,
            routed16[e],
            order.now((seconds_even[j], second_core[j])),
            (grads_even[j], grad_core[j]),
            prev,
            gates,
            capacity,
        )

    shared_core = [permute_core(order.now(p)) for p in (shared_cut, *shared_near)]
    sort_rows = (jnp.arange(model_width, dtype=jnp.int32)[None, :] == relative_rows(me, model_width)[:, None]).astype(BF)
    sort = lambda values: lax.dot_general(
        sort_rows, values, (((1,), (1,)), ((), ())), preferred_element_type=F32
    ).astype(BF)
    out_rel, second_rel = [sort(order.now(v)) for v in (grad_out16, second16)]
    order.close(second_core, shared_far, shared_core, out_rel, second_rel)
    shared_core.append(permute_core(order.now(shared_far)))
    shared_all = [p for both in zip((shared_cut, *shared_near, shared_far), shared_core) for p in both]
    shared16 = place_rows([shared_all], me, [(0, j, 0, shared_weight.shape[2]) for j in range(3)])
    shared_out, shared_back, shared_even, shared_odd = shared_call(
        order.now(second16), second_rel, grad_out16, out_rel, shared16
    )
    order.close(shared_back, second_near)

    results = [[None] * 4 for _ in range(per_device)]
    second_far = permute_far(order.now(select(second_near)))
    second_core += [permute_core(order.now(p)) for p in second_near]
    grad_far = permute_far(order.now(select(grad_near)))
    grads_even.append(grad_far)
    shared_sum = piece_sum(shared_even, shared_odd, is_core0)
    shared_core = shared_sum.core(order)
    results[0][0] = pair(0, 0, None, None)
    first_rel, context_rel = [sort(after(v, results[0][0][1])) for v in (first16, context16)]
    order.close(second_core, results[0][0][1], second_far, shared_core, grad_far, first_rel, context_rel)
    grad_core.append(permute_core(order.now(grad_far)))
    seconds_even.append(second_far)
    second_core.append(permute_core(order.now(second_far)))
    shared_far = shared_sum.far(order)
    results[0][1] = pair(0, 1, None, None)
    order.close(second_core[3], grad_core[3], results[0][1][1], shared_far)
    shared_near = shared_sum.near(order)
    results[0][2] = pair(0, 2, None, None)
    order.close(results[0][2][1])
    results[0][3] = pair(0, 3, None, None)
    order.close(results[0][3][1], shared_near)
    routed_grads = []

    def finish_expert(e):
        grads = weight_grad_call(order.now([result[2] for result in results[e]]), parts)
        routed_grads.append(lax.psum_scatter(grads, "dp", scatter_dimension=0, tiled=False))
        return grads

    order.close(finish_expert(0))
    for e in range(1, per_device):
        back_sum = PlaneSum([None] * 4, [None] * 4, is_core0) if e == per_device - 1 else None
        out_sum = PlaneSum([None] * 4, [None] * 4, is_core0) if e == per_device - 1 else None

        def step(j):
            results[e][j] = pair(e, j, results[e - 1][j][0], results[e - 1][j][3])
            if back_sum is not None:
                for total, found in zip((out_sum, back_sum), results[e][j][0]):
                    total.even[j], total.odd[j] = found

        step(3)
        order.close(results[e][3][1])
        waits = []
        if back_sum is not None:
            waits += [back_sum.core_of(3, order), out_sum.core_of(3, order)]
        step(1)
        order.close(results[e][1][1], waits)
        if back_sum is not None:
            waits = [back_sum.far(order), back_sum.core_of(1, order), out_sum.core_of(1, order)]
        step(2)
        order.close(results[e][2][1], waits)
        if back_sum is not None:
            order.close(back_sum.core_of(2, order))
            sides = back_sum.near(order)
            waits = [out_sum.core_of(2, order)]
        step(0)
        if back_sum is not None:
            gate_grads = [jnp.concatenate([result[1][:, 0] for result in row]) for row in results]
            gate_sent = jnp.take(jnp.stack(gate_grads, axis=1), relative, axis=0)
            gate_back = lax.all_to_all(gate_sent, "expert", split_axis=0, concat_axis=0, tiled=True)
            waits += [sides, gate_back]
        order.close(results[e][0][1], waits)
        if back_sum is not None:
            waits = [back_sum.core_of(0, order), out_sum.far(order), out_sum.core_of(0, order)]
        order.close(finish_expert(e), waits)
    grad_gate = order.now(gate_back).reshape(routed_count, seq_len).T
    logits = lax.dot_general(second16, router16t, (((1,), (1,)), ((), ())), preferred_element_type=F32)
    table = jnp.any(choices[:, :, None] == jnp.arange(routed_count, dtype=jnp.int32)[None, None, :], axis=1)
    chosen = jnp.where(table, logits, masked_score)
    chosen_exp = jnp.where(table, jnp.exp(chosen - jnp.max(chosen, axis=1, keepdims=True)), 0.0)
    gate_weights = chosen_exp / jnp.sum(chosen_exp, axis=1, keepdims=True)
    grad_logits = grad_gate - gate_weights * jnp.sum(grad_gate, axis=1, keepdims=True)
    wide_logits = jnp.pad(grad_logits, ((0, 0), (0, 128 - routed_count)))
    router_grad_full = lax.dot_general(
        grad_logits, second16.astype(F32), (((0,), (0,)), ((), ())), precision=lax.Precision.HIGHEST
    )
    order.close(order.now(wide_logits))

    out_near = out_sum.near(order)
    grad_hidden_state, grad_context16, out_even, out_odd, grad_gain_second = hidden_back_call(
        shared_back, order.now(wide_logits), router_pad, back_sum.take(0), sides, hidden_state, grad_out16, gains, context_rel, attn16[3]
    )
    order.close(grad_context16)

    proj_sum = piece_sum(out_even, out_odd, is_core0)
    proj_core = proj_sum.core(order)
    grad_query16, grad_key16, grad_value16, head_even, head_odd = heads_back_call(
        query16, key16, value16, order.now(grad_context16), log_totals, cosine, sine, first_rel, lengths, score_scale
    )
    order.close(proj_core, grad_query16, out_near)

    head_sum = piece_sum(head_even, head_odd, is_core0)
    proj_far = proj_sum.far(order)
    head_core = head_sum.core(order)
    input_grad, grad_gain_first, input_square = input_back_call(
        order.now(grad_query16), grad_key16, grad_value16, tokens, gains, grad_hidden_state, lengths, attn16[:3]
    )
    order.close(head_core, proj_far, input_grad)

    head_far = head_sum.far(order)
    proj_near = proj_sum.near(order)
    shared_grad = lax.all_to_all(
        jnp.swapaxes(shared_sum.total().astype(BF), 0, 1), "dp", split_axis=0, concat_axis=0, tiled=True
    )
    early_parts = update_call(
        0, order.now(routed_grads[0]), routed_weight, routed_moment, routed_average, [], rate_routed * step_root
    )
    order.close(head_far, proj_near, early_parts[-1])

    head_near = head_sum.near(order)
    proj_found = send_terms(after(proj_sum.total().astype(BF), head_sum.sent), 1, order)
    held = head_sum.sent
    block_value = after(hidden_state, held) + shared_out + out_sum.total()
    scalars = jnp.stack(
        [
            jnp.sum(valid_rows * block_value * block_value),
            input_square[0],
            length_here.astype(F32),
        ]
    )
    small_grads = jnp.concatenate([router_grad_full, grad_gain_first, grad_gain_second])
    scalars = jnp.broadcast_to(scalars[:, None], (3, model_width))
    small_grads = jnp.concatenate([small_grads, scalars])
    small_grads = jnp.pad(small_grads, ((0, 128 - small_grads.shape[0]), (0, 0)))
    small_grads = jnp.swapaxes(small_grads.T.reshape(parts, groups, -1, 128), 0, 1)
    small_found = lax.all_to_all(small_grads, "expert", split_axis=0, concat_axis=0, tiled=True)
    routed_parts = early_parts
    for e in range(1, per_device):
        routed_parts = update_call(
            e, order.now(routed_grads[e]), routed_weight, routed_moment, routed_average, routed_parts, rate_routed * step_root
        )
    order.close(head_near, routed_parts[-1])

    head_total = order.now(head_sum.total().astype(BF))
    head_found = send_terms(head_total, 1, order)
    proj_found, shared_grad, small_found = after((proj_found, shared_grad, small_found), head_total)
    small_total = tree_sum([small_found[r] for r in range(groups)])
    small_found = lax.all_to_all(small_total, "dp", split_axis=0, concat_axis=0, tiled=True)
    small_grad = tree_sum([small_found[d] for d in range(parts)])
    shared_grad = sum_terms([shared_grad[d] for d in range(parts)])
    attn_grad = jnp.concatenate([sum_terms(head_found), sum_terms(proj_found)])
    router_grad = small_grad[:, :routed_count]
    gain_grad = small_grad[:, routed_count : routed_count + 2].T
    row_sums = small_grad[0, routed_count + 2 : routed_count + 5]
    denominator = model_width * row_sums[2]
    masked_rms = jnp.stack(
        [jnp.sqrt(row_sums[0] / denominator), jnp.sqrt(row_sums[1] / denominator)]
    )
    attn_parts = update(
        attn_weight, attn_moment, attn_average, attn_grad, rate_attention * step_root
    )
    router_parts = update(
        router_weight, router_moment, router_average, router_grad, rate_router * step_root
    )
    shared_parts = update(
        shared_weight, shared_moment, shared_average, shared_grad, rate_shared * step_root
    )
    gain_parts = update(norm_gains, gain_moment, gain_average, gain_grad, rate_gains * step_root)
    return (
        block_value.astype(BF),
        input_grad,
        masked_rms,
        attn_parts[0],
        attn_parts[1],
        attn_parts[2],
        attn_parts[3],
        attn_parts[4],
        router_parts[0],
        router_parts[1],
        router_parts[2],
        router_parts[3],
        router_parts[4],
        shared_parts[0],
        shared_parts[1],
        shared_parts[2],
        shared_parts[3],
        shared_parts[4],
        routed_parts[0],
        routed_parts[1],
        routed_parts[2],
        routed_parts[3],
        routed_parts[4],
        gain_parts[0],
        gain_parts[1],
        gain_parts[2],
        gain_parts[3],
    )


def solution(mesh):
    placed = (
        P(("dp", "expert"), None),
        P(("dp", "expert"), None),
        P(("dp", "expert")),
        P(("dp", "expert"), None),
        P(None, ("dp", "expert"), None),
        P(None, ("dp", "expert"), None),
        P(None, ("dp", "expert"), None),
        P(("dp", "expert"), None),
        P(("dp", "expert"), None),
        P(("dp", "expert"), None),
        P(None, ("dp", "expert"), None),
        P(None, ("dp", "expert"), None),
        P(None, ("dp", "expert"), None),
        P("expert", None, "dp", None),
        P("expert", None, "dp", None),
        P("expert", None, "dp", None),
        P(None, ("dp", "expert")),
        P(None, ("dp", "expert")),
        P(None, ("dp", "expert")),
    )
    return jax.shard_map(
        local,
        mesh=mesh,
        in_specs=placed,
        out_specs=(
            P(("dp", "expert"), None),
            P(("dp", "expert"), None),
            P(),
            P(None, ("dp", "expert"), None),
            P(None, ("dp", "expert"), None),
            P(None, ("dp", "expert"), None),
            P(None, ("dp", "expert"), None),
            P(None, ("dp", "expert"), None),
            P(("dp", "expert"), None),
            P(("dp", "expert"), None),
            P(("dp", "expert"), None),
            P(("dp", "expert"), None),
            P(("dp", "expert"), None),
            P(None, ("dp", "expert"), None),
            P(None, ("dp", "expert"), None),
            P(None, ("dp", "expert"), None),
            P(None, ("dp", "expert"), None),
            P(None, ("dp", "expert"), None),
            P("expert", None, "dp", None),
            P("expert", None, "dp", None),
            P("expert", None, "dp", None),
            P("expert", None, "dp", None),
            P("expert", None, "dp", None),
            P(None, ("dp", "expert")),
            P(None, ("dp", "expert")),
            P(None, ("dp", "expert")),
            P(None, ("dp", "expert")),
        ),
        check_vma=False,
    )
```

```python
import functools
import math

import jax
import jax.numpy as jnp
from jax import lax
from jax.experimental import pallas as pl
from jax.experimental.layout import Layout, with_layout_constraint
from jax.experimental.pallas import tpu as pltpu
from jax.sharding import PartitionSpec as P

HEADS = 10
STEP = 3
BF = jnp.bfloat16
F32 = jnp.float32
BOTH = ("dp", "expert")


eps_norm = 1e-06
momentum_rate = 0.9
decay_rate = 0.0001
rate_attention = 0.01
rate_router = 0.03
rate_shared = 0.01
rate_routed = 0.04
rate_gains = 0.2
masked_score = -1e30
VMEM_LIMIT = 58 * 1024 * 1024


def silu_slope(pre_value):
    sigmoid_part = jax.nn.sigmoid(pre_value)
    return sigmoid_part * (1.0 + pre_value * (1.0 - sigmoid_part))


def update(weight, moment, average, gradient, step_rate):
    decayed = gradient + decay_rate * weight
    moment_new = momentum_rate * moment + decayed
    weight_new = weight - step_rate * (decayed + momentum_rate * moment_new)
    average_new = average + (weight_new - average) / (STEP + 1.0)
    return (gradient, weight_new, moment_new, average_new, weight_new.astype(BF))


def estimate(flops):
    return pl.CostEstimate(flops=flops, bytes_accessed=1, transcendentals=0)


def dot_nn(a,b): return lax.dot_general(a,b,(((1,),(0,)),((),())),preferred_element_type=F32)
def dot_nt(a,b): return lax.dot_general(a,b,(((1,),(1,)),((),())),preferred_element_type=F32)
def dot_tn(a,b): return lax.dot_general(a,b,(((0,),(0,)),((),())),preferred_element_type=F32)

def chunks(n,c): return [(s,min(c,n-s)) for s in range(0,n,c)]

def pair_columns(ff):
    return [(c0, cn, 2 * c0, 2 * c0 + cn) for c0, cn in chunks(ff, 256)]


def expert_pair_kernel(first, *refs):
    it = iter(refs)
    take = lambda count: [next(it) for _ in range(count)]
    eid_ref, choice_ref, slot_ref, router_ref, w_hbm = take(5)
    gate_ref = None if first else next(it)
    sources = [take(2), take(2)]
    prev = [] if first else [take(2), take(2)]
    outs = [take(2), take(2)]
    dg_ref, rows_out, dy_out, h_out, dab_out = take(5)
    gate_out = next(it) if first else None
    gu_v, down_v, tok, rows_v, dy_v, h_v, dab_v, ob, wsem, dsem, tsem, psem, osem, ssem = it
    n_dp = w_hbm.shape[0]
    width, ff = down_v.shape
    slab = width // n_dp
    seq = slot_ref.shape[1]
    cap = rows_v.shape[0] // 2
    tcopies = [[pltpu.make_async_copy(sources[j][q], tok.at[q, j], tsem.at[q, j]) for j in range(2)] for q in range(2)]
    wcopies = []
    for d in range(n_dp):
        own = pl.ds(d * slab, slab)
        for c, (c0, cn, g0, u0) in enumerate(pair_columns(ff)):
            for j, to in ((0, g0), (1, u0)):
                src = w_hbm.at[d, j, pl.ds(0, slab), pl.ds(c0, cn)]
                wcopies.append(pltpu.make_async_copy(src, gu_v.at[own, pl.ds(to, cn)], wsem.at[d, c, j]))
    dcopies = [
        pltpu.make_async_copy(w_hbm.at[d, 2, pl.ds(0, slab)], down_v.at[pl.ds(d * slab, slab)], dsem.at[d]) for d in range(n_dp)
    ]
    for copies in tcopies:
        for copy in copies:
            copy.start()
    lane = lax.broadcasted_iota(jnp.int32, (seq, 128), 1)
    sub = lax.broadcasted_iota(jnp.int32, (cap, seq), 0)
    eid = eid_ref[0]
    gcols, onehots = [], []
    for q in range(2):
        tcopies[q][0].wait()
        if q == 0:
            for copy in wcopies + dcopies:
                copy.start()
        sec = tok[q, 0]
        if first:
            logits = dot_nt(sec, router_ref[...])
            table = choice_ref[q, :, 0:1] == lane
            for k in range(1, choice_ref.shape[2]):
                table = table | (choice_ref[q, :, k : k + 1] == lane)
            masked = jnp.where(table, logits, masked_score)
            weight = jnp.where(table, jnp.exp(masked - jnp.max(masked, axis=1, keepdims=True)), 0.0)
            gates = weight / jnp.sum(weight, axis=1, keepdims=True)
            gate_out[q] = gates
        else:
            gates = gate_ref[q]
        gcol = jnp.sum(jnp.where(lane == eid, gates, 0.0), axis=1, keepdims=True)
        onehot = (slot_ref[q : q + 1, :] == sub).astype(F32).astype(BF)
        rows_v[q * cap : (q + 1) * cap, :] = dot_nn(onehot, sec).astype(BF)
        tcopies[q][1].wait()
        gated = (gcol * tok[q, 1].astype(F32)).astype(BF)
        dy_v[q * cap : (q + 1) * cap, :] = dot_nn(onehot, gated).astype(BF)
        gcols.append(gcol)
        onehots.append(onehot)
    pcopies = [pltpu.make_async_copy(prev[j][q], ob.at[q, j], psem.at[q, j]) for q in range(2) for j in range(2) if not first]
    for copy in pcopies:
        copy.start()
    saves = [pltpu.make_async_copy(rows_v, rows_out, ssem.at[0]), pltpu.make_async_copy(dy_v, dy_out, ssem.at[1])]
    for copy in saves:
        copy.start()
    for copy in wcopies + dcopies:
        copy.wait()
    gain_sum = jnp.zeros((2 * cap, 128), F32)
    for c0, cn, g0, u0 in pair_columns(ff):
        both = dot_nn(rows_v[...], gu_v[:, g0 : g0 + 2 * cn])
        a, b = both[:, :cn], both[:, cn:]
        dh = dot_nn(dy_v[...], down_v[:, c0 : c0 + cn])
        sigmoid = 0.5 * jnp.tanh(0.5 * a) + 0.5
        silu = a * sigmoid
        dsilu = dh * silu
        gain = dsilu * b
        for p0, pn in chunks(cn, 128):
            gain_sum = gain_sum + gain[:, p0 : p0 + pn]
        h_v[:, c0 : c0 + cn] = (silu * b).astype(BF)
        dab_v[:, g0 : g0 + cn] = (dh * b * (sigmoid + silu * (1.0 - sigmoid))).astype(BF)
        dab_v[:, u0 : u0 + cn] = dsilu.astype(BF)
    late = [pltpu.make_async_copy(h_v, h_out, ssem.at[2]), pltpu.make_async_copy(dab_v, dab_out, ssem.at[3])]
    for copy in late:
        copy.start()
    for copy in pcopies:
        copy.wait()
    sends = []
    gain_slot = jnp.sum(gain_sum, axis=1, keepdims=True)
    for q in range(2):
        spread = onehots[q].astype(F32) * gain_slot[q * cap : (q + 1) * cap]
        dg_ref[q] = jnp.broadcast_to(jnp.sum(spread, axis=0, keepdims=True), (8, seq))
    for n, (n0, nn) in enumerate(chunks(width, 512)):
        ns = slice(n0, n0 + nn)
        y = dot_nt(h_v[...], down_v[ns, :]).astype(BF)
        dr = dot_nt(dab_v[...], gu_v[ns, :]).astype(BF)
        for q in range(2):
            yt = dot_tn(onehots[q], y[q * cap : (q + 1) * cap])
            dt = dot_tn(onehots[q], dr[q * cap : (q + 1) * cap])
            yt = yt * gcols[q]
            if not first:
                yt = yt + ob[q, 0, :, ns].astype(F32)
                dt = dt + ob[q, 1, :, ns].astype(F32)
            ob[q, 0, :, ns] = yt.astype(BF)
            ob[q, 1, :, ns] = dt.astype(BF)
            for j in range(2):
                part = pl.ds(n0, nn)
                copy = pltpu.make_async_copy(ob.at[q, j, :, part], outs[j][q].at[:, part], osem.at[q, j, n])
                copy.start()
                sends.append(copy)
    for copy in saves + late + sends:
        copy.wait()


def expert_pair_call(eid, choice, slots, router_pad, w, secs, douts, prev, gates, cap):
    seq = slots.shape[1]
    width = secs[0].shape[1]
    n_dp, _, _, ff = w.shape
    parts = len(chunks(width, 512))
    flat = [] if prev is None else [v for pair in prev for v in pair]
    full = jax.ShapeDtypeStruct((seq, width), BF)
    shapes = [(2 * cap, width), (2 * cap, width), (2 * cap, ff), (2 * cap, 2 * ff)]
    dma = pltpu.SemaphoreType.DMA
    out = pl.pallas_call(
        functools.partial(expert_pair_kernel, prev is None),
        out_shape=[full] * 4
        + [jax.ShapeDtypeStruct((2, 8, seq), F32)]
        + [jax.ShapeDtypeStruct(shape, BF) for shape in shapes]
        + [jax.ShapeDtypeStruct((2, seq, 128), F32)] * (prev is None),
        in_specs=kernel_specs("svvva" + "v" * (prev is not None) + "a" * (4 + len(flat))),
        out_specs=kernel_specs("aaaavaaaa" + "v" * (prev is None)),
        scratch_shapes=[pltpu.VMEM((width, 2 * ff), BF), pltpu.VMEM((width, ff), BF), pltpu.VMEM((2, 2, seq, width), BF)]
        + [pltpu.VMEM(shape, BF) for shape in shapes]
        + [pltpu.VMEM((2, 2, seq, width), BF)]
        + [dma((n_dp, len(chunks(ff, 256)), 2)), dma((n_dp,)), dma((2, 2)), dma((2, 2)), dma((2, 2, parts)), dma((4,))],
        compiler_params=pltpu.CompilerParams(vmem_limit_bytes=VMEM_LIMIT),
        cost_estimate=estimate(18 * cap * width * ff),
        name="expert_pair",
    )(eid, choice, slots, router_pad, w, *([] if prev is None else [gates]), *secs, *douts, *flat)
    return (out[0:2], out[2:4]), out[4], out[5:9], out[9] if prev is None else gates


def weight_grad_kernel(count, *refs):
    saved = [refs[4 * i : 4 * i + 4] for i in range(count)]
    out_ref, rows_v, dy_v, h_v, dab_v, g_v, isem, osem = refs[4 * count :]
    width, ff = g_v.shape[1:]
    n_dp = out_ref.shape[0]
    slab = width // n_dp
    piece = rows_v.shape[0] // count
    loads = {}
    for j, to in ((1, dy_v), (2, h_v), (0, rows_v), (3, dab_v)):
        loads[j] = [
            pltpu.make_async_copy(saved[i][j], to.at[pl.ds(i * piece, piece)], isem.at[j, i]) for i in range(count)
        ]
        for copy in loads[j]:
            copy.start()
    stores = [
        [pltpu.make_async_copy(g_v.at[j, pl.ds(d * slab, slab)], out_ref.at[d, j], osem.at[j, d]) for d in range(n_dp)]
        for j in range(3)
    ]
    for copy in loads[1] + loads[2]:
        copy.wait()

    def down(i, carry):
        m = pl.ds(pl.multiple_of(i * 256, 256), 256)
        g_v[2, m, :] = dot_tn(dy_v[:, m], h_v[...]).astype(BF)
        return carry

    lax.fori_loop(0, width // 256, down, 0)
    for copy in stores[2]:
        copy.start()
    for copy in loads[0] + loads[3]:
        copy.wait()

    def front(i, carry):
        m = pl.ds(pl.multiple_of(i * 256, 256), 256)
        both = dot_tn(rows_v[:, m], dab_v[...])
        for c0, cn, g0, u0 in pair_columns(ff):
            g_v[0, m, c0 : c0 + cn] = both[:, g0 : g0 + cn].astype(BF)
            g_v[1, m, c0 : c0 + cn] = both[:, u0 : u0 + cn].astype(BF)
        return carry

    lax.fori_loop(0, width // 256, front, 0)
    for copy in stores[0] + stores[1]:
        copy.start()
    for copy in stores[0] + stores[1] + stores[2]:
        copy.wait()


def weight_grad_call(saved, n_dp):
    count = len(saved)
    width, ff = saved[0][0].shape[1], saved[0][2].shape[1]
    rows = count * saved[0][0].shape[0]
    dma = pltpu.SemaphoreType.DMA
    return pl.pallas_call(
        functools.partial(weight_grad_kernel, count),
        out_shape=jax.ShapeDtypeStruct((n_dp, 3, width // n_dp, ff), BF),
        in_specs=kernel_specs("a" * (4 * count)),
        out_specs=pl.BlockSpec(memory_space=pl.ANY),
        scratch_shapes=[pltpu.VMEM((rows, n), BF) for n in (width, width, ff, 2 * ff)]
        + [pltpu.VMEM((3, width, ff), BF), dma((4, count)), dma((3, n_dp))],
        compiler_params=pltpu.CompilerParams(vmem_limit_bytes=VMEM_LIMIT),
        cost_estimate=estimate(6 * rows * width * ff),
        name="expert_weights",
    )(*[v for part in saved for v in part])


def rotated(values, cosine, sine):
    return values * cosine + pltpu.roll(values, values.shape[1] // 2, 1) * sine


def head_block(h):
    return pl.ds(pl.multiple_of(h * 128, 128), 128)


def masked_scores(query, key, start, length, scale):
    scores = dot_nt(query, key) * scale
    at = lax.broadcasted_iota(jnp.int32, scores.shape, 0) + start
    to = lax.broadcasted_iota(jnp.int32, scores.shape, 1)
    return jnp.where((to <= at) & (to < length), scores, masked_score)


def attention_kernel(
    scale, tok_ref, gain_ref, cos_ref, sin_ref, len_ref, wq, wk, wv, wo,
    first_ref, q_ref, k_ref, v_ref, ctx_ref, lse_ref, hidden_ref, second_ref, w_v, sem,
):
    copies = [pltpu.make_async_copy(w, w_v.at[j], sem.at[j]) for j, w in enumerate((wq, wk, wv, wo))]
    for copy in copies:
        copy.start()
    seq, width = tok_ref.shape
    length = len_ref[0]
    x = tok_ref[...].astype(F32)
    inverse = lax.rsqrt(jnp.mean(x * x, axis=1, keepdims=True) + eps_norm)
    first_ref[...] = (x * inverse * gain_ref[0:1, :]).astype(BF)
    for j, out_ref in enumerate((q_ref, k_ref, v_ref)):
        copies[j].wait()
        for c0, cn in chunks(width, 256):
            lin = dot_nn(first_ref[...], w_v[j, :, c0 : c0 + cn])
            for h0, hn in chunks(cn, 128):
                part = lin[:, h0 : h0 + hn]
                if j < 2:
                    part = rotated(part, cos_ref[...], sin_ref[...])
                out_ref[:, c0 + h0 : c0 + h0 + hn] = part.astype(BF)
    lane = lax.broadcasted_iota(jnp.int32, (seq, 128), 1)
    block = 256

    def heads(g, carry):
        for u in range(2):
            h = g * 2 + u
            hs = head_block(h)
            logs = []
            for start in range(0, seq, block):
                end = start + block
                masked = masked_scores(q_ref[start:end, hs], k_ref[:end, hs], start, length, scale)
                peak = jnp.max(masked, axis=1, keepdims=True)
                weight = jnp.exp(masked - peak)
                total = jnp.sum(weight, axis=1, keepdims=True)
                probs = (weight / total).astype(BF)
                ctx_ref[start:end, hs] = dot_nn(probs, v_ref[:end, hs]).astype(BF)
                logs.append(peak + jnp.log(total))
            log = jnp.concatenate(logs, axis=0)
            lse_ref[...] = jnp.where(lane == h, log, lse_ref[...])
        return carry

    lse_ref[...] = jnp.zeros_like(lse_ref)
    lax.fori_loop(0, width // 256, heads, 0)
    copies[3].wait()
    squares = jnp.zeros((seq, 1), F32)
    for c0, cn in chunks(width, 256):
        cs = slice(c0, c0 + cn)
        hidden = tok_ref[:, cs].astype(F32) + dot_nn(ctx_ref[...], w_v[3, :, cs])
        hidden_ref[:, cs] = hidden
        squares = squares + jnp.sum(hidden * hidden, axis=1, keepdims=True)
    inverse = lax.rsqrt(squares / width + eps_norm)
    second_ref[...] = (hidden_ref[...] * inverse * gain_ref[1:2, :]).astype(BF)


def kernel_specs(places):
    kinds = {"v": pltpu.VMEM, "s": pltpu.SMEM, "a": pl.ANY}
    return [pl.BlockSpec(memory_space=kinds[p]) for p in places]


def attention_call(tokens, gains, cosine, sine, lengths, weights, scale):
    seq, width = tokens.shape
    half = jax.ShapeDtypeStruct((seq, width), BF)
    return pl.pallas_call(
        functools.partial(attention_kernel, scale),
        out_shape=[half] * 5
        + [jax.ShapeDtypeStruct((seq, 128), F32), jax.ShapeDtypeStruct((seq, width), F32), half],
        in_specs=kernel_specs("vvvvsaaaa"),
        out_specs=kernel_specs("vvvvvvvv"),
        scratch_shapes=[pltpu.VMEM((4, width, width), BF), pltpu.SemaphoreType.DMA((4,))],
        compiler_params=pltpu.CompilerParams(vmem_limit_bytes=VMEM_LIMIT),
        cost_estimate=estimate(0),
        name="attention_forward",
    )(tokens, gains, cosine, sine, lengths, *weights)


def store_pieces(even_ref, odd_ref, slot, rows_ref, grad_ref):
    count, _, piece, _ = even_ref.shape
    for part, out_ref in enumerate((even_ref, odd_ref)):
        for j in range(count):
            at = (part * count + j) * piece
            out_ref[j, slot] = dot_nn(rows_ref[at : at + piece, :], grad_ref[...]).astype(BF)


def piece_shape(number, width, out_width):
    count = lax.axis_size("expert") // 2
    return jax.ShapeDtypeStruct((count, number, width // (2 * count), out_width), BF)


def hidden_back_kernel(
    dn_ref, logit_ref, router_ref, base_ref, core_ref, side_x_ref, side_y_ref, hidden_ref, dout_ref, gain_ref, ctx_ref, wo, dhid_ref, dctx_ref, even_ref, odd_ref, gain_out, w_v, dattn_v, sem
):
    copy = pltpu.make_async_copy(wo, w_v, sem)
    copy.start()
    seq, width = hidden_ref.shape
    hidden = hidden_ref[...]
    inverse = lax.rsqrt(jnp.mean(hidden * hidden, axis=1, keepdims=True) + eps_norm)
    hat = hidden * inverse
    logits = logit_ref[...]
    high = logits.astype(BF)
    rest = logits - high.astype(F32)
    low = rest.astype(BF)
    least = (rest - low.astype(F32)).astype(BF)
    routers = sum(dot_nn(part, router_ref[...]) for part in (least, low, high))
    dn = dn_ref[...] + routers + base_ref[...].astype(F32) + core_ref[...].astype(F32) + side_x_ref[...].astype(F32) + side_y_ref[...].astype(F32)
    gain_out[...] = jnp.sum(dn * hat, axis=0, keepdims=True)
    scaled = dn * gain_ref[1:2, :]
    mean = jnp.mean(scaled * hat, axis=1, keepdims=True)
    dhid = dout_ref[...].astype(F32) + inverse * (scaled - hat * mean)
    dhid_ref[...] = dhid
    dattn_v[...] = dhid.astype(BF)
    store_pieces(even_ref, odd_ref, 0, ctx_ref, dattn_v)
    copy.wait()
    for c0, cn in chunks(width, 256):
        dctx_ref[:, c0 : c0 + cn] = dot_nt(dattn_v[...], w_v[c0 : c0 + cn, :]).astype(BF)


def hidden_back_call(dn, logits, router, base, core, sides, hidden, dout, gains, ctx_rel, wo):
    seq, width = hidden.shape
    half = jax.ShapeDtypeStruct((seq, width), BF)
    part = piece_shape(1, width, width)
    return pl.pallas_call(
        hidden_back_kernel,
        out_shape=[jax.ShapeDtypeStruct((seq, width), F32), half, part, part, jax.ShapeDtypeStruct((1, width), F32)],
        in_specs=kernel_specs("vvvvvvvvvvva"),
        out_specs=kernel_specs("vvvvv"),
        scratch_shapes=[pltpu.VMEM((width, width), BF), pltpu.VMEM((seq, width), BF), pltpu.SemaphoreType.DMA],
        compiler_params=pltpu.CompilerParams(vmem_limit_bytes=VMEM_LIMIT),
        cost_estimate=estimate(15 * seq * width * width),
        name="hidden_backward",
    )(dn, logits, router, base, core, *sides, hidden, dout, gains, ctx_rel, wo)


def heads_back_kernel(
    scale, q_ref, k_ref, v_ref, dctx_ref, lse_ref, cos_ref, sin_ref, first_ref, len_ref,
    dq_ref, dk_ref, dv_ref, even_ref, odd_ref,
):
    seq, width = q_ref.shape
    length = len_ref[0]
    lane = lax.broadcasted_iota(jnp.int32, (seq, 128), 1)
    block = 256

    def heads(g, carry):
        for u in range(2):
            h = g * 2 + u
            hs = head_block(h)
            log = jnp.sum(jnp.where(lane == h, lse_ref[...], 0.0), axis=1, keepdims=True)
            key_parts, value_parts = [], []
            for start in range(0, seq, block):
                end = start + block
                rows = slice(start, end)
                masked = masked_scores(q_ref[rows, hs], k_ref[:end, hs], start, length, scale)
                probs = jnp.exp(masked - log[rows])
                dprobs = dot_nt(dctx_ref[rows, hs], v_ref[:end, hs])
                delta = jnp.sum(probs * dprobs, axis=1, keepdims=True)
                dscores = (probs * (dprobs - delta)).astype(BF)
                dq = dot_nn(dscores, k_ref[:end, hs]) * scale
                dq_ref[rows, hs] = rotated(dq, cos_ref[rows, :], -sin_ref[rows, :]).astype(BF)
                key_parts.append(dot_tn(dscores, q_ref[rows, hs]))
                value_parts.append(dot_tn(probs.astype(BF), dctx_ref[rows, hs]))
            for start in range(0, seq, block):
                rows = slice(start, start + block)
                dk = sum(p[rows] for p in key_parts if p.shape[0] > start) * scale
                dv = sum(p[rows] for p in value_parts if p.shape[0] > start)
                dk_ref[rows, hs] = rotated(dk, cos_ref[rows, :], -sin_ref[rows, :]).astype(BF)
                dv_ref[rows, hs] = dv.astype(BF)
        return carry

    lax.fori_loop(0, width // 256, heads, 0)
    store_pieces(even_ref, odd_ref, 2, first_ref, dv_ref)
    store_pieces(even_ref, odd_ref, 0, first_ref, dq_ref)
    store_pieces(even_ref, odd_ref, 1, first_ref, dk_ref)


def heads_back_call(q, k, v, dctx, lse, cosine, sine, first_rel, lengths, scale):
    seq, width = q.shape
    half = jax.ShapeDtypeStruct((seq, width), BF)
    wide = piece_shape(3, width, width)
    return pl.pallas_call(
        functools.partial(heads_back_kernel, scale),
        out_shape=[half] * 3 + [wide] * 2,
        in_specs=kernel_specs("vvvvvvvvs"),
        out_specs=kernel_specs("v" * 5),
        compiler_params=pltpu.CompilerParams(vmem_limit_bytes=VMEM_LIMIT),
        cost_estimate=estimate(26 * seq * width * width),
        name="heads_backward",
    )(q, k, v, dctx, lse, cosine, sine, first_rel, lengths)


def input_back_kernel(
    dq_ref, dk_ref, dv_ref, tok_ref, gain_ref, dhid_ref, len_ref, wq, wk, wv, out_ref, gain_out, sum_ref, w_v, dn_v, sem
):
    copies = [pltpu.make_async_copy(w, w_v.at[j], sem.at[j]) for j, w in enumerate((wq, wk, wv))]
    for copy in copies:
        copy.start()
    seq, width = tok_ref.shape
    x = tok_ref[...].astype(F32)
    inverse = lax.rsqrt(jnp.mean(x * x, axis=1, keepdims=True) + eps_norm)
    for copy in copies:
        copy.wait()
    for c0, cn in chunks(width, 256):
        cs = slice(c0, c0 + cn)
        dn_v[:, cs] = (
            dot_nt(dq_ref[...], w_v[0, cs, :]) + dot_nt(dk_ref[...], w_v[1, cs, :]) + dot_nt(dv_ref[...], w_v[2, cs, :])
        )
    hat = tok_ref[...].astype(F32) * inverse
    dn = dn_v[...]
    gain_out[...] = jnp.sum(dn * hat, axis=0, keepdims=True)
    scaled = dn * gain_ref[0:1, :]
    mean = jnp.mean(scaled * hat, axis=1, keepdims=True)
    result = dhid_ref[...] + inverse * (scaled - hat * mean)
    out_ref[...] = result
    valid = lax.broadcasted_iota(jnp.int32, result.shape, 0) < len_ref[0]
    sum_ref[0] = jnp.sum(jnp.where(valid, result * result, 0.0))


def input_back_call(dq, dk, dv, tokens, gains, dhidden, lengths, weights):
    seq, width = tokens.shape
    return pl.pallas_call(
        input_back_kernel,
        out_shape=[
            jax.ShapeDtypeStruct((seq, width), F32),
            jax.ShapeDtypeStruct((1, width), F32),
            jax.ShapeDtypeStruct((1,), F32),
        ],
        in_specs=kernel_specs("vvvvvvsaaa"),
        out_specs=kernel_specs("vvs"),
        scratch_shapes=[pltpu.VMEM((3, width, width), BF), pltpu.VMEM((seq, width), F32), pltpu.SemaphoreType.DMA((3,))],
        compiler_params=pltpu.CompilerParams(vmem_limit_bytes=VMEM_LIMIT),
        cost_estimate=estimate(18 * seq * width * width),
        name="input_backward",
    )(dq, dk, dv, tokens, gains, dhidden, lengths, *weights)


def shared_kernel(
    second_ref, second_rel_ref, dout_ref, dout_rel_ref, wg, wu, wd, out_ref, dn_ref, even_ref, odd_ref, w_v, h_v, da_v, db_v, sem
):
    copies = [pltpu.make_async_copy(w, w_v.at[j], sem.at[j]) for j, w in enumerate((wg, wu, wd))]
    for copy in copies:
        copy.start()
    for copy in copies:
        copy.wait()
    width, ff = w_v.shape[1:]
    for c0, cn in chunks(ff, 256):
        cs = slice(c0, c0 + cn)
        gate = dot_nn(second_ref[...], w_v[0, :, cs])
        up = dot_nn(second_ref[...], w_v[1, :, cs])
        back = dot_nn(dout_ref[...], w_v[2, :, cs])
        sigmoid = 1.0 / (1.0 + jnp.exp(-gate))
        silu = gate * sigmoid
        h_v[:, cs] = (silu * up).astype(BF)
        da_v[:, cs] = (back * up * (sigmoid * (1.0 + gate * (1.0 - sigmoid)))).astype(BF)
        db_v[:, cs] = (back * silu).astype(BF)
    for c0, cn in chunks(width, 256):
        cs = slice(c0, c0 + cn)
        out_ref[:, cs] = dot_nt(h_v[...], w_v[2, cs, :])
        dn_ref[:, cs] = dot_nt(da_v[...], w_v[0, cs, :]) + dot_nt(db_v[...], w_v[1, cs, :])
    store_pieces(even_ref, odd_ref, 0, second_rel_ref, da_v)
    store_pieces(even_ref, odd_ref, 1, second_rel_ref, db_v)
    store_pieces(even_ref, odd_ref, 2, dout_rel_ref, h_v)


def shared_call(second, second_rel, dout, dout_rel, weights):
    seq, width = second.shape
    ff = weights[0].shape[1]
    full = jax.ShapeDtypeStruct((seq, width), F32)
    part = piece_shape(3, width, ff)
    return pl.pallas_call(
        shared_kernel,
        out_shape=[full, full, part, part],
        in_specs=kernel_specs("vvvvaaa"),
        out_specs=kernel_specs("vvvv"),
        scratch_shapes=[pltpu.VMEM((3, width, ff), BF)]
        + [pltpu.VMEM((seq, ff), BF)] * 3
        + [pltpu.SemaphoreType.DMA((3,))],
        compiler_params=pltpu.CompilerParams(vmem_limit_bytes=VMEM_LIMIT),
        cost_estimate=estimate(0),
        name="shared_expert",
    )(second, second_rel, dout, dout_rel, *weights)


def update_kernel(rate, grad_ref, w_ref, m_ref, a_ref, *refs):
    grad_out, new_out, moment_out, average_out, copy_out = refs[-5:]
    parts = update(w_ref[0, 0], m_ref[0, 0], a_ref[0, 0], grad_ref[0].astype(F32), rate)
    for target, part in zip((grad_out, new_out, moment_out, average_out, copy_out), parts):
        target[0, 0] = part


def update_call(e, grad, weight, moment, average, done, rate):
    experts, kinds, rows, ff = weight.shape
    cuts = 2 if rows % 32 == 0 else 1
    full = pl.BlockSpec((1, 1, rows // cuts, ff), lambda j, i: (e, j, i, 0))
    return pl.pallas_call(
        functools.partial(update_kernel, rate),
        grid=(kinds, cuts),
        out_shape=[jax.ShapeDtypeStruct(weight.shape, F32)] * 4 + [jax.ShapeDtypeStruct(weight.shape, BF)],
        in_specs=[pl.BlockSpec((1, rows // cuts, ff), lambda j, i: (j, i, 0))]
        + [full] * 3
        + [pl.BlockSpec(memory_space=pl.ANY)] * len(done),
        out_specs=[full] * 5,
        input_output_aliases={4 + i: i for i in range(len(done))},
        compiler_params=pltpu.CompilerParams(vmem_limit_bytes=VMEM_LIMIT),
        cost_estimate=estimate(10_000_000_000),
        name="routed_update",
    )(grad, weight, moment, average, *done)


def permute(values, pairs):
    return lax.ppermute(values, "expert", pairs)


def pairs_of(mask, count):
    return [(i, i ^ mask) for i in range(count)]


def mixed_pairs(even_mask, odd_mask, count):
    return [(i, i ^ (odd_mask if i % 2 else even_mask)) for i in range(count)]


def after(values, *others):
    return lax.optimization_barrier((values, others))[0] if others else values


class Order:
    def __init__(self):
        self.last = ()

    def now(self, values):
        return after(values, *self.last)

    def close(self, *values):
        self.last = values


def send_dp(values, k):
    return lax.ppermute(values, "dp", [(i, i ^ k) for i in range(lax.axis_size("dp"))])


def stack_kernel(at_ref, *refs):
    count = (len(refs) - 2)
    copies = [
        pltpu.make_async_copy(refs[k], refs[count].at[at_ref[0] ^ k], refs[-1].at[k]) for k in range(count)
    ]
    for copy in copies:
        copy.start()
    for copy in copies:
        copy.wait()


def stack_dp(pieces):
    count = len(pieces)
    return pl.pallas_call(
        stack_kernel,
        out_shape=jax.ShapeDtypeStruct((count,) + pieces[0].shape, BF),
        in_specs=kernel_specs("s" + "a" * count),
        out_specs=pl.BlockSpec(memory_space=pltpu.VMEM),
        scratch_shapes=[pltpu.SemaphoreType.DMA((count,))],
        compiler_params=pltpu.CompilerParams(vmem_limit_bytes=VMEM_LIMIT),
        cost_estimate=estimate(0),
        name="stack_dp",
    )(lax.axis_index("dp")[None], *pieces)


def send_terms(terms, axis, order):
    here = lax.axis_index("dp")
    found = []
    for k in range(lax.axis_size("dp")):
        term = lax.dynamic_index_in_dim(terms, here ^ k, axis=axis, keepdims=False)
        found.append(send_dp(order.now(term), k) if k else order.now(term))
    return found


def sum_terms(found):
    return tree_sum([term.astype(F32) for term in found])


def tree_sum(terms):
    while len(terms) > 1:
        terms = [a + b for a, b in zip(terms[::2], terms[1::2])]
    return terms[0]


def permute_near(values):
    count = lax.axis_size("expert")
    return permute(values, pairs_of(2, count)), permute(values, pairs_of(4, count))


def permute_far(values):
    return permute(values, mixed_pairs(4, 2, lax.axis_size("expert")))


def permute_core(values):
    return permute(values, pairs_of(1, lax.axis_size("expert")))


def row_major(values):
    return with_layout_constraint(values, Layout(tuple(range(values.ndim))))


class PlaneSum:
    def __init__(self, even, odd, is_core0):
        self.even, self.odd, self.is_core0, self.kind = even, odd, is_core0, getattr(even, "dtype", BF)
        self.other = [None] * len(even)

    def take(self, j):
        return self.even[j].astype(F32) + self.other[j].astype(F32)

    def core(self, order):
        self.other = row_major(permute_core(row_major(order.now(self.odd))))
        return self.other

    def core_of(self, j, order):
        self.other[j] = permute_core(order.now(self.odd[j]))
        return self.other[j]

    def far(self, order):
        self.third = permute_far(order.now(self.take(3).astype(self.kind)))
        return self.third

    def near(self, order):
        count = lax.axis_size("expert")
        if not isinstance(self.other, list):
            self.other = order.now(self.other)
        third = self.third.astype(F32)
        to_x = (self.take(1) + jnp.where(self.is_core0, third, 0.0)).astype(self.kind)
        to_y = (self.take(2) + jnp.where(self.is_core0, 0.0, third)).astype(self.kind)
        to_x, to_y = self.sent = order.now((to_x, to_y))
        self.sides = (permute(to_x, pairs_of(2, count)), permute(to_y, pairs_of(4, count)))
        return self.sides

    def total(self):
        return self.take(0) + self.sides[0].astype(F32) + self.sides[1].astype(F32)


def place_kernel(cuts, at_ref, *refs):
    sem = refs[-1]
    outs = refs[-1 - len(cuts) : -1]
    count = sem.shape[0]
    copies = []
    for i, (group, kind, column) in enumerate(cuts):
        for r in range(count):
            source = refs[group * count + r].at[:, kind, :, pl.ds(column, outs[i].shape[3])]
            copies.append(pltpu.make_async_copy(source, outs[i].at[:, at_ref[0] ^ r], sem.at[r, i]))
    for copy in copies:
        copy.start()
    for copy in copies:
        copy.wait()


def place_rows(groups, me, cuts):
    count = len(groups[0])
    parts, _, rows, _ = groups[0][0].shape
    shapes = [(parts, count, rows, cut[3]) for cut in cuts]
    out = pl.pallas_call(
        functools.partial(place_kernel, [cut[:3] for cut in cuts]),
        out_shape=[jax.ShapeDtypeStruct(shape, BF) for shape in shapes],
        in_specs=kernel_specs("s" + "a" * (count * len(groups))),
        out_specs=kernel_specs("v" * len(cuts)),
        scratch_shapes=[pltpu.SemaphoreType.DMA((count, len(cuts)))],
        compiler_params=pltpu.CompilerParams(vmem_limit_bytes=VMEM_LIMIT),
        cost_estimate=estimate(0),
        name="place_rows",
    )(me[None], *[piece for group in groups for piece in group])
    return [v.reshape(parts * count * rows, v.shape[3]) for v in out]


def piece_sum(even, odd, is_core0):
    parts = lax.axis_size("dp")
    cut = even.shape[:2] + (parts, even.shape[2] // parts, even.shape[3])
    return PlaneSum(even.reshape(cut), odd.reshape(cut), is_core0)


def relative_rows(me, width):
    parts, count = lax.axis_size("dp"), lax.axis_size("expert")
    rows = width // (parts * count)
    far = jnp.concatenate([jnp.arange(0, count, 2, dtype=jnp.int32), jnp.arange(1, count, 2, dtype=jnp.int32)])
    owner = jnp.arange(parts, dtype=jnp.int32)[None, :] * count + (me ^ far)[:, None]
    return (owner[:, :, None] * rows + jnp.arange(rows, dtype=jnp.int32)).reshape(width)


def local(
    tokens,
    cotangent,
    lengths,
    choices,
    attn_weight,
    attn_moment,
    attn_average,
    router_weight,
    router_moment,
    router_average,
    shared_weight,
    shared_moment,
    shared_average,
    routed_weight,
    routed_moment,
    routed_average,
    norm_gains,
    gain_moment,
    gain_average,
):
    seq_len, model_width = tokens.shape
    topk_count = choices.shape[1]
    head_dim = model_width // HEADS
    groups = lax.axis_size("expert")
    routed_count = routed_weight.shape[0] * groups
    capacity = (seq_len * topk_count * 8 // (7 * routed_count) + 7) // 8 * 8
    total_tokens = seq_len * groups * lax.axis_size("dp")
    step_root = 1.0 / math.sqrt(total_tokens)
    score_scale = 1.0 / math.sqrt(head_dim)
    me = lax.axis_index("expert")
    is_core0 = lax.rem(me, 2) == 0
    relative = me ^ jnp.arange(groups, dtype=jnp.int32)
    per_device = routed_weight.shape[0]
    positions = jnp.arange(seq_len, dtype=jnp.int32)
    length_here = lengths[0]
    valid_rows = (positions < length_here).astype(F32)[:, None]
    grad_out = cotangent.astype(F32) * valid_rows
    grad_out16 = grad_out.astype(BF)

    order = Order()
    select = lambda pair: jnp.where(is_core0, *pair)
    small = jnp.concatenate([router_weight, norm_gains.T], axis=1)
    small = jnp.pad(small[None], ((0, 1), (0, 0), (0, 128 - small.shape[1])))
    parts = lax.axis_size("dp")
    front_own = jnp.concatenate([attn_weight[:2], small], axis=2).astype(BF)
    back_own = attn_weight[2:].astype(BF)
    shared_own = shared_weight.astype(BF)
    front_parts = [front_own] + [send_dp(front_own, k) for k in range(1, parts)]
    grad_near = permute_near(grad_out16)
    order.close(front_parts, grad_near)
    back_parts = [back_own] + [send_dp(order.now(back_own), k) for k in range(1, parts)]
    front = stack_dp(front_parts)

    choice_own = jnp.pad(choices.T.astype(BF), ((0, 16 - topk_count), (0, 0)))
    choice_all = lax.all_to_all(
        jnp.broadcast_to(choice_own, (groups,) + choice_own.shape), "expert", split_axis=0, concat_axis=0, tiled=True
    )
    front_near = permute_near(order.now(front))
    order.close(front_near, back_parts)
    back = stack_dp(back_parts)
    shared_cut = lax.all_to_all(
        order.now(jnp.broadcast_to(shared_own, (parts,) + shared_own.shape)), "dp", split_axis=0, concat_axis=0, tiled=True
    )

    front_held = list(order.now((front, *front_near)))
    back_near = permute_near(order.now(back))
    front_far = permute_far(order.now(select(front_near)))
    front_core = [permute_core(order.now(p)) for p in (front, *front_near)]
    order.close(back_near, front_far, front_core, shared_cut)
    routed_low = [routed_weight[e].astype(BF) for e in range(per_device)]
    routed16 = [lax.all_gather(low, "dp", axis=0, tiled=False) for low in order.now(routed_low)]

    back_held = list(order.now((back, *back_near)))
    back_far = permute_far(order.now(select(back_near)))
    back_core = [permute_core(order.now(p)) for p in (back, *back_near)]
    front_core.append(permute_core(order.now(front_far)))
    order.close(back_far, back_core, front_core)
    back_core.append(permute_core(order.now(back_far)))
    shared_near = permute_near(order.now(shared_cut))
    grad_core = [permute_core(order.now(p)) for p in (grad_out16, *grad_near)]
    front = [p for pair in zip((*front_held, front_far), front_core) for p in pair]
    back = [p for pair in zip((*back_held, back_far), back_core) for p in pair]
    cuts = [(group, kind, 0, model_width) for group in range(2) for kind in range(2)]
    *attn16, small_all = place_rows([front, back], me, cuts + [(0, 0, model_width, 128)])
    small_all = small_all.T
    router16t = small_all[:routed_count]
    gains16 = small_all[routed_count : routed_count + 2]
    choice_all = jnp.take(choice_all[:, :topk_count], relative, axis=0).astype(jnp.int32)
    own_experts = me * per_device + jnp.arange(per_device, dtype=jnp.int32)
    hits = jnp.any(choice_all[:, None] == own_experts[None, :, None, None], axis=2)
    before = (positions[:, None] < positions[None, :]).astype(BF)
    ranks = jnp.einsum("set,tu->seu", hits.astype(BF), before, preferred_element_type=F32).astype(jnp.int32)
    slot_all = jnp.where(hits, ranks, -1)
    choice_all = jnp.transpose(choice_all, (0, 2, 1))
    gain_first = gains16[0].astype(F32)
    gain_second = gains16[1].astype(F32)
    half_dim = head_dim // 2
    frequency = 10000.0 ** (-jnp.arange(half_dim, dtype=F32) / half_dim)
    angles = positions.astype(F32)[:, None] * frequency[None, :]
    cosine = jnp.concatenate([jnp.cos(angles), jnp.cos(angles)], axis=1)
    sine = jnp.concatenate([-jnp.sin(angles), jnp.sin(angles)], axis=1)
    gains = jnp.stack([gain_first, gain_second])
    first16, query16, key16, value16, context16, log_totals, hidden_state, second16 = attention_call(
        tokens, gains, cosine, sine, lengths, attn16, score_scale
    )
    order.close(second16, shared_near, grad_core)

    router_pad = jnp.pad(router16t, ((0, 128 - routed_count), (0, 0)))
    shared_sent = order.now(select(shared_near))
    shared_far = permute_far(shared_sent)
    second_near = permute_near(after(second16, shared_sent))
    second_core = [permute_core(second16)]
    grads_even = [grad_out16, *grad_near]
    seconds_even = [second16, *second_near]

    def pair(e, j, prev, gates):
        return expert_pair_call(
            own_experts[e][None],
            choice_all[2 * j : 2 * j + 2],
            slot_all[2 * j : 2 * j + 2, e],
            router_pad,
            routed16[e],
            order.now((seconds_even[j], second_core[j])),
            (grads_even[j], grad_core[j]),
            prev,
            gates,
            capacity,
        )

    shared_core = [permute_core(order.now(p)) for p in (shared_cut, *shared_near)]
    sort_rows = (jnp.arange(model_width, dtype=jnp.int32)[None, :] == relative_rows(me, model_width)[:, None]).astype(BF)
    sort = lambda values: lax.dot_general(
        sort_rows, values, (((1,), (1,)), ((), ())), preferred_element_type=F32
    ).astype(BF)
    out_rel, second_rel = [sort(order.now(v)) for v in (grad_out16, second16)]
    order.close(second_core, shared_far, shared_core, out_rel, second_rel)
    shared_core.append(permute_core(order.now(shared_far)))
    shared_all = [p for both in zip((shared_cut, *shared_near, shared_far), shared_core) for p in both]
    shared16 = place_rows([shared_all], me, [(0, j, 0, shared_weight.shape[2]) for j in range(3)])
    shared_out, shared_back, shared_even, shared_odd = shared_call(
        order.now(second16), second_rel, grad_out16, out_rel, shared16
    )
    order.close(shared_back, second_near)

    results = [[None] * 4 for _ in range(per_device)]
    second_far = permute_far(order.now(select(second_near)))
    second_core += [permute_core(order.now(p)) for p in second_near]
    grad_far = permute_far(order.now(select(grad_near)))
    grads_even.append(grad_far)
    shared_sum = piece_sum(shared_even, shared_odd, is_core0)
    shared_core = shared_sum.core(order)
    results[0][0] = pair(0, 0, None, None)
    first_rel, context_rel = [sort(after(v, results[0][0][1])) for v in (first16, context16)]
    order.close(second_core, results[0][0][1], second_far, shared_core, grad_far, first_rel, context_rel)
    grad_core.append(permute_core(order.now(grad_far)))
    seconds_even.append(second_far)
    second_core.append(permute_core(order.now(second_far)))
    shared_far = shared_sum.far(order)
    results[0][1] = pair(0, 1, None, None)
    order.close(second_core[3], grad_core[3], results[0][1][1], shared_far)
    shared_near = shared_sum.near(order)
    results[0][2] = pair(0, 2, None, None)
    order.close(results[0][2][1])
    results[0][3] = pair(0, 3, None, None)
    order.close(results[0][3][1], shared_near)
    routed_grads = []

    def finish_expert(e):
        grads = weight_grad_call(order.now([result[2] for result in results[e]]), parts)
        routed_grads.append(lax.psum_scatter(grads, "dp", scatter_dimension=0, tiled=False))
        return grads

    order.close(finish_expert(0))
    for e in range(1, per_device):
        back_sum = PlaneSum([None] * 4, [None] * 4, is_core0) if e == per_device - 1 else None
        out_sum = PlaneSum([None] * 4, [None] * 4, is_core0) if e == per_device - 1 else None

        def step(j):
            results[e][j] = pair(e, j, results[e - 1][j][0], results[e - 1][j][3])
            if back_sum is not None:
                for total, found in zip((out_sum, back_sum), results[e][j][0]):
                    total.even[j], total.odd[j] = found

        step(3)
        order.close(results[e][3][1])
        waits = []
        if back_sum is not None:
            waits += [back_sum.core_of(3, order), out_sum.core_of(3, order)]
        step(1)
        order.close(results[e][1][1], waits)
        if back_sum is not None:
            waits = [back_sum.far(order), back_sum.core_of(1, order), out_sum.core_of(1, order)]
        step(2)
        order.close(results[e][2][1], waits)
        if back_sum is not None:
            order.close(back_sum.core_of(2, order))
            sides = back_sum.near(order)
            waits = [out_sum.core_of(2, order)]
        step(0)
        if back_sum is not None:
            gate_grads = [jnp.concatenate([result[1][:, 0] for result in row]) for row in results]
            gate_sent = jnp.take(jnp.stack(gate_grads, axis=1), relative, axis=0)
            gate_back = lax.all_to_all(gate_sent, "expert", split_axis=0, concat_axis=0, tiled=True)
            waits += [sides, gate_back]
        order.close(results[e][0][1], waits)
        if back_sum is not None:
            waits = [back_sum.core_of(0, order), out_sum.far(order), out_sum.core_of(0, order)]
        order.close(finish_expert(e), waits)
    grad_gate = order.now(gate_back).reshape(routed_count, seq_len).T
    logits = lax.dot_general(second16, router16t, (((1,), (1,)), ((), ())), preferred_element_type=F32)
    table = jnp.any(choices[:, :, None] == jnp.arange(routed_count, dtype=jnp.int32)[None, None, :], axis=1)
    chosen = jnp.where(table, logits, masked_score)
    chosen_exp = jnp.where(table, jnp.exp(chosen - jnp.max(chosen, axis=1, keepdims=True)), 0.0)
    gate_weights = chosen_exp / jnp.sum(chosen_exp, axis=1, keepdims=True)
    grad_logits = grad_gate - gate_weights * jnp.sum(grad_gate, axis=1, keepdims=True)
    wide_logits = jnp.pad(grad_logits, ((0, 0), (0, 128 - routed_count)))
    router_grad_full = lax.dot_general(
        grad_logits, second16.astype(F32), (((0,), (0,)), ((), ())), precision=lax.Precision.HIGHEST
    )
    order.close(order.now(wide_logits))

    out_near = out_sum.near(order)
    grad_hidden_state, grad_context16, out_even, out_odd, grad_gain_second = hidden_back_call(
        shared_back, order.now(wide_logits), router_pad, back_sum.even[0], back_sum.other[0], sides, hidden_state, grad_out16, gains, context_rel, attn16[3]
    )
    order.close(grad_context16)

    proj_sum = piece_sum(out_even, out_odd, is_core0)
    proj_core = proj_sum.core(order)
    grad_query16, grad_key16, grad_value16, head_even, head_odd = heads_back_call(
        query16, key16, value16, order.now(grad_context16), log_totals, cosine, sine, first_rel, lengths, score_scale
    )
    order.close(proj_core, grad_query16, out_near)

    head_sum = piece_sum(head_even, head_odd, is_core0)
    proj_far = proj_sum.far(order)
    head_core = head_sum.core(order)
    input_grad, grad_gain_first, input_square = input_back_call(
        order.now(grad_query16), grad_key16, grad_value16, tokens, gains, grad_hidden_state, lengths, attn16[:3]
    )
    order.close(head_core, proj_far, input_grad)

    head_far = head_sum.far(order)
    proj_near = proj_sum.near(order)
    shared_grad = lax.all_to_all(
        order.now(jnp.swapaxes(shared_sum.total().astype(BF), 0, 1)), "dp", split_axis=0, concat_axis=0, tiled=True
    )
    early_parts = update_call(
        0, order.now(routed_grads[0]), routed_weight, routed_moment, routed_average, [], rate_routed * step_root
    )
    order.close(head_far, proj_near, early_parts[-1])

    head_near = head_sum.near(order)
    proj_found = send_terms(after(proj_sum.total().astype(BF), head_sum.sent), 1, order)
    held = head_sum.sent
    block_value = after(hidden_state, held) + shared_out + out_sum.total()
    scalars = jnp.stack(
        [
            jnp.sum(valid_rows * block_value * block_value),
            input_square[0],
            length_here.astype(F32),
        ]
    )
    small_grads = jnp.concatenate([router_grad_full, grad_gain_first, grad_gain_second])
    scalars = jnp.broadcast_to(scalars[:, None], (3, model_width))
    small_grads = jnp.concatenate([small_grads, scalars])
    small_grads = jnp.pad(small_grads, ((0, 128 - small_grads.shape[0]), (0, 0)))
    small_grads = jnp.swapaxes(small_grads.T.reshape(parts, groups, -1, 128), 0, 1)
    small_found = lax.all_to_all(small_grads, "expert", split_axis=0, concat_axis=0, tiled=True)
    order.close(head_near, routed_grads[1:])

    head_total = order.now(head_sum.total().astype(BF))
    head_found = send_terms(head_total, 1, order)
    routed_parts = early_parts
    for e in range(1, per_device):
        routed_parts = update_call(
            e, after(order.now(routed_grads[e]), head_total), routed_weight, routed_moment, routed_average, routed_parts, rate_routed * step_root
        )
    proj_found, shared_grad, small_found = after((proj_found, shared_grad, small_found), head_total)
    small_total = tree_sum([small_found[r] for r in range(groups)])
    small_found = lax.all_to_all(small_total, "dp", split_axis=0, concat_axis=0, tiled=True)
    small_grad = tree_sum([small_found[d] for d in range(parts)])
    shared_grad = sum_terms([shared_grad[d] for d in range(parts)])
    head_found = after(head_found, routed_parts[-1])
    attn_grad = jnp.concatenate([sum_terms(head_found), sum_terms(proj_found)])
    router_grad = small_grad[:, :routed_count]
    gain_grad = small_grad[:, routed_count : routed_count + 2].T
    row_sums = small_grad[0, routed_count + 2 : routed_count + 5]
    denominator = model_width * row_sums[2]
    masked_rms = jnp.stack(
        [jnp.sqrt(row_sums[0] / denominator), jnp.sqrt(row_sums[1] / denominator)]
    )
    attn_parts = update(
        attn_weight, attn_moment, attn_average, attn_grad, rate_attention * step_root
    )
    router_parts = update(
        router_weight, router_moment, router_average, router_grad, rate_router * step_root
    )
    shared_parts = update(
        shared_weight, shared_moment, shared_average, shared_grad, rate_shared * step_root
    )
    gain_parts = update(norm_gains, gain_moment, gain_average, gain_grad, rate_gains * step_root)
    return (
        block_value.astype(BF),
        input_grad,
        masked_rms,
        attn_parts[0],
        attn_parts[1],
        attn_parts[2],
        attn_parts[3],
        attn_parts[4],
        router_parts[0],
        router_parts[1],
        router_parts[2],
        router_parts[3],
        router_parts[4],
        shared_parts[0],
        shared_parts[1],
        shared_parts[2],
        shared_parts[3],
        shared_parts[4],
        routed_parts[0],
        routed_parts[1],
        routed_parts[2],
        routed_parts[3],
        routed_parts[4],
        gain_parts[0],
        gain_parts[1],
        gain_parts[2],
        gain_parts[3],
    )


def solution(mesh):
    placed = (
        P(("dp", "expert"), None),
        P(("dp", "expert"), None),
        P(("dp", "expert")),
        P(("dp", "expert"), None),
        P(None, ("dp", "expert"), None),
        P(None, ("dp", "expert"), None),
        P(None, ("dp", "expert"), None),
        P(("dp", "expert"), None),
        P(("dp", "expert"), None),
        P(("dp", "expert"), None),
        P(None, ("dp", "expert"), None),
        P(None, ("dp", "expert"), None),
        P(None, ("dp", "expert"), None),
        P("expert", None, "dp", None),
        P("expert", None, "dp", None),
        P("expert", None, "dp", None),
        P(None, ("dp", "expert")),
        P(None, ("dp", "expert")),
        P(None, ("dp", "expert")),
    )
    return jax.shard_map(
        local,
        mesh=mesh,
        in_specs=placed,
        out_specs=(
            P(("dp", "expert"), None),
            P(("dp", "expert"), None),
            P(),
            P(None, ("dp", "expert"), None),
            P(None, ("dp", "expert"), None),
            P(None, ("dp", "expert"), None),
            P(None, ("dp", "expert"), None),
            P(None, ("dp", "expert"), None),
            P(("dp", "expert"), None),
            P(("dp", "expert"), None),
            P(("dp", "expert"), None),
            P(("dp", "expert"), None),
            P(("dp", "expert"), None),
            P(None, ("dp", "expert"), None),
            P(None, ("dp", "expert"), None),
            P(None, ("dp", "expert"), None),
            P(None, ("dp", "expert"), None),
            P(None, ("dp", "expert"), None),
            P("expert", None, "dp", None),
            P("expert", None, "dp", None),
            P("expert", None, "dp", None),
            P("expert", None, "dp", None),
            P("expert", None, "dp", None),
            P(None, ("dp", "expert")),
            P(None, ("dp", "expert")),
            P(None, ("dp", "expert")),
            P(None, ("dp", "expert")),
        ),
        check_vma=False,
    )
```

```python
import functools
import math

import jax
import jax.numpy as jnp
from jax import lax
from jax.experimental import pallas as pl
from jax.experimental.layout import Layout, with_layout_constraint
from jax.experimental.pallas import tpu as pltpu
from jax.sharding import PartitionSpec as P

HEADS = 10
STEP = 3
BF = jnp.bfloat16
F32 = jnp.float32
BOTH = ("dp", "expert")


eps_norm = 1e-06
momentum_rate = 0.9
decay_rate = 0.0001
rate_attention = 0.01
rate_router = 0.03
rate_shared = 0.01
rate_routed = 0.04
rate_gains = 0.2
masked_score = -1e30
VMEM_LIMIT = 58 * 1024 * 1024


def silu_slope(pre_value):
    sigmoid_part = jax.nn.sigmoid(pre_value)
    return sigmoid_part * (1.0 + pre_value * (1.0 - sigmoid_part))


def update(weight, moment, average, gradient, step_rate):
    decayed = gradient + decay_rate * weight
    moment_new = momentum_rate * moment + decayed
    weight_new = weight - step_rate * (decayed + momentum_rate * moment_new)
    average_new = average + (weight_new - average) / (STEP + 1.0)
    return (gradient, weight_new, moment_new, average_new, weight_new.astype(BF))


def estimate(flops):
    return pl.CostEstimate(flops=flops, bytes_accessed=1, transcendentals=0)


def dot_nn(a,b): return lax.dot_general(a,b,(((1,),(0,)),((),())),preferred_element_type=F32)
def dot_nt(a,b): return lax.dot_general(a,b,(((1,),(1,)),((),())),preferred_element_type=F32)
def dot_tn(a,b): return lax.dot_general(a,b,(((0,),(0,)),((),())),preferred_element_type=F32)

def chunks(n,c): return [(s,min(c,n-s)) for s in range(0,n,c)]

def pair_columns(ff):
    return [(c0, cn, 2 * c0, 2 * c0 + cn) for c0, cn in chunks(ff, 256)]


def expert_pair_kernel(first, *refs):
    it = iter(refs)
    take = lambda count: [next(it) for _ in range(count)]
    eid_ref, choice_ref, slot_ref, router_ref, w_hbm = take(5)
    gate_ref = None if first else next(it)
    sources = [take(2), take(2)]
    prev = [] if first else [take(2), take(2)]
    outs = [take(2), take(2)]
    dg_ref, rows_out, dy_out, h_out, dab_out = take(5)
    gate_out = next(it) if first else None
    gu_v, down_v, tok, rows_v, dy_v, h_v, dab_v, ob, wsem, dsem, tsem, psem, osem, ssem = it
    n_dp = w_hbm.shape[0]
    width, ff = down_v.shape
    slab = width // n_dp
    seq = slot_ref.shape[1]
    cap = rows_v.shape[0] // 2
    tcopies = [[pltpu.make_async_copy(sources[j][q], tok.at[q, j], tsem.at[q, j]) for j in range(2)] for q in range(2)]
    wcopies = []
    for d in range(n_dp):
        own = pl.ds(d * slab, slab)
        for c, (c0, cn, g0, u0) in enumerate(pair_columns(ff)):
            for j, to in ((0, g0), (1, u0)):
                src = w_hbm.at[d, j, pl.ds(0, slab), pl.ds(c0, cn)]
                wcopies.append(pltpu.make_async_copy(src, gu_v.at[own, pl.ds(to, cn)], wsem.at[d, c, j]))
    dcopies = [
        pltpu.make_async_copy(w_hbm.at[d, 2, pl.ds(0, slab)], down_v.at[pl.ds(d * slab, slab)], dsem.at[d]) for d in range(n_dp)
    ]
    for copies in tcopies:
        for copy in copies:
            copy.start()
    lane = lax.broadcasted_iota(jnp.int32, (seq, 128), 1)
    sub = lax.broadcasted_iota(jnp.int32, (cap, seq), 0)
    eid = eid_ref[0]
    gcols, onehots = [], []
    for q in range(2):
        tcopies[q][0].wait()
        if q == 0:
            for copy in wcopies + dcopies:
                copy.start()
        sec = tok[q, 0]
        if first:
            logits = dot_nt(sec, router_ref[...])
            table = choice_ref[q, :, 0:1] == lane
            for k in range(1, choice_ref.shape[2]):
                table = table | (choice_ref[q, :, k : k + 1] == lane)
            masked = jnp.where(table, logits, masked_score)
            weight = jnp.where(table, jnp.exp(masked - jnp.max(masked, axis=1, keepdims=True)), 0.0)
            gates = weight / jnp.sum(weight, axis=1, keepdims=True)
            gate_out[q] = gates
        else:
            gates = gate_ref[q]
        gcol = jnp.sum(jnp.where(lane == eid, gates, 0.0), axis=1, keepdims=True)
        onehot = (slot_ref[q : q + 1, :] == sub).astype(F32).astype(BF)
        rows_v[q * cap : (q + 1) * cap, :] = dot_nn(onehot, sec).astype(BF)
        tcopies[q][1].wait()
        gated = (gcol * tok[q, 1].astype(F32)).astype(BF)
        dy_v[q * cap : (q + 1) * cap, :] = dot_nn(onehot, gated).astype(BF)
        gcols.append(gcol)
        onehots.append(onehot)
    pcopies = [pltpu.make_async_copy(prev[j][q], ob.at[q, j], psem.at[q, j]) for q in range(2) for j in range(2) if not first]
    for copy in pcopies:
        copy.start()
    saves = [pltpu.make_async_copy(rows_v, rows_out, ssem.at[0]), pltpu.make_async_copy(dy_v, dy_out, ssem.at[1])]
    for copy in saves:
        copy.start()
    for copy in wcopies + dcopies:
        copy.wait()
    gain_sum = jnp.zeros((2 * cap, 128), F32)
    for c0, cn, g0, u0 in pair_columns(ff):
        both = dot_nn(rows_v[...], gu_v[:, g0 : g0 + 2 * cn])
        a, b = both[:, :cn], both[:, cn:]
        dh = dot_nn(dy_v[...], down_v[:, c0 : c0 + cn])
        sigmoid = 0.5 * jnp.tanh(0.5 * a) + 0.5
        silu = a * sigmoid
        dsilu = dh * silu
        gain = dsilu * b
        for p0, pn in chunks(cn, 128):
            gain_sum = gain_sum + gain[:, p0 : p0 + pn]
        h_v[:, c0 : c0 + cn] = (silu * b).astype(BF)
        dab_v[:, g0 : g0 + cn] = (dh * b * (sigmoid + silu * (1.0 - sigmoid))).astype(BF)
        dab_v[:, u0 : u0 + cn] = dsilu.astype(BF)
    late = [pltpu.make_async_copy(h_v, h_out, ssem.at[2]), pltpu.make_async_copy(dab_v, dab_out, ssem.at[3])]
    for copy in late:
        copy.start()
    for copy in pcopies:
        copy.wait()
    sends = []
    gain_slot = jnp.sum(gain_sum, axis=1, keepdims=True)
    for q in range(2):
        spread = onehots[q].astype(F32) * gain_slot[q * cap : (q + 1) * cap]
        dg_ref[q] = jnp.broadcast_to(jnp.sum(spread, axis=0, keepdims=True), (8, seq))
    for n, (n0, nn) in enumerate(chunks(width, 512)):
        ns = slice(n0, n0 + nn)
        y = dot_nt(h_v[...], down_v[ns, :]).astype(BF)
        dr = dot_nt(dab_v[...], gu_v[ns, :]).astype(BF)
        for q in range(2):
            yt = dot_tn(onehots[q], y[q * cap : (q + 1) * cap])
            dt = dot_tn(onehots[q], dr[q * cap : (q + 1) * cap])
            yt = yt * gcols[q]
            if not first:
                yt = yt + ob[q, 0, :, ns].astype(F32)
                dt = dt + ob[q, 1, :, ns].astype(F32)
            ob[q, 0, :, ns] = yt.astype(BF)
            ob[q, 1, :, ns] = dt.astype(BF)
            for j in range(2):
                part = pl.ds(n0, nn)
                copy = pltpu.make_async_copy(ob.at[q, j, :, part], outs[j][q].at[:, part], osem.at[q, j, n])
                copy.start()
                sends.append(copy)
    for copy in saves + late + sends:
        copy.wait()


def expert_pair_call(eid, choice, slots, router_pad, w, secs, douts, prev, gates, cap):
    seq = slots.shape[1]
    width = secs[0].shape[1]
    n_dp, _, _, ff = w.shape
    parts = len(chunks(width, 512))
    flat = [] if prev is None else [v for pair in prev for v in pair]
    full = jax.ShapeDtypeStruct((seq, width), BF)
    shapes = [(2 * cap, width), (2 * cap, width), (2 * cap, ff), (2 * cap, 2 * ff)]
    dma = pltpu.SemaphoreType.DMA
    out = pl.pallas_call(
        functools.partial(expert_pair_kernel, prev is None),
        out_shape=[full] * 4
        + [jax.ShapeDtypeStruct((2, 8, seq), F32)]
        + [jax.ShapeDtypeStruct(shape, BF) for shape in shapes]
        + [jax.ShapeDtypeStruct((2, seq, 128), F32)] * (prev is None),
        in_specs=kernel_specs("svvva" + "v" * (prev is not None) + "a" * (4 + len(flat))),
        out_specs=kernel_specs("aaaavaaaa" + "v" * (prev is None)),
        scratch_shapes=[pltpu.VMEM((width, 2 * ff), BF), pltpu.VMEM((width, ff), BF), pltpu.VMEM((2, 2, seq, width), BF)]
        + [pltpu.VMEM(shape, BF) for shape in shapes]
        + [pltpu.VMEM((2, 2, seq, width), BF)]
        + [dma((n_dp, len(chunks(ff, 256)), 2)), dma((n_dp,)), dma((2, 2)), dma((2, 2)), dma((2, 2, parts)), dma((4,))],
        compiler_params=pltpu.CompilerParams(vmem_limit_bytes=VMEM_LIMIT),
        cost_estimate=estimate(18 * cap * width * ff),
        name="expert_pair",
    )(eid, choice, slots, router_pad, w, *([] if prev is None else [gates]), *secs, *douts, *flat)
    return (out[0:2], out[2:4]), out[4], out[5:9], out[9] if prev is None else gates


def weight_grad_kernel(count, *refs):
    saved = [refs[4 * i : 4 * i + 4] for i in range(count)]
    out_ref, rows_v, dy_v, h_v, dab_v, g_v, isem, osem = refs[4 * count :]
    width, ff = g_v.shape[1:]
    n_dp = out_ref.shape[0]
    slab = width // n_dp
    piece = rows_v.shape[0] // count
    cuts = chunks(width, 256)
    loads = {2: [], 3: [], 1: [[] for _ in cuts], 0: [[] for _ in cuts]}
    for i in range(count):
        own = pl.ds(i * piece, piece)
        for j, to in ((2, h_v), (3, dab_v)):
            loads[j].append(pltpu.make_async_copy(saved[i][j], to.at[own], isem.at[j, i, 0]))
        for j, to in ((1, dy_v), (0, rows_v)):
            for c, (c0, cn) in enumerate(cuts):
                source = saved[i][j].at[:, pl.ds(c0, cn)]
                loads[j][c].append(pltpu.make_async_copy(source, to.at[own, pl.ds(c0, cn)], isem.at[j, i, c]))
    for copy in loads[2] + sum(loads[1], []) + loads[3] + sum(loads[0], []):
        copy.start()
    stores = [
        [pltpu.make_async_copy(g_v.at[j, pl.ds(d * slab, slab)], out_ref.at[d, j], osem.at[j, d]) for d in range(n_dp)]
        for j in range(3)
    ]

    def send(j, c):
        done, before = sum(cuts[c]), cuts[c][0]
        for d in range(n_dp):
            if before < (d + 1) * slab <= done:
                stores[j][d].start()

    for copy in loads[2]:
        copy.wait()
    for c, (c0, cn) in enumerate(cuts):
        for copy in loads[1][c]:
            copy.wait()
        g_v[2, c0 : c0 + cn, :] = dot_tn(dy_v[:, c0 : c0 + cn], h_v[...]).astype(BF)
        send(2, c)
    for copy in loads[3]:
        copy.wait()
    for c, (c0, cn) in enumerate(cuts):
        for copy in loads[0][c]:
            copy.wait()
        both = dot_tn(rows_v[:, c0 : c0 + cn], dab_v[...])
        for f0, fn, g0, u0 in pair_columns(ff):
            g_v[0, c0 : c0 + cn, f0 : f0 + fn] = both[:, g0 : g0 + fn].astype(BF)
            g_v[1, c0 : c0 + cn, f0 : f0 + fn] = both[:, u0 : u0 + fn].astype(BF)
        send(0, c)
        send(1, c)
    for copy in stores[0] + stores[1] + stores[2]:
        copy.wait()


def weight_grad_call(saved, n_dp):
    count = len(saved)
    width, ff = saved[0][0].shape[1], saved[0][2].shape[1]
    rows = count * saved[0][0].shape[0]
    dma = pltpu.SemaphoreType.DMA
    return pl.pallas_call(
        functools.partial(weight_grad_kernel, count),
        out_shape=jax.ShapeDtypeStruct((n_dp, 3, width // n_dp, ff), BF),
        in_specs=kernel_specs("a" * (4 * count)),
        out_specs=pl.BlockSpec(memory_space=pl.ANY),
        scratch_shapes=[pltpu.VMEM((rows, n), BF) for n in (width, width, ff, 2 * ff)]
        + [pltpu.VMEM((3, width, ff), BF), dma((4, count, len(chunks(width, 256)))), dma((3, n_dp))],
        compiler_params=pltpu.CompilerParams(vmem_limit_bytes=VMEM_LIMIT),
        cost_estimate=estimate(6 * rows * width * ff),
        name="expert_weights",
    )(*[v for part in saved for v in part])


def rotated(values, cosine, sine):
    return values * cosine + pltpu.roll(values, values.shape[1] // 2, 1) * sine


def head_block(h):
    return pl.ds(pl.multiple_of(h * 128, 128), 128)


def masked_scores(query, key, start, length, scale):
    scores = dot_nt(query, key) * scale
    at = lax.broadcasted_iota(jnp.int32, scores.shape, 0) + start
    to = lax.broadcasted_iota(jnp.int32, scores.shape, 1)
    return jnp.where((to <= at) & (to < length), scores, masked_score)


def attention_kernel(
    scale, tok_ref, gain_ref, cos_ref, sin_ref, len_ref, wq, wk, wv, wo,
    first_ref, q_ref, k_ref, v_ref, ctx_ref, lse_ref, hidden_ref, second_ref, w_v, sem,
):
    copies = [pltpu.make_async_copy(w, w_v.at[j], sem.at[j]) for j, w in enumerate((wq, wk, wv, wo))]
    for copy in copies:
        copy.start()
    seq, width = tok_ref.shape
    length = len_ref[0]
    x = tok_ref[...].astype(F32)
    inverse = lax.rsqrt(jnp.mean(x * x, axis=1, keepdims=True) + eps_norm)
    first_ref[...] = (x * inverse * gain_ref[0:1, :]).astype(BF)
    for j, out_ref in enumerate((q_ref, k_ref, v_ref)):
        copies[j].wait()
        for c0, cn in chunks(width, 256):
            lin = dot_nn(first_ref[...], w_v[j, :, c0 : c0 + cn])
            for h0, hn in chunks(cn, 128):
                part = lin[:, h0 : h0 + hn]
                if j < 2:
                    part = rotated(part, cos_ref[...], sin_ref[...])
                out_ref[:, c0 + h0 : c0 + h0 + hn] = part.astype(BF)
    lane = lax.broadcasted_iota(jnp.int32, (seq, 128), 1)
    block = 256

    def heads(g, carry):
        for u in range(2):
            h = g * 2 + u
            hs = head_block(h)
            logs = []
            for start in range(0, seq, block):
                end = start + block
                masked = masked_scores(q_ref[start:end, hs], k_ref[:end, hs], start, length, scale)
                peak = jnp.max(masked, axis=1, keepdims=True)
                weight = jnp.exp(masked - peak)
                total = jnp.sum(weight, axis=1, keepdims=True)
                probs = (weight / total).astype(BF)
                ctx_ref[start:end, hs] = dot_nn(probs, v_ref[:end, hs]).astype(BF)
                logs.append(peak + jnp.log(total))
            log = jnp.concatenate(logs, axis=0)
            lse_ref[...] = jnp.where(lane == h, log, lse_ref[...])
        return carry

    lse_ref[...] = jnp.zeros_like(lse_ref)
    lax.fori_loop(0, width // 256, heads, 0)
    copies[3].wait()
    squares = jnp.zeros((seq, 1), F32)
    for c0, cn in chunks(width, 256):
        cs = slice(c0, c0 + cn)
        hidden = tok_ref[:, cs].astype(F32) + dot_nn(ctx_ref[...], w_v[3, :, cs])
        hidden_ref[:, cs] = hidden
        squares = squares + jnp.sum(hidden * hidden, axis=1, keepdims=True)
    inverse = lax.rsqrt(squares / width + eps_norm)
    second_ref[...] = (hidden_ref[...] * inverse * gain_ref[1:2, :]).astype(BF)


def kernel_specs(places):
    kinds = {"v": pltpu.VMEM, "s": pltpu.SMEM, "a": pl.ANY}
    return [pl.BlockSpec(memory_space=kinds[p]) for p in places]


def attention_call(tokens, gains, cosine, sine, lengths, weights, scale):
    seq, width = tokens.shape
    half = jax.ShapeDtypeStruct((seq, width), BF)
    return pl.pallas_call(
        functools.partial(attention_kernel, scale),
        out_shape=[half] * 5
        + [jax.ShapeDtypeStruct((seq, 128), F32), jax.ShapeDtypeStruct((seq, width), F32), half],
        in_specs=kernel_specs("vvvvsaaaa"),
        out_specs=kernel_specs("vvvvvvvv"),
        scratch_shapes=[pltpu.VMEM((4, width, width), BF), pltpu.SemaphoreType.DMA((4,))],
        compiler_params=pltpu.CompilerParams(vmem_limit_bytes=VMEM_LIMIT),
        cost_estimate=estimate(0),
        name="attention_forward",
    )(tokens, gains, cosine, sine, lengths, *weights)


def store_pieces(even_ref, odd_ref, slot, rows_ref, grad_ref):
    count, _, piece, _ = even_ref.shape
    for part, out_ref in enumerate((even_ref, odd_ref)):
        for j in range(count):
            at = (part * count + j) * piece
            out_ref[j, slot] = dot_nn(rows_ref[at : at + piece, :], grad_ref[...]).astype(BF)


def piece_shape(number, width, out_width):
    count = lax.axis_size("expert") // 2
    return jax.ShapeDtypeStruct((count, number, width // (2 * count), out_width), BF)


def hidden_back_kernel(
    dn_ref, logit_ref, router_ref, base_ref, core_ref, side_x_ref, side_y_ref, hidden_ref, dout_ref, gain_ref, ctx_ref, wo, dhid_ref, dctx_ref, even_ref, odd_ref, gain_out, w_v, dattn_v, sem
):
    copy = pltpu.make_async_copy(wo, w_v, sem)
    copy.start()
    seq, width = hidden_ref.shape
    hidden = hidden_ref[...]
    inverse = lax.rsqrt(jnp.mean(hidden * hidden, axis=1, keepdims=True) + eps_norm)
    hat = hidden * inverse
    logits = logit_ref[...]
    high = logits.astype(BF)
    rest = logits - high.astype(F32)
    low = rest.astype(BF)
    least = (rest - low.astype(F32)).astype(BF)
    routers = sum(dot_nn(part, router_ref[...]) for part in (least, low, high))
    dn = dn_ref[...] + routers + base_ref[...].astype(F32) + core_ref[...].astype(F32) + side_x_ref[...].astype(F32) + side_y_ref[...].astype(F32)
    gain_out[...] = jnp.sum(dn * hat, axis=0, keepdims=True)
    scaled = dn * gain_ref[1:2, :]
    mean = jnp.mean(scaled * hat, axis=1, keepdims=True)
    dhid = dout_ref[...].astype(F32) + inverse * (scaled - hat * mean)
    dhid_ref[...] = dhid
    dattn_v[...] = dhid.astype(BF)
    store_pieces(even_ref, odd_ref, 0, ctx_ref, dattn_v)
    copy.wait()
    for c0, cn in chunks(width, 256):
        dctx_ref[:, c0 : c0 + cn] = dot_nt(dattn_v[...], w_v[c0 : c0 + cn, :]).astype(BF)


def hidden_back_call(dn, logits, router, base, core, sides, hidden, dout, gains, ctx_rel, wo):
    seq, width = hidden.shape
    half = jax.ShapeDtypeStruct((seq, width), BF)
    part = piece_shape(1, width, width)
    return pl.pallas_call(
        hidden_back_kernel,
        out_shape=[jax.ShapeDtypeStruct((seq, width), F32), half, part, part, jax.ShapeDtypeStruct((1, width), F32)],
        in_specs=kernel_specs("vvvvvvvvvvva"),
        out_specs=kernel_specs("vvvvv"),
        scratch_shapes=[pltpu.VMEM((width, width), BF), pltpu.VMEM((seq, width), BF), pltpu.SemaphoreType.DMA],
        compiler_params=pltpu.CompilerParams(vmem_limit_bytes=VMEM_LIMIT),
        cost_estimate=estimate(15 * seq * width * width),
        name="hidden_backward",
    )(dn, logits, router, base, core, *sides, hidden, dout, gains, ctx_rel, wo)


def heads_back_kernel(
    scale, q_ref, k_ref, v_ref, dctx_ref, lse_ref, cos_ref, sin_ref, first_ref, len_ref,
    dq_ref, dk_ref, dv_ref, even_ref, odd_ref, even_v, odd_v, sem,
):
    seq, width = q_ref.shape
    length = len_ref[0]
    lane = lax.broadcasted_iota(jnp.int32, (seq, 128), 1)
    block = 256

    def heads(g, carry):
        for u in range(2):
            h = g * 2 + u
            hs = head_block(h)
            log = jnp.sum(jnp.where(lane == h, lse_ref[...], 0.0), axis=1, keepdims=True)
            key_parts, value_parts = [], []
            for start in range(0, seq, block):
                end = start + block
                rows = slice(start, end)
                masked = masked_scores(q_ref[rows, hs], k_ref[:end, hs], start, length, scale)
                probs = jnp.exp(masked - log[rows])
                dprobs = dot_nt(dctx_ref[rows, hs], v_ref[:end, hs])
                delta = jnp.sum(probs * dprobs, axis=1, keepdims=True)
                dscores = (probs * (dprobs - delta)).astype(BF)
                dq = dot_nn(dscores, k_ref[:end, hs]) * scale
                dq_ref[rows, hs] = rotated(dq, cos_ref[rows, :], -sin_ref[rows, :]).astype(BF)
                key_parts.append(dot_tn(dscores, q_ref[rows, hs]))
                value_parts.append(dot_tn(probs.astype(BF), dctx_ref[rows, hs]))
            for start in range(0, seq, block):
                rows = slice(start, start + block)
                dk = sum(p[rows] for p in key_parts if p.shape[0] > start) * scale
                dv = sum(p[rows] for p in value_parts if p.shape[0] > start)
                dk_ref[rows, hs] = rotated(dk, cos_ref[rows, :], -sin_ref[rows, :]).astype(BF)
                dv_ref[rows, hs] = dv.astype(BF)
        return carry

    lax.fori_loop(0, width // 256, heads, 0)
    copies = []
    for j, grad_ref in ((2, dv_ref), (0, dq_ref), (1, dk_ref)):
        store_pieces(even_v, odd_v, j, first_ref, grad_ref)
        for part, (held, out_ref) in enumerate(((even_v, even_ref), (odd_v, odd_ref))):
            copies.append(pltpu.make_async_copy(held.at[:, j], out_ref.at[:, j], sem.at[j, part]))
            copies[-1].start()
    for copy in copies:
        copy.wait()


def heads_back_call(q, k, v, dctx, lse, cosine, sine, first_rel, lengths, scale):
    seq, width = q.shape
    half = jax.ShapeDtypeStruct((seq, width), BF)
    wide = piece_shape(3, width, width)
    return pl.pallas_call(
        functools.partial(heads_back_kernel, scale),
        out_shape=[half] * 3 + [wide] * 2,
        in_specs=kernel_specs("vvvvvvvvs"),
        out_specs=kernel_specs("vvvaa"),
        scratch_shapes=[pltpu.VMEM(wide.shape, BF)] * 2 + [pltpu.SemaphoreType.DMA((3, 2))],
        compiler_params=pltpu.CompilerParams(vmem_limit_bytes=VMEM_LIMIT),
        cost_estimate=estimate(26 * seq * width * width),
        name="heads_backward",
    )(q, k, v, dctx, lse, cosine, sine, first_rel, lengths)


def input_back_kernel(
    dq_ref, dk_ref, dv_ref, tok_ref, gain_ref, dhid_ref, len_ref, wq, wk, wv, out_ref, gain_out, sum_ref, w_v, dn_v, sem
):
    copies = [pltpu.make_async_copy(w, w_v.at[j], sem.at[j]) for j, w in enumerate((wq, wk, wv))]
    for copy in copies:
        copy.start()
    seq, width = tok_ref.shape
    x = tok_ref[...].astype(F32)
    inverse = lax.rsqrt(jnp.mean(x * x, axis=1, keepdims=True) + eps_norm)
    for copy in copies:
        copy.wait()
    for c0, cn in chunks(width, 256):
        cs = slice(c0, c0 + cn)
        dn_v[:, cs] = (
            dot_nt(dq_ref[...], w_v[0, cs, :]) + dot_nt(dk_ref[...], w_v[1, cs, :]) + dot_nt(dv_ref[...], w_v[2, cs, :])
        )
    hat = tok_ref[...].astype(F32) * inverse
    dn = dn_v[...]
    gain_out[...] = jnp.sum(dn * hat, axis=0, keepdims=True)
    scaled = dn * gain_ref[0:1, :]
    mean = jnp.mean(scaled * hat, axis=1, keepdims=True)
    result = dhid_ref[...] + inverse * (scaled - hat * mean)
    out_ref[...] = result
    valid = lax.broadcasted_iota(jnp.int32, result.shape, 0) < len_ref[0]
    sum_ref[0] = jnp.sum(jnp.where(valid, result * result, 0.0))


def input_back_call(dq, dk, dv, tokens, gains, dhidden, lengths, weights):
    seq, width = tokens.shape
    return pl.pallas_call(
        input_back_kernel,
        out_shape=[
            jax.ShapeDtypeStruct((seq, width), F32),
            jax.ShapeDtypeStruct((1, width), F32),
            jax.ShapeDtypeStruct((1,), F32),
        ],
        in_specs=kernel_specs("vvvvvvsaaa"),
        out_specs=kernel_specs("vvs"),
        scratch_shapes=[pltpu.VMEM((3, width, width), BF), pltpu.VMEM((seq, width), F32), pltpu.SemaphoreType.DMA((3,))],
        compiler_params=pltpu.CompilerParams(vmem_limit_bytes=VMEM_LIMIT),
        cost_estimate=estimate(18 * seq * width * width),
        name="input_backward",
    )(dq, dk, dv, tokens, gains, dhidden, lengths, *weights)


def shared_kernel(
    second_ref, second_rel_ref, dout_ref, dout_rel_ref, wg, wu, wd, out_ref, dn_ref, even_ref, odd_ref, w_v, h_v, da_v, db_v, sem
):
    copies = [pltpu.make_async_copy(w, w_v.at[j], sem.at[j]) for j, w in enumerate((wg, wu, wd))]
    for copy in copies:
        copy.start()
    for copy in copies:
        copy.wait()
    width, ff = w_v.shape[1:]
    for c0, cn in chunks(ff, 256):
        cs = slice(c0, c0 + cn)
        gate = dot_nn(second_ref[...], w_v[0, :, cs])
        up = dot_nn(second_ref[...], w_v[1, :, cs])
        back = dot_nn(dout_ref[...], w_v[2, :, cs])
        sigmoid = 1.0 / (1.0 + jnp.exp(-gate))
        silu = gate * sigmoid
        h_v[:, cs] = (silu * up).astype(BF)
        da_v[:, cs] = (back * up * (sigmoid * (1.0 + gate * (1.0 - sigmoid)))).astype(BF)
        db_v[:, cs] = (back * silu).astype(BF)
    for c0, cn in chunks(width, 256):
        cs = slice(c0, c0 + cn)
        out_ref[:, cs] = dot_nt(h_v[...], w_v[2, cs, :])
        dn_ref[:, cs] = dot_nt(da_v[...], w_v[0, cs, :]) + dot_nt(db_v[...], w_v[1, cs, :])
    store_pieces(even_ref, odd_ref, 0, second_rel_ref, da_v)
    store_pieces(even_ref, odd_ref, 1, second_rel_ref, db_v)
    store_pieces(even_ref, odd_ref, 2, dout_rel_ref, h_v)


def shared_call(second, second_rel, dout, dout_rel, weights):
    seq, width = second.shape
    ff = weights[0].shape[1]
    full = jax.ShapeDtypeStruct((seq, width), F32)
    part = piece_shape(3, width, ff)
    return pl.pallas_call(
        shared_kernel,
        out_shape=[full, full, part, part],
        in_specs=kernel_specs("vvvvaaa"),
        out_specs=kernel_specs("vvvv"),
        scratch_shapes=[pltpu.VMEM((3, width, ff), BF)]
        + [pltpu.VMEM((seq, ff), BF)] * 3
        + [pltpu.SemaphoreType.DMA((3,))],
        compiler_params=pltpu.CompilerParams(vmem_limit_bytes=VMEM_LIMIT),
        cost_estimate=estimate(0),
        name="shared_expert",
    )(second, second_rel, dout, dout_rel, *weights)


def update_kernel(rate, grad_ref, w_ref, m_ref, a_ref, *refs):
    grad_out, new_out, moment_out, average_out, copy_out = refs[-5:]
    parts = update(w_ref[0, 0], m_ref[0, 0], a_ref[0, 0], grad_ref[0].astype(F32), rate)
    for target, part in zip((grad_out, new_out, moment_out, average_out, copy_out), parts):
        target[0, 0] = part


def update_call(e, grad, weight, moment, average, done, rate):
    experts, kinds, rows, ff = weight.shape
    cuts = 2 if rows % 32 == 0 else 1
    full = pl.BlockSpec((1, 1, rows // cuts, ff), lambda j, i: (e, j, i, 0))
    return pl.pallas_call(
        functools.partial(update_kernel, rate),
        grid=(kinds, cuts),
        out_shape=[jax.ShapeDtypeStruct(weight.shape, F32)] * 4 + [jax.ShapeDtypeStruct(weight.shape, BF)],
        in_specs=[pl.BlockSpec((1, rows // cuts, ff), lambda j, i: (j, i, 0))]
        + [full] * 3
        + [pl.BlockSpec(memory_space=pl.ANY)] * len(done),
        out_specs=[full] * 5,
        input_output_aliases={4 + i: i for i in range(len(done))},
        compiler_params=pltpu.CompilerParams(vmem_limit_bytes=VMEM_LIMIT),
        cost_estimate=estimate(10_000_000_000),
        name="routed_update",
    )(grad, weight, moment, average, *done)


def permute(values, pairs):
    return lax.ppermute(values, "expert", pairs)


def pairs_of(mask, count):
    return [(i, i ^ mask) for i in range(count)]


def mixed_pairs(even_mask, odd_mask, count):
    return [(i, i ^ (odd_mask if i % 2 else even_mask)) for i in range(count)]


def after(values, *others):
    return lax.optimization_barrier((values, others))[0] if others else values


class Order:
    def __init__(self):
        self.last = ()

    def now(self, values):
        return after(values, *self.last)

    def close(self, *values):
        self.last = values


def send_dp(values, k):
    return lax.ppermute(values, "dp", [(i, i ^ k) for i in range(lax.axis_size("dp"))])


def stack_kernel(at_ref, *refs):
    count = (len(refs) - 2)
    copies = [
        pltpu.make_async_copy(refs[k], refs[count].at[at_ref[0] ^ k], refs[-1].at[k]) for k in range(count)
    ]
    for copy in copies:
        copy.start()
    for copy in copies:
        copy.wait()


def stack_dp(pieces):
    count = len(pieces)
    return pl.pallas_call(
        stack_kernel,
        out_shape=jax.ShapeDtypeStruct((count,) + pieces[0].shape, BF),
        in_specs=kernel_specs("s" + "a" * count),
        out_specs=pl.BlockSpec(memory_space=pltpu.VMEM),
        scratch_shapes=[pltpu.SemaphoreType.DMA((count,))],
        compiler_params=pltpu.CompilerParams(vmem_limit_bytes=VMEM_LIMIT),
        cost_estimate=estimate(0),
        name="stack_dp",
    )(lax.axis_index("dp")[None], *pieces)


def send_terms(terms, axis, order):
    here = lax.axis_index("dp")
    found = []
    for k in range(lax.axis_size("dp")):
        term = lax.dynamic_index_in_dim(terms, here ^ k, axis=axis, keepdims=False)
        found.append(send_dp(order.now(term), k) if k else order.now(term))
    return found


def sum_terms(found):
    return tree_sum([term.astype(F32) for term in found])


def tree_sum(terms):
    while len(terms) > 1:
        terms = [a + b for a, b in zip(terms[::2], terms[1::2])]
    return terms[0]


def permute_near(values):
    count = lax.axis_size("expert")
    return permute(values, pairs_of(2, count)), permute(values, pairs_of(4, count))


def permute_far(values):
    return permute(values, mixed_pairs(4, 2, lax.axis_size("expert")))


def permute_core(values):
    return permute(values, pairs_of(1, lax.axis_size("expert")))


def row_major(values):
    return with_layout_constraint(values, Layout(tuple(range(values.ndim))))


class PlaneSum:
    def __init__(self, even, odd, is_core0):
        self.even, self.odd, self.is_core0, self.kind = even, odd, is_core0, getattr(even, "dtype", BF)
        self.other = [None] * len(even)

    def take(self, j):
        return self.even[j].astype(F32) + self.other[j].astype(F32)

    def core(self, order):
        self.other = row_major(permute_core(row_major(order.now(self.odd))))
        return self.other

    def core_of(self, j, order):
        self.other[j] = permute_core(order.now(self.odd[j]))
        return self.other[j]

    def far(self, order):
        self.third = permute_far(order.now(self.take(3).astype(self.kind)))
        return self.third

    def near(self, order):
        count = lax.axis_size("expert")
        if not isinstance(self.other, list):
            self.other = order.now(self.other)
        third = self.third.astype(F32)
        to_x = (self.take(1) + jnp.where(self.is_core0, third, 0.0)).astype(self.kind)
        to_y = (self.take(2) + jnp.where(self.is_core0, 0.0, third)).astype(self.kind)
        to_x, to_y = self.sent = order.now((to_x, to_y))
        self.sides = (permute(to_x, pairs_of(2, count)), permute(to_y, pairs_of(4, count)))
        return self.sides

    def total(self):
        return self.take(0) + self.sides[0].astype(F32) + self.sides[1].astype(F32)


def place_kernel(cuts, at_ref, *refs):
    sem = refs[-1]
    outs = refs[-1 - len(cuts) : -1]
    count = sem.shape[0]
    copies = []
    for i, (group, kind, column) in enumerate(cuts):
        for r in range(count):
            source = refs[group * count + r].at[:, kind, :, pl.ds(column, outs[i].shape[3])]
            copies.append(pltpu.make_async_copy(source, outs[i].at[:, at_ref[0] ^ r], sem.at[r, i]))
    for copy in copies:
        copy.start()
    for copy in copies:
        copy.wait()


def place_rows(groups, me, cuts):
    count = len(groups[0])
    parts, _, rows, _ = groups[0][0].shape
    shapes = [(parts, count, rows, cut[3]) for cut in cuts]
    out = pl.pallas_call(
        functools.partial(place_kernel, [cut[:3] for cut in cuts]),
        out_shape=[jax.ShapeDtypeStruct(shape, BF) for shape in shapes],
        in_specs=kernel_specs("s" + "a" * (count * len(groups))),
        out_specs=kernel_specs("v" * len(cuts)),
        scratch_shapes=[pltpu.SemaphoreType.DMA((count, len(cuts)))],
        compiler_params=pltpu.CompilerParams(vmem_limit_bytes=VMEM_LIMIT),
        cost_estimate=estimate(0),
        name="place_rows",
    )(me[None], *[piece for group in groups for piece in group])
    return [v.reshape(parts * count * rows, v.shape[3]) for v in out]


def piece_sum(even, odd, is_core0):
    parts = lax.axis_size("dp")
    cut = even.shape[:2] + (parts, even.shape[2] // parts, even.shape[3])
    return PlaneSum(even.reshape(cut), odd.reshape(cut), is_core0)


def relative_rows(me, width):
    parts, count = lax.axis_size("dp"), lax.axis_size("expert")
    rows = width // (parts * count)
    far = jnp.concatenate([jnp.arange(0, count, 2, dtype=jnp.int32), jnp.arange(1, count, 2, dtype=jnp.int32)])
    owner = jnp.arange(parts, dtype=jnp.int32)[None, :] * count + (me ^ far)[:, None]
    return (owner[:, :, None] * rows + jnp.arange(rows, dtype=jnp.int32)).reshape(width)


def local(
    tokens,
    cotangent,
    lengths,
    choices,
    attn_weight,
    attn_moment,
    attn_average,
    router_weight,
    router_moment,
    router_average,
    shared_weight,
    shared_moment,
    shared_average,
    routed_weight,
    routed_moment,
    routed_average,
    norm_gains,
    gain_moment,
    gain_average,
):
    seq_len, model_width = tokens.shape
    topk_count = choices.shape[1]
    head_dim = model_width // HEADS
    groups = lax.axis_size("expert")
    routed_count = routed_weight.shape[0] * groups
    capacity = (seq_len * topk_count * 8 // (7 * routed_count) + 7) // 8 * 8
    total_tokens = seq_len * groups * lax.axis_size("dp")
    step_root = 1.0 / math.sqrt(total_tokens)
    score_scale = 1.0 / math.sqrt(head_dim)
    me = lax.axis_index("expert")
    is_core0 = lax.rem(me, 2) == 0
    relative = me ^ jnp.arange(groups, dtype=jnp.int32)
    per_device = routed_weight.shape[0]
    positions = jnp.arange(seq_len, dtype=jnp.int32)
    length_here = lengths[0]
    valid_rows = (positions < length_here).astype(F32)[:, None]
    grad_out = cotangent.astype(F32) * valid_rows
    grad_out16 = grad_out.astype(BF)

    order = Order()
    select = lambda pair: jnp.where(is_core0, *pair)
    small = jnp.concatenate([router_weight, norm_gains.T], axis=1)
    small = jnp.pad(small[None], ((0, 1), (0, 0), (0, 128 - small.shape[1])))
    parts = lax.axis_size("dp")
    front_own = jnp.concatenate([attn_weight[:2], small], axis=2).astype(BF)
    back_own = attn_weight[2:].astype(BF)
    shared_own = shared_weight.astype(BF)
    front_parts = [front_own] + [send_dp(front_own, k) for k in range(1, parts)]
    grad_near = permute_near(grad_out16)
    order.close(front_parts, grad_near)
    back_parts = [back_own] + [send_dp(order.now(back_own), k) for k in range(1, parts)]
    front = stack_dp(front_parts)

    choice_own = jnp.pad(choices.T.astype(BF), ((0, 16 - topk_count), (0, 0)))
    choice_all = lax.all_to_all(
        jnp.broadcast_to(choice_own, (groups,) + choice_own.shape), "expert", split_axis=0, concat_axis=0, tiled=True
    )
    front_near = permute_near(order.now(front))
    order.close(front_near, back_parts)
    back = stack_dp(back_parts)
    shared_cut = lax.all_to_all(
        order.now(jnp.broadcast_to(shared_own, (parts,) + shared_own.shape)), "dp", split_axis=0, concat_axis=0, tiled=True
    )

    front_held = list(order.now((front, *front_near)))
    back_near = permute_near(order.now(back))
    front_far = permute_far(order.now(select(front_near)))
    front_core = [permute_core(order.now(p)) for p in (front, *front_near)]
    order.close(back_near, front_far, front_core, shared_cut)
    routed_low = [routed_weight[e].astype(BF) for e in range(per_device)]
    routed16 = [lax.all_gather(low, "dp", axis=0, tiled=False) for low in order.now(routed_low)]

    back_held = list(order.now((back, *back_near)))
    back_far = permute_far(order.now(select(back_near)))
    back_core = [permute_core(order.now(p)) for p in (back, *back_near)]
    front_core.append(permute_core(order.now(front_far)))
    order.close(back_far, back_core, front_core)
    back_core.append(permute_core(order.now(back_far)))
    shared_near = permute_near(order.now(shared_cut))
    grad_core = [permute_core(order.now(p)) for p in (grad_out16, *grad_near)]
    front = [p for pair in zip((*front_held, front_far), front_core) for p in pair]
    back = [p for pair in zip((*back_held, back_far), back_core) for p in pair]
    cuts = [(group, kind, 0, model_width) for group in range(2) for kind in range(2)]
    *attn16, small_all = place_rows([front, back], me, cuts + [(0, 0, model_width, 128)])
    small_all = small_all.T
    router16t = small_all[:routed_count]
    gains16 = small_all[routed_count : routed_count + 2]
    choice_all = jnp.take(choice_all[:, :topk_count], relative, axis=0).astype(jnp.int32)
    own_experts = me * per_device + jnp.arange(per_device, dtype=jnp.int32)
    hits = jnp.any(choice_all[:, None] == own_experts[None, :, None, None], axis=2)
    before = (positions[:, None] < positions[None, :]).astype(BF)
    ranks = jnp.einsum("set,tu->seu", hits.astype(BF), before, preferred_element_type=F32).astype(jnp.int32)
    slot_all = jnp.where(hits, ranks, -1)
    choice_all = jnp.transpose(choice_all, (0, 2, 1))
    gain_first = gains16[0].astype(F32)
    gain_second = gains16[1].astype(F32)
    half_dim = head_dim // 2
    frequency = 10000.0 ** (-jnp.arange(half_dim, dtype=F32) / half_dim)
    angles = positions.astype(F32)[:, None] * frequency[None, :]
    cosine = jnp.concatenate([jnp.cos(angles), jnp.cos(angles)], axis=1)
    sine = jnp.concatenate([-jnp.sin(angles), jnp.sin(angles)], axis=1)
    gains = jnp.stack([gain_first, gain_second])
    first16, query16, key16, value16, context16, log_totals, hidden_state, second16 = attention_call(
        tokens, gains, cosine, sine, lengths, attn16, score_scale
    )
    order.close(second16, shared_near, grad_core)

    router_pad = jnp.pad(router16t, ((0, 128 - routed_count), (0, 0)))
    shared_sent = order.now(select(shared_near))
    shared_far = permute_far(shared_sent)
    second_near = permute_near(after(second16, shared_sent))
    second_core = [permute_core(second16)]
    grads_even = [grad_out16, *grad_near]
    seconds_even = [second16, *second_near]

    def pair(e, j, prev, gates):
        return expert_pair_call(
            own_experts[e][None],
            choice_all[2 * j : 2 * j + 2],
            slot_all[2 * j : 2 * j + 2, e],
            router_pad,
            routed16[e],
            order.now((seconds_even[j], second_core[j])),
            (grads_even[j], grad_core[j]),
            prev,
            gates,
            capacity,
        )

    shared_core = [permute_core(order.now(p)) for p in (shared_cut, *shared_near)]
    sort_rows = (jnp.arange(model_width, dtype=jnp.int32)[None, :] == relative_rows(me, model_width)[:, None]).astype(BF)
    sort = lambda values: lax.dot_general(
        sort_rows, values, (((1,), (1,)), ((), ())), preferred_element_type=F32
    ).astype(BF)
    out_rel, second_rel, first_rel, context_rel = [
        sort(order.now(v)) for v in (grad_out16, second16, first16, context16)
    ]
    order.close(second_core, shared_far, shared_core, out_rel, second_rel, first_rel, context_rel)
    shared_core.append(permute_core(order.now(shared_far)))
    shared_all = [p for both in zip((shared_cut, *shared_near, shared_far), shared_core) for p in both]
    shared16 = place_rows([shared_all], me, [(0, j, 0, shared_weight.shape[2]) for j in range(3)])
    shared_out, shared_back, shared_even, shared_odd = shared_call(
        order.now(second16), second_rel, grad_out16, out_rel, shared16
    )
    order.close(shared_back, second_near)

    results = [[None] * 4 for _ in range(per_device)]
    second_far = permute_far(order.now(select(second_near)))
    second_core += [permute_core(order.now(p)) for p in second_near]
    grad_far = permute_far(order.now(select(grad_near)))
    grads_even.append(grad_far)
    shared_sum = piece_sum(shared_even, shared_odd, is_core0)
    shared_core = shared_sum.core(order)
    results[0][0] = pair(0, 0, None, None)
    order.close(second_core, results[0][0][1], second_far, shared_core, grad_far)
    grad_core.append(permute_core(order.now(grad_far)))
    seconds_even.append(second_far)
    second_core.append(permute_core(order.now(second_far)))
    shared_far = shared_sum.far(order)
    results[0][1] = pair(0, 1, None, None)
    order.close(second_core[3], grad_core[3], results[0][1][1], shared_far)
    shared_near = shared_sum.near(order)
    results[0][2] = pair(0, 2, None, None)
    order.close(results[0][2][1])
    results[0][3] = pair(0, 3, None, None)
    order.close(results[0][3][1], shared_near)
    routed_grads = []

    def finish_expert(e):
        grads = weight_grad_call(order.now([result[2] for result in results[e]]), parts)
        routed_grads.append(lax.psum_scatter(grads, "dp", scatter_dimension=0, tiled=False))
        return grads

    order.close(finish_expert(0))
    for e in range(1, per_device):
        back_sum = PlaneSum([None] * 4, [None] * 4, is_core0) if e == per_device - 1 else None
        out_sum = PlaneSum([None] * 4, [None] * 4, is_core0) if e == per_device - 1 else None

        def step(j):
            results[e][j] = pair(e, j, results[e - 1][j][0], results[e - 1][j][3])
            if back_sum is not None:
                for total, found in zip((out_sum, back_sum), results[e][j][0]):
                    total.even[j], total.odd[j] = found

        step(3)
        order.close(results[e][3][1])
        waits = []
        if back_sum is not None:
            waits += [back_sum.core_of(3, order), out_sum.core_of(3, order)]
        step(1)
        order.close(results[e][1][1], waits)
        if back_sum is not None:
            waits = [back_sum.far(order), back_sum.core_of(1, order), out_sum.core_of(1, order)]
        step(2)
        order.close(results[e][2][1], waits)
        if back_sum is not None:
            order.close(back_sum.core_of(2, order))
            sides = back_sum.near(order)
            waits = [out_sum.core_of(2, order)]
        step(0)
        if back_sum is not None:
            gate_grads = [jnp.concatenate([result[1][:, 0] for result in row]) for row in results]
            gate_sent = jnp.take(jnp.stack(gate_grads, axis=1), relative, axis=0)
            gate_back = lax.all_to_all(gate_sent, "expert", split_axis=0, concat_axis=0, tiled=True)
            waits += [sides, gate_back]
        order.close(results[e][0][1], waits)
        if back_sum is not None:
            waits = [back_sum.core_of(0, order), out_sum.far(order), out_sum.core_of(0, order)]
        order.close(finish_expert(e), waits)
    grad_gate = order.now(gate_back).reshape(routed_count, seq_len).T
    logits = lax.dot_general(second16, router16t, (((1,), (1,)), ((), ())), preferred_element_type=F32)
    table = jnp.any(choices[:, :, None] == jnp.arange(routed_count, dtype=jnp.int32)[None, None, :], axis=1)
    chosen = jnp.where(table, logits, masked_score)
    chosen_exp = jnp.where(table, jnp.exp(chosen - jnp.max(chosen, axis=1, keepdims=True)), 0.0)
    gate_weights = chosen_exp / jnp.sum(chosen_exp, axis=1, keepdims=True)
    grad_logits = grad_gate - gate_weights * jnp.sum(grad_gate, axis=1, keepdims=True)
    wide_logits = jnp.pad(grad_logits, ((0, 0), (0, 128 - routed_count)))
    router_grad_full = lax.dot_general(
        grad_logits, second16.astype(F32), (((0,), (0,)), ((), ())), precision=lax.Precision.HIGHEST
    )
    order.close(order.now(wide_logits))

    out_near = out_sum.near(order)
    grad_hidden_state, grad_context16, out_even, out_odd, grad_gain_second = hidden_back_call(
        shared_back, order.now(wide_logits), router_pad, back_sum.even[0], back_sum.other[0], sides, hidden_state, grad_out16, gains, context_rel, attn16[3]
    )
    order.close(grad_context16)

    proj_sum = piece_sum(out_even, out_odd, is_core0)
    proj_core = proj_sum.core(order)
    grad_query16, grad_key16, grad_value16, head_even, head_odd = heads_back_call(
        query16, key16, value16, order.now(grad_context16), log_totals, cosine, sine, first_rel, lengths, score_scale
    )
    order.close(proj_core, grad_query16, out_near)

    head_sum = piece_sum(head_even, head_odd, is_core0)
    proj_far = proj_sum.far(order)
    head_core = head_sum.core(order)
    input_grad, grad_gain_first, input_square = input_back_call(
        order.now(grad_query16), grad_key16, grad_value16, tokens, gains, grad_hidden_state, lengths, attn16[:3]
    )
    order.close(head_core, proj_far, input_grad)

    head_far = head_sum.far(order)
    proj_near = proj_sum.near(order)
    shared_grad = lax.all_to_all(
        order.now(jnp.swapaxes(shared_sum.total().astype(BF), 0, 1)), "dp", split_axis=0, concat_axis=0, tiled=True
    )
    early_parts = update_call(
        0, order.now(routed_grads[0]), routed_weight, routed_moment, routed_average, [], rate_routed * step_root
    )
    order.close(head_far, proj_near, early_parts[-1])

    head_near = head_sum.near(order)
    proj_found = send_terms(after(proj_sum.total().astype(BF), head_sum.sent), 1, order)
    held = head_sum.sent
    block_value = after(hidden_state, held) + shared_out + out_sum.total()
    scalars = jnp.stack(
        [
            jnp.sum(valid_rows * block_value * block_value),
            input_square[0],
            length_here.astype(F32),
        ]
    )
    small_grads = jnp.concatenate([router_grad_full, grad_gain_first, grad_gain_second])
    scalars = jnp.broadcast_to(scalars[:, None], (3, model_width))
    small_grads = jnp.concatenate([small_grads, scalars])
    small_grads = jnp.pad(small_grads, ((0, 128 - small_grads.shape[0]), (0, 0)))
    small_grads = jnp.swapaxes(small_grads.T.reshape(parts, groups, -1, 128), 0, 1)
    small_found = lax.all_to_all(small_grads, "expert", split_axis=0, concat_axis=0, tiled=True)
    order.close(head_near, routed_grads[1:])

    head_total = order.now(head_sum.total().astype(BF))
    head_found = send_terms(head_total, 1, order)
    routed_parts = early_parts
    for e in range(1, per_device):
        routed_parts = update_call(
            e, after(order.now(routed_grads[e]), head_total), routed_weight, routed_moment, routed_average, routed_parts, rate_routed * step_root
        )
    proj_found, shared_grad, small_found = after((proj_found, shared_grad, small_found), head_total)
    small_total = tree_sum([small_found[r] for r in range(groups)])
    small_found = lax.all_to_all(small_total, "dp", split_axis=0, concat_axis=0, tiled=True)
    small_grad = tree_sum([small_found[d] for d in range(parts)])
    shared_grad = sum_terms([shared_grad[d] for d in range(parts)])
    head_found = after(head_found, routed_parts[-1])
    attn_grad = jnp.concatenate([sum_terms(head_found), sum_terms(proj_found)])
    router_grad = small_grad[:, :routed_count]
    gain_grad = small_grad[:, routed_count : routed_count + 2].T
    row_sums = small_grad[0, routed_count + 2 : routed_count + 5]
    denominator = model_width * row_sums[2]
    masked_rms = jnp.stack(
        [jnp.sqrt(row_sums[0] / denominator), jnp.sqrt(row_sums[1] / denominator)]
    )
    attn_parts = update(
        attn_weight, attn_moment, attn_average, attn_grad, rate_attention * step_root
    )
    router_parts = update(
        router_weight, router_moment, router_average, router_grad, rate_router * step_root
    )
    shared_parts = update(
        shared_weight, shared_moment, shared_average, shared_grad, rate_shared * step_root
    )
    gain_parts = update(norm_gains, gain_moment, gain_average, gain_grad, rate_gains * step_root)
    return (
        block_value.astype(BF),
        input_grad,
        masked_rms,
        attn_parts[0],
        attn_parts[1],
        attn_parts[2],
        attn_parts[3],
        attn_parts[4],
        router_parts[0],
        router_parts[1],
        router_parts[2],
        router_parts[3],
        router_parts[4],
        shared_parts[0],
        shared_parts[1],
        shared_parts[2],
        shared_parts[3],
        shared_parts[4],
        routed_parts[0],
        routed_parts[1],
        routed_parts[2],
        routed_parts[3],
        routed_parts[4],
        gain_parts[0],
        gain_parts[1],
        gain_parts[2],
        gain_parts[3],
    )


def solution(mesh):
    placed = (
        P(("dp", "expert"), None),
        P(("dp", "expert"), None),
        P(("dp", "expert")),
        P(("dp", "expert"), None),
        P(None, ("dp", "expert"), None),
        P(None, ("dp", "expert"), None),
        P(None, ("dp", "expert"), None),
        P(("dp", "expert"), None),
        P(("dp", "expert"), None),
        P(("dp", "expert"), None),
        P(None, ("dp", "expert"), None),
        P(None, ("dp", "expert"), None),
        P(None, ("dp", "expert"), None),
        P("expert", None, "dp", None),
        P("expert", None, "dp", None),
        P("expert", None, "dp", None),
        P(None, ("dp", "expert")),
        P(None, ("dp", "expert")),
        P(None, ("dp", "expert")),
    )
    return jax.shard_map(
        local,
        mesh=mesh,
        in_specs=placed,
        out_specs=(
            P(("dp", "expert"), None),
            P(("dp", "expert"), None),
            P(),
            P(None, ("dp", "expert"), None),
            P(None, ("dp", "expert"), None),
            P(None, ("dp", "expert"), None),
            P(None, ("dp", "expert"), None),
            P(None, ("dp", "expert"), None),
            P(("dp", "expert"), None),
            P(("dp", "expert"), None),
            P(("dp", "expert"), None),
            P(("dp", "expert"), None),
            P(("dp", "expert"), None),
            P(None, ("dp", "expert"), None),
            P(None, ("dp", "expert"), None),
            P(None, ("dp", "expert"), None),
            P(None, ("dp", "expert"), None),
            P(None, ("dp", "expert"), None),
            P("expert", None, "dp", None),
            P("expert", None, "dp", None),
            P("expert", None, "dp", None),
            P("expert", None, "dp", None),
            P("expert", None, "dp", None),
            P(None, ("dp", "expert")),
            P(None, ("dp", "expert")),
            P(None, ("dp", "expert")),
            P(None, ("dp", "expert")),
        ),
        check_vma=False,
    )
```
